32 devices in a mesh: ty: 4 (over y, x), tx: 8 (over z, core).
Axes of the slice: x: 2, y: 2, z: 4, core: 2. Of those that a mesh axis runs over, the one named last changes fastest.
Arguments:
- ensemble: bfloat16 [8, 8, 32, 1024], P('tx', None, 'ty'), may hold values from -6 to 6
- diffusivity: float32 [32, 1024], P('ty', 'tx'), may hold values from 0.1 to 0.245
- vertical: float32 [8, 8], replicated, as said below
- weights: float32 [8], replicated, may hold values from 0.0625 to 0.25
- obs_value: float32 [32, 8, 8], P(('ty', 'tx')), may hold values from -6 to 6
- obs_cell: int32 [32, 8, 8], P(('ty', 'tx')), may hold values from 0 to 8191
- obs_count: int32 [32, 8], P(('ty', 'tx')), may hold values from 0 to 8, as said below
Outputs:
- increment: float32 [8, 32, 1024], P(None, 'ty', 'tx')
- projected: float32 [32, 8, 8], P(('ty', 'tx'))
The draws below stay inside these ranges and needn't reach their ends.
Inputs may be any that keep to these rules, and one draw needn't show every extreme that they name: `obs_count`: in every tile row one destination column, drawn from the seed, receives 8 live slots from every source of that row; other loads are uneven across destination columns. `vertical`: Banded: entries more than two levels off the diagonal are zero.
All inputs are finite; a program needn't handle non-finite values.
Results may differ from the reference program's by a relative error of at most 0.0003.
Values may be sent and summed in bfloat16 or wider, within the bound.
No kernel may reach another device: no remote copies, remote signals or barrier semaphores. Data moves between devices by JAX's collectives and lax.ppermute only.
A program may use at most 64 MiB of HBM per device.

```python
import math
import jax
import jax.numpy as jnp
from jax import lax

LEVELS = 8
TILE_ROWS = 8
TILE_COLS = 128
STEPS = 4
SLOTS = 8
MEMBERS = 8
ROWS = 32
COLS = 1024
TILES_X = 8
TILES_Y = 4
SOURCES = 32


def draw_vertical(key, part):
    first, second = jax.random.split(key)
    diag_part = jax.random.uniform(first, (LEVELS,), jnp.float32, 1.0, 1.5)
    off_part = jax.random.uniform(second, (LEVELS, LEVELS), jnp.float32, -0.25, 0.25)
    rows_idx = jnp.arange(LEVELS)[:, None]
    cols_idx = jnp.arange(LEVELS)[None, :]
    gap_size = jnp.abs(rows_idx - cols_idx)
    banded = jnp.where((gap_size > 0) & (gap_size <= 2), off_part, jnp.float32(0.0))
    return banded + jnp.diag(diag_part)


def draw_obs_count(key, part):
    first, second, third = jax.random.split(key, 3)
    factor = jax.random.randint(first, (TILES_X,), 1, 5)
    base_load = jax.random.randint(second, (SOURCES, TILES_X), 0, SLOTS // 2 + 1)
    loads = jnp.minimum(base_load * factor[None, :], SLOTS)
    full_col = jax.random.randint(third, (TILES_Y,), 0, TILES_X)
    src_row = jnp.arange(SOURCES) // TILES_X
    hit_col = jnp.arange(TILES_X)[None, :] == full_col[src_row][:, None]
    return jnp.where(hit_col, SLOTS, loads).astype(jnp.int32)


def with_ends(values, key, smallest, largest):
    longest = values.shape.index(max(values.shape))
    spots = []
    for shift in (0, 1):
        where = [jax.random.randint(jax.random.fold_in(key, axis), (), 0, length) for axis, length in enumerate(values.shape)]
        where[longest] = (where[longest] + shift) % values.shape[longest]
        spots.append(tuple(where))
    return values.at[spots[0]].set(smallest).at[spots[1]].set(largest)


def steps_of(rng, extent, cuts, low, largest):
    loudness, own = 1.0, jax.random.fold_in(rng, 6)
    for dim, blocks in cuts:
        steps = jnp.exp(jax.random.uniform(jax.random.fold_in(own, dim), (blocks,), jnp.float32, low / len(cuts), largest / len(cuts)))
        loudness = loudness * jnp.repeat(steps, extent[dim] // blocks).reshape([-1 if axis == dim else 1 for axis in range(len(extent))])
    return loudness


def bell_draw(key, extent, width, limit, pieces=(), held_as=jnp.bfloat16):
    factor_of = steps_of(key, extent, pieces, -0.22, 0.18) if pieces else 1.0
    drawn = jax.random.normal(key, extent, jnp.float32) * width * factor_of
    return jnp.minimum(jnp.maximum(drawn, -limit), limit).astype(held_as)


def setup_inputs(seed: int = 0) -> dict:
    key_list = jax.random.split(jax.random.key(seed), 8)
    ensemble = bell_draw(key_list[0], (MEMBERS, LEVELS, ROWS, COLS), 1.0, 6.0, ((0, 8), (2, 4)))
    diffusivity = jnp.clip(jnp.exp(math.log(0.245) - 0.896088 * jax.random.uniform(key_list[1], (ROWS, COLS), jnp.float32) ** steps_of(key_list[1], (ROWS, COLS), ((0, 4), (1, 8)), -0.2, 0.2)), 0.1, 0.245)
    vertical = draw_vertical(jax.random.fold_in(key_list[7], 71), 0)
    weights = jnp.clip(jnp.exp(jax.random.uniform(key_list[3], (MEMBERS,), jnp.float32, math.log(0.0625), math.log(0.25))), 0.0625, 0.25)
    obs_value = bell_draw(key_list[4], (SOURCES, TILES_X, SLOTS), 1.0, 6.0, ((0, 32),), jnp.float32)
    obs_cell = with_ends(jax.random.randint(key_list[5], (SOURCES, TILES_X, SLOTS), 0, LEVELS * TILE_ROWS * TILE_COLS), jax.random.fold_in(key_list[5], 1), 0, (LEVELS * TILE_ROWS * TILE_COLS) - 1).astype(jnp.int32)
    obs_count = draw_obs_count(jax.random.fold_in(key_list[7], 71), 0)
    return dict(ensemble=ensemble, diffusivity=diffusivity, vertical=vertical, weights=weights, obs_value=obs_value, obs_cell=obs_cell, obs_count=obs_count)


def diffuse(current, diffusivity):
    padded = jnp.pad(current, ((0, 0), (1, 1), (1, 1)))
    beside = padded[:, :-2, 1:-1] + padded[:, 2:, 1:-1] + padded[:, 1:-1, :-2] + padded[:, 1:-1, 2:]
    return current + diffusivity * (beside - 4.0 * current)


def reference(ensemble, diffusivity, vertical, weights, obs_value, obs_cell, obs_count):
    tile_cells = TILE_ROWS * TILE_COLS
    source = jnp.arange(SOURCES, dtype=jnp.int32)
    tile_row = source // TILES_X
    dest_col = jnp.arange(TILES_X, dtype=jnp.int32)
    level_of = obs_cell // tile_cells
    in_tile = obs_cell % tile_cells
    glob_row = tile_row[:, None, None] * TILE_ROWS + in_tile // TILE_COLS
    glob_col = dest_col[None, :, None] * TILE_COLS + in_tile % TILE_COLS
    live_slots = jnp.arange(SLOTS, dtype=jnp.int32)[None, None, :] < obs_count[:, :, None]
    flat_index = ((level_of * ROWS + glob_row) * COLS + glob_col).astype(jnp.int32)
    forcing = jnp.zeros((LEVELS * ROWS * COLS,), jnp.float32)
    forcing = forcing.at[flat_index.ravel()].add(jnp.where(live_slots, obs_value, jnp.float32(0.0)).ravel())
    forcing = forcing.reshape(LEVELS, ROWS, COLS)

    def add_member(accum_sum, inputs):
        member, weight = inputs
        perturb = member.astype(jnp.float32)
        current = perturb * forcing
        for repeat in range(STEPS):
            current = diffuse(current, diffusivity)
        current = jnp.einsum("lm,mrc->lrc", vertical, current, precision=lax.Precision.HIGHEST)
        return accum_sum + weight * perturb * current, None

    result, unused = lax.scan(add_member, jnp.zeros((LEVELS, ROWS, COLS), jnp.float32), (ensemble, weights))
    projected = jnp.where(live_slots, result.ravel()[flat_index], jnp.float32(0.0))
    return result, projected
```

```python
import functools

import jax
import jax.numpy as jnp
from jax import lax
from jax.experimental import pallas as pl
from jax.experimental.pallas import tpu as pltpu
from jax.sharding import PartitionSpec as P

STEPS = 4
BAND = 2
LANES = 128
GROUP = 8
F32, BF16 = jnp.float32, jnp.bfloat16
VMEM = pl.BlockSpec(memory_space=pltpu.VMEM)
SMEM = pl.BlockSpec(memory_space=pltpu.SMEM)


def round_up(n, m):
    return -(-n // m) * m


def log2(n):
    assert n & (n - 1) == 0
    return n.bit_length() - 1


def iota(shape, axis):
    return lax.broadcasted_iota(jnp.int32, shape, axis)


def pieces(x):
    high = x.astype(BF16).astype(F32)
    rest = x - high
    middle = rest.astype(BF16).astype(F32)
    return high, middle, rest - middle


def stagger(x):
    return pltpu.roll(x, 0, 1, stride=GROUP, stride_axis=0)


def pick(x, place):
    if isinstance(place, int):
        shift = (-GROUP * place) % LANES
    else:
        shift = lax.rem(LANES - GROUP * place, LANES)
    rolled = pltpu.roll(x, shift, 1)
    own = iota(x.shape, 1) // GROUP == iota(x.shape, 0)
    return jnp.sum(jnp.where(own, rolled, 0.0), axis=0, keepdims=True)


def live_mask(count_ref, slots):
    tiles = count_ref.shape[1]
    count = jnp.broadcast_to(count_ref[...].astype(F32), (tiles, tiles))
    diagonal = iota((tiles, tiles), 0) == iota((tiles, tiles), 1)
    column = jnp.sum(jnp.where(diagonal, count, 0.0), axis=1, keepdims=True)
    return iota((tiles, slots), 1).astype(F32) < column


def pack_kernel(levels, value_ref, cell_ref, count_ref, diff_ref, out_ref, wide):
    _, tiles, slots = value_ref.shape
    rows = diff_ref.shape[0]
    block = min(tiles, LANES // GROUP)
    blocks = tiles // block
    cell = cell_ref[0]
    flat = lax.shift_right_logical(cell, log2(LANES))
    level = lax.shift_right_logical(flat, log2(rows))
    row = flat & (rows - 1)
    found = (
        jnp.where(live_mask(count_ref, slots), value_ref[0], 0.0),
        (row * levels + level).astype(F32),
        (cell & (LANES - 1)).astype(F32),
    )
    out_ref[...] = jnp.zeros_like(out_ref)
    out_ref[0:rows, :] = diff_ref[...]
    wide[...] = jnp.zeros_like(wide)
    for q, x in enumerate(found):
        wide[q, :, 0:slots] = x
        for b in range(blocks):
            line = pick(stagger(wide[q, b * block : (b + 1) * block, :]), 0)
            out_ref[pl.ds(rows + q * blocks + b, 1), :] = line


def turn_kernel(ens_ref, out_ref, wide):
    _, levels, rows, columns = ens_ref.shape
    for t in range(columns // LANES):
        at = slice(t * LANES, (t + 1) * LANES)
        wide[t] = ens_ref[0, :, :, at].astype(F32).reshape(levels * rows, LANES)
        for r in range(0, rows, 2):
            both = [wide[t, pl.ds(r + i, levels, stride=rows), :] for i in range(2)]
            out_ref[r * levels : (r + 2) * levels, at] = jnp.concatenate(both, axis=0).astype(BF16)


def gather_kernel(near, rows, levels, *refs):
    got, (turned_ref, d_ref, obs_ref, a_ref, b_ref, packs, halo_a, halo_b) = refs[:near], refs[near:]
    tiles = packs.shape[0]
    blocks = obs_ref.shape[2] // LANES
    me, even = lax.axis_index("tx"), lax.rem(lax.axis_index("ty"), 2) == 0
    chip, core = me // 2, lax.rem(me, 2)
    for far, ref in enumerate(got):
        for side in range(2):
            packs[2 * (chip ^ far) + (core ^ side)] = ref[side]
    for q in range(3):
        for b in range(blocks):
            obs_ref[q, :, b * LANES : (b + 1) * LANES] = packs[:, rows + q * blocks + b, :]
    half = STEPS * levels
    off_a, off_b = jnp.where(even, half, 0), jnp.where(even, 0, half)
    a_ref[0:half, :] = turned_ref[pl.ds(pl.multiple_of(off_a, half), half), :]
    b_ref[0:half, :] = turned_ref[pl.ds(pl.multiple_of(off_b, half), half), :]
    extra = halo_a.shape[0]
    deep = STEPS - 1
    halo_a[...] = jnp.zeros_like(halo_a)
    halo_b[...] = jnp.zeros_like(halo_b)
    for t in range(tiles):
        at = slice(t * LANES, (t + 1) * LANES)
        d = packs[t, 0:rows, :]
        d_ref[:, at] = d
        for p, piece in enumerate(pieces(d)):
            low = pltpu.roll(piece, deep, 0)
            halo_a[p * deep : (p + 1) * deep, :] = jnp.where(even, low, piece)[0:deep]
            halo_b[p * deep : (p + 1) * deep, :] = jnp.where(even, piece, low)[0:deep]
        first = 3 * deep
        for p, piece in enumerate(pieces(packs[t, rows : rows + blocks, :])):
            halo_a[first + p * blocks : first + (p + 1) * blocks, :] = piece
            halo_b[first + p * blocks : first + (p + 1) * blocks, :] = piece
        first += 3 * blocks
        where_at = packs[t, rows + blocks : rows + 3 * blocks, :]
        halo_a[first : first + 2 * blocks, :] = where_at
        halo_b[first : first + 2 * blocks, :] = where_at
        a_ref[half : half + extra, at] = halo_a[...].astype(BF16)
        b_ref[half : half + extra, at] = halo_b[...].astype(BF16)


def lines_of(x, tile, block):
    size = x[0][0].shape[0]
    return jnp.concatenate([pick(part, tile % size) for part in x[tile // size]], axis=1)


def spread(line_value, line_key, hits, count, first):
    key = line_key - first
    on = iota((count, line_key.shape[1]), 0).astype(F32) == key
    stacked = jnp.concatenate([jnp.where(on, piece, 0.0) for piece in pieces(line_value)], axis=0)
    found = lax.dot_general(
        stacked.astype(BF16), hits, (((1,), (1,)), ((), ())), preferred_element_type=F32
    )
    return found[0:count] + found[count : 2 * count] + found[2 * count :]


def hits_of(line_column):
    shape = (LANES, line_column.shape[1])
    return jnp.where(iota(shape, 0).astype(F32) == line_column, 1.0, 0.0).astype(BF16)


def main_kernel(
    rows, levels, d_ref, obs_ref, turned_ref, a_ref, b_ref, vertical_ref, weights_ref, mine_ref, other_ref,
    member, d_all, halo, first, second, hits_all, key_all, back,
):
    tiles = obs_ref.shape[1]
    blocks = obs_ref.shape[2] // LANES
    block = min(tiles, LANES // GROUP)
    columns = d_ref.shape[1]
    me, band = lax.axis_index("tx"), lax.axis_index("ty")
    even, last = lax.rem(band, 2) == 0, lax.axis_size("ty") - 1
    core = lax.rem(me, 2)
    half, own = STEPS * levels, rows * levels
    deep = STEPS - 1

    member[half : half + own, :] = turned_ref[...].astype(F32)
    d_all[STEPS : STEPS + rows, :] = d_ref[...]
    got_a, got_b = a_ref[...].astype(F32), b_ref[...].astype(F32)
    above = jnp.where(band == 0, 0.0, jnp.where(even, got_b, got_a))
    below = jnp.where(band == last, 0.0, jnp.where(even, got_a, got_b))
    member[0:half, :] = above[0:half]
    member[half + own :, :] = below[0:half]

    def cut(lines):
        return [
            [
                [stagger(part[q * block : (q + 1) * block]) for q in range(tiles // block)]
                for part in line
            ]
            for line in lines
        ]

    sets = [cut([[obs_ref[q, :, b * LANES : (b + 1) * LANES] for b in range(blocks)] for q in range(3)])]
    for side, (got, start) in enumerate(((above, 1), (below, STEPS + rows))):
        for t in range(tiles):
            halo[side, t] = got[half:, t * LANES : (t + 1) * LANES]
            d = halo[side, t, 0:deep, :] + halo[side, t, deep : 2 * deep, :] + halo[side, t, 2 * deep : 3 * deep, :]
            d_all[start : start + deep, t * LANES : (t + 1) * LANES] = d
        at = 3 * deep
        lines = [[halo[side, :, at + i * blocks + b, :] for b in range(blocks)] for i in range(5)]
        value = [lines[0][b] + lines[1][b] + lines[2][b] for b in range(blocks)]
        sets.append(cut([value, lines[3], lines[4]]))

    places = ((half, own, 0), (0, half, own - half), (half + own, half, 0))
    for t in range(tiles):
        at = slice(t * LANES, (t + 1) * LANES)
        for i, (begin, count, base) in enumerate(places):
            value, key, column = (lines_of(x, t, block) for x in sets[i])
            hits = hits_of(column)
            if i == 0:
                hits_all[t] = hits
                key_all[t] = jnp.broadcast_to(key, (8, key.shape[1]))
            field = spread(value, key, hits, count, float(base))
            first[begin : begin + count, at] = field * member[begin : begin + count, at]

    source, target = first, second
    left_end = iota((levels, columns), 1) == 0
    right_end = iota((levels, columns), 1) == columns - 1
    for step in range(STEPS):
        for r in range(step + 1, 2 * STEPS + rows - 1 - step):
            mid = source[r * levels : (r + 1) * levels, :]
            beside = (
                source[(r - 1) * levels : r * levels, :]
                + source[(r + 1) * levels : (r + 2) * levels, :]
                + jnp.where(left_end, 0.0, pltpu.roll(mid, 1, 1))
                + jnp.where(right_end, 0.0, pltpu.roll(mid, columns - 1, 1))
            )
            d = jnp.broadcast_to(d_all[r : r + 1, :], (levels, columns))
            target[r * levels : (r + 1) * levels, :] = mid + d * (beside - 4.0 * mid)
        source, target = target, source

    vertical = vertical_ref[...] * weights_ref[me]
    gap = iota((levels, levels), 1) - iota((levels, levels), 0)
    factors = [
        (o, jnp.sum(jnp.where(gap == o, vertical, 0.0), axis=1, keepdims=True)) for o in range(-BAND, BAND + 1)
    ]
    factors = [(o, jnp.broadcast_to(f, (levels, LANES))) for o, f in factors]
    chips = mine_ref.shape[0]
    for z in range(chips):
        for side, out in enumerate((mine_ref, other_ref)):
            t = 2 * z + (core ^ side)
            mirror = 2 * (2 * z // block * block) + block - 1
            at = pl.ds(pl.multiple_of(t * LANES, LANES), LANES)
            parts = []
            for r in range(rows):
                x = source[half + r * levels : half + (r + 1) * levels, at]
                mixed = sum(f * (pltpu.roll(x, -o % levels, 0) if o else x) for o, f in factors)
                part = mixed * member[half + r * levels : half + (r + 1) * levels, at]
                out[z, r * levels : (r + 1) * levels, :] = part
                parts.append(part)
            stacked = jnp.concatenate(pieces(jnp.concatenate(parts, axis=0)), axis=0).astype(BF16)
            found = jnp.dot(stacked, hits_all[t], preferred_element_type=F32)
            found = found[0:own] + found[own : 2 * own] + found[2 * own :]
            on = iota(found.shape, 0).astype(F32) == key_all[t][0:1]
            line = jnp.sum(jnp.where(on, found, 0.0), axis=0, keepdims=True)
            for q in range(tiles // block):
                back[q, pl.ds(mirror - t, 1), :] = line[:, q * LANES : (q + 1) * LANES]
    turned = [
        [stagger(back[q, b * block : (b + 1) * block, :]) for b in range(blocks)] for q in range(tiles // block)
    ]
    for z in range(chips):
        for side, out in enumerate((mine_ref, other_ref)):
            out[z, own:, :] = jnp.zeros((out.shape[1] - own, LANES), F32)
            place = 2 * z % block + (core ^ side)
            for b in range(blocks):
                out[z, own + b : own + b + 1, :] = pick(turned[2 * z // block][b], place)


def pair_kernel(mine_ref, got_ref, *outs):
    chip = lax.axis_index("tx") // 2
    for far, out in enumerate(outs):
        out[...] = mine_ref[chip ^ far] + got_ref[chip ^ far]


def final_kernel(near, *refs):
    got, (count_ref, inc_ref, proj_ref, total, wide) = refs[:near], refs[near:]
    levels, rows, _ = inc_ref.shape
    _, tiles, slots = proj_ref.shape
    block = min(tiles, LANES // GROUP)
    sums = got[0][...]
    for ref in got[1:]:
        sums = sums + ref[...]
    total[...] = sums
    for level in range(levels):
        inc_ref[level] = total[pl.ds(level, rows, stride=levels), :]
    for b in range(tiles // block):
        line = jnp.broadcast_to(total[rows * levels + b : rows * levels + b + 1, :], (block, LANES))
        line = pltpu.roll(line, (LANES - GROUP * (block - 1)) % LANES, 1)
        wide[b * block : (b + 1) * block, :] = stagger(line)
    proj_ref[0] = jnp.where(live_mask(count_ref, slots), wide[:, 0:slots], 0.0)


def call(kernel, out_shape, ins, scratch, flops=0, moved=0):
    return pl.pallas_call(
        kernel,
        out_shape=out_shape,
        in_specs=ins,
        out_specs=jax.tree.map(lambda _: VMEM, out_shape),
        scratch_shapes=scratch,
        compiler_params=pltpu.CompilerParams(vmem_limit_bytes=48 << 20),
        cost_estimate=pl.CostEstimate(flops=flops, bytes_accessed=moved, transcendentals=0),
    )


def shards(ensemble, diffusivity, vertical, weights, obs_value, obs_cell, obs_count):
    _, levels, rows, columns = ensemble.shape
    tiles, slots = obs_value.shape[1:]
    chips = tiles // 2
    bands = lax.axis_size("ty")
    assert diffusivity.shape == (rows, LANES) and slots == GROUP and rows == 2 * STEPS
    blocks = -(-tiles * GROUP // LANES)
    block = min(tiles, LANES // GROUP)
    shape = jax.ShapeDtypeStruct
    packet_rows = round_up(rows + 3 * blocks, 8)
    half, own = STEPS * levels, rows * levels
    extra = round_up(3 * (STEPS - 1) + 5 * blocks, 16)
    lanes = tiles // block * LANES

    packet = call(
        functools.partial(pack_kernel, levels),
        shape((packet_rows, LANES), F32),
        [VMEM] * 4,
        [pltpu.VMEM((3, tiles, LANES), F32)],
    )(obs_value, obs_cell, obs_count, diffusivity)
    turned = call(
        turn_kernel, shape((own, columns), BF16), [VMEM], [pltpu.VMEM((tiles, own, LANES), F32)], 1000000, 1000000
    )(ensemble)

    def swap(x, far):
        return lax.ppermute(x, "tx", [(i, i ^ far) for i in range(tiles)])

    pair = jnp.stack([packet, swap(packet, 1)])
    row = [pair] + [swap(pair, 2 * far) for far in range(1, chips)]
    d_row, obs, to_a, to_b = call(
        functools.partial(gather_kernel, chips, rows, levels),
        (
            shape((rows, columns), F32),
            shape((3, tiles, blocks * LANES), F32),
            shape((half + extra, columns), BF16),
            shape((half + extra, columns), BF16),
        ),
        [VMEM] * (chips + 1),
        [
            pltpu.VMEM((tiles, packet_rows, LANES), F32),
            pltpu.VMEM((extra, LANES), F32),
            pltpu.VMEM((extra, LANES), F32),
        ],
    )(*row, turned)
    pairs_a = [(i, i ^ 1) for i in range(bands)]
    pairs_b = [(i, (i + 1 if i % 2 else i - 1) % bands) for i in range(bands)]
    from_a = lax.ppermute(to_a, "ty", pairs_a)
    from_b = lax.ppermute(to_b, "ty", pairs_b)

    chunk = own + 8
    mine, other = call(
        functools.partial(main_kernel, rows, levels),
        (shape((chips, chunk, LANES), F32), shape((chips, chunk, LANES), F32)),
        [VMEM] * 6 + [SMEM],
        [
            pltpu.VMEM((2 * half + own, columns), F32),
            pltpu.VMEM((2 * STEPS + rows, columns), F32),
            pltpu.VMEM((2, tiles, extra, LANES), F32),
            pltpu.VMEM((2 * half + own, columns), F32),
            pltpu.VMEM((2 * half + own, columns), F32),
            pltpu.VMEM((tiles, LANES, lanes), BF16),
            pltpu.VMEM((tiles, 8, lanes), F32),
            pltpu.VMEM((tiles // block, tiles, LANES), F32),
        ],
    )(d_row, obs, turned, from_a, from_b, vertical, weights)
    sums = call(
        pair_kernel, tuple(shape((chunk, LANES), F32) for _ in range(chips)), [VMEM] * 2, []
    )(mine, swap(other, 1))
    sums = [sums[0]] + [swap(sums[far], 2 * far) for far in range(1, chips)]
    return call(
        functools.partial(final_kernel, chips),
        (shape((levels, rows, LANES), F32), shape((1, tiles, slots), F32)),
        [VMEM] * (chips + 1),
        [pltpu.VMEM((chunk, LANES), F32), pltpu.VMEM((tiles, LANES), F32)],
    )(*sums, obs_count)


def solution(mesh):
    placed = (
        P("tx", None, "ty", None),
        P("ty", "tx"),
        P(),
        P(),
        P(("ty", "tx"), None, None),
        P(("ty", "tx"), None, None),
        P(("ty", "tx"), None),
    )
    return jax.shard_map(
        shards,
        mesh=mesh,
        in_specs=placed,
        out_specs=(P(None, "ty", "tx"), P(("ty", "tx"), None, None)),
        check_vma=False,
    )
```

```python
import functools

import jax
import jax.numpy as jnp
from jax import lax
from jax.experimental import pallas as pl
from jax.experimental.pallas import tpu as pltpu
from jax.sharding import PartitionSpec as P

STEPS = 4
BAND = 2
LANES = 128
GROUP = 8
F32, BF16 = jnp.float32, jnp.bfloat16
VMEM = pl.BlockSpec(memory_space=pltpu.VMEM)
HBM = pl.BlockSpec(memory_space=pltpu.HBM)


def round_up(n, m):
    return -(-n // m) * m


def log2(n):
    assert n & (n - 1) == 0
    return n.bit_length() - 1


def iota(shape, axis):
    return lax.broadcasted_iota(jnp.int32, shape, axis)


def pieces(x):
    high = x.astype(BF16).astype(F32)
    rest = x - high
    middle = rest.astype(BF16).astype(F32)
    return high, middle, rest - middle


def stagger(x):
    return pltpu.roll(x, 0, 1, stride=GROUP, stride_axis=0)


def pick(x, place):
    if isinstance(place, int):
        shift = (-GROUP * place) % LANES
    else:
        shift = lax.rem(LANES - GROUP * place, LANES)
    rolled = pltpu.roll(x, shift, 1)
    own = iota(x.shape, 1) // GROUP == iota(x.shape, 0)
    return jnp.sum(jnp.where(own, rolled, 0.0), axis=0, keepdims=True)


def live_mask(count_ref, slots):
    tiles = count_ref.shape[1]
    count = jnp.broadcast_to(count_ref[...].astype(F32), (tiles, tiles))
    diagonal = iota((tiles, tiles), 0) == iota((tiles, tiles), 1)
    column = jnp.sum(jnp.where(diagonal, count, 0.0), axis=1, keepdims=True)
    return iota((tiles, slots), 1).astype(F32) < column


def first_kernel(
    copies, value_hbm, cell_hbm, count_hbm, diff_hbm, ens_hbm, vertical_hbm, weights_hbm,
    sent_ref, turned_ref, a_ref, b_ref, factors_ref, live_ref,
    value_ref, cell_ref, count_ref, diff_ref, ens_ref, vertical_ref, weights_ref, wide, packet, tall, sems,
):
    pairs = (
        (value_hbm, value_ref), (cell_hbm, cell_ref), (count_hbm, count_ref), (diff_hbm, diff_ref),
        (ens_hbm, ens_ref), (vertical_hbm, vertical_ref), (weights_hbm, weights_ref),
    )
    moves = [pltpu.make_async_copy(x, y, sems.at[i]) for i, (x, y) in enumerate(pairs)]
    for move in moves:
        move.start()
    wide[...] = jnp.zeros_like(wide)
    for move in moves[:4]:
        move.wait()
    _, tiles, slots = value_ref.shape
    rows = diff_ref.shape[0]
    block = min(tiles, LANES // GROUP)
    live = live_mask(count_ref, slots)
    wide[0, :, 0:slots] = jnp.where(live, value_ref[0], 0.0)
    wide[1, :, 0:slots] = cell_ref[0].astype(F32)
    live_ref[...] = jnp.zeros_like(live_ref)
    live_ref[:, 0:slots] = jnp.where(live, 1.0, 0.0)
    packet[0:rows, :] = diff_ref[...]
    lines = [pick(stagger(wide[q, b : b + block, :]), 0) for q in range(2) for b in range(0, tiles, block)]
    if block * GROUP < LANES:
        lines = [lines[0] + pltpu.roll(lines[1], block * GROUP, 1)]
    for i, line in enumerate(lines):
        packet[rows + i : rows + i + 1, :] = line
    height = packet.shape[0]
    for i in range(copies):
        sent_ref[i * height : (i + 1) * height, :] = packet[...]

    for move in moves[4:]:
        move.wait()
    _, levels, _, columns = ens_ref.shape
    for t in range(columns // LANES):
        at = slice(t * LANES, (t + 1) * LANES)
        tall[t] = ens_ref[0, :, :, at].astype(F32).reshape(levels * rows, LANES)
        for r in range(0, rows, 2):
            both = [tall[t, pl.ds(r + i, levels, stride=rows), :] for i in range(2)]
            turned_ref[r * levels : (r + 2) * levels, at] = jnp.concatenate(both, axis=0).astype(BF16)
    half = STEPS * levels
    even = lax.rem(lax.axis_index("ty"), 2) == 0
    off_a, off_b = jnp.where(even, half, 0), jnp.where(even, 0, half)
    a_ref[...] = turned_ref[pl.ds(pl.multiple_of(off_a, half), half), :]
    b_ref[...] = turned_ref[pl.ds(pl.multiple_of(off_b, half), half), :]
    vertical = vertical_ref[...] * weights_ref[lax.axis_index("tx")]
    gap = iota((levels, levels), 1) - iota((levels, levels), 0)
    for i in range(2 * BAND + 1):
        factor = jnp.sum(jnp.where(gap == i - BAND, vertical, 0.0), axis=1, keepdims=True)
        factors_ref[i] = jnp.broadcast_to(factor, (levels, LANES))


def lines_of(staggered, place, tiles):
    size = staggered[0][0].shape[0]
    groups = LANES // GROUP
    return jnp.concatenate([pick(part, place % groups) for part in staggered[place // groups]], axis=1)


def spread(line_value, line_key, hits, count, first):
    key = line_key - first
    on = iota((count, line_key.shape[1]), 0).astype(F32) == key
    stacked = jnp.concatenate([jnp.where(on, piece, 0.0) for piece in pieces(line_value)], axis=0)
    found = lax.dot_general(
        stacked.astype(BF16), hits, (((1,), (1,)), ((), ())), preferred_element_type=F32
    )
    return found[0:count] + found[count : 2 * count] + found[2 * count :]


def hits_of(line_column):
    shape = (LANES, line_column.shape[1])
    return jnp.where(iota(shape, 0).astype(F32) == line_column, 1.0, 0.0).astype(BF16)


def forcing_kernel(rows, levels, tiles, got_ref, field_ref, d_ref, hits_ref, key_ref):
    band, last = lax.axis_index("ty"), lax.axis_size("ty") - 1
    half, own, deep = STEPS * levels, rows * levels, STEPS - 1
    height = got_ref.shape[0] // (tiles * (last + 1))
    lines, block = height - rows, min(tiles, LANES // GROUP)
    bands = (
        (band, None, half, own, 0, STEPS, rows, 0),
        (jnp.maximum(band - 1, 0), band > 0, 0, half, own - half, 1, deep, rows - deep),
        (jnp.minimum(band + 1, last), band < last, half + own, half, 0, STEPS + rows, deep, 0),
    )
    for side, (which, inside, begin, count, base, d_begin, d_count, d_base) in enumerate(bands):
        start = which * (tiles * height)
        values, keys, columns = [], [], []
        for i in range(lines):
            x = got_ref[pl.ds(start + rows + i, tiles, stride=height), :]
            cell = x.astype(jnp.int32)
            flat = lax.shift_right_logical(cell, log2(LANES))
            key = (flat & (rows - 1)) * levels + lax.shift_right_logical(flat, log2(rows))
            if inside is not None:
                x = jnp.where(inside, x, 0.0)
            for out, part in ((values, x), (keys, key.astype(F32)), (columns, (cell & (LANES - 1)).astype(F32))):
                out.append([stagger(part[q : q + block]) for q in range(0, tiles, block)])
        for t in range(tiles):
            at = slice(t * LANES, (t + 1) * LANES)
            d = got_ref[pl.ds(start + t * height + d_base, d_count), :]
            d_ref[d_begin : d_begin + d_count, at] = d if inside is None else jnp.where(inside, d, 0.0)
            value = lines_of(values, t, tiles)
            key, column = lines_of(keys, tiles + t, tiles), lines_of(columns, tiles + t, tiles)
            hits = hits_of(column)
            if side == 0:
                hits_ref[t] = hits
                key_ref[t] = jnp.broadcast_to(key, (8, key.shape[1]))
            field_ref[begin : begin + count, at] = spread(value, key, hits, count, float(base))


def main_kernel(
    rows, levels, field_ref, d_all, hits_all, key_all, turned_ref, a_ref, b_ref, factors_ref, mine_ref, other_ref,
    member, first, second, back,
):
    tiles = hits_all.shape[0]
    blocks = -(-tiles * GROUP // LANES)
    block = min(tiles, LANES // GROUP)
    columns = turned_ref.shape[1]
    band, core = lax.axis_index("ty"), lax.rem(lax.axis_index("tx"), 2)
    even, last = lax.rem(band, 2) == 0, lax.axis_size("ty") - 1
    half, own = STEPS * levels, rows * levels

    member[...] = turned_ref[...].astype(F32)
    first[half : half + own, :] = field_ref[half : half + own, :] * member[...]
    got_a, got_b = a_ref[...].astype(F32), b_ref[...].astype(F32)
    above = jnp.where(band == 0, 0.0, jnp.where(even, got_b, got_a))
    below = jnp.where(band == last, 0.0, jnp.where(even, got_a, got_b))
    first[0:half, :] = field_ref[0:half, :] * above
    first[half + own :, :] = field_ref[half + own :, :] * below

    source, target = first, second
    left_end = iota((levels, columns), 1) == 0
    right_end = iota((levels, columns), 1) == columns - 1
    for step in range(STEPS):
        for r in range(step + 1, 2 * STEPS + rows - 1 - step):
            mid = source[r * levels : (r + 1) * levels, :]
            beside = (
                source[(r - 1) * levels : r * levels, :]
                + source[(r + 1) * levels : (r + 2) * levels, :]
                + jnp.where(left_end, 0.0, pltpu.roll(mid, 1, 1))
                + jnp.where(right_end, 0.0, pltpu.roll(mid, columns - 1, 1))
            )
            d = jnp.broadcast_to(d_all[r : r + 1, :], (levels, columns))
            target[r * levels : (r + 1) * levels, :] = mid + d * (beside - 4.0 * mid)
        source, target = target, source

    factors = [(i - BAND, factors_ref[i]) for i in range(2 * BAND + 1)]
    chips = mine_ref.shape[0]
    for z in range(chips):
        for side, out in enumerate((mine_ref, other_ref)):
            t = 2 * z + (core ^ side)
            mirror = 2 * (2 * z // block * block) + block - 1
            at = pl.ds(pl.multiple_of(t * LANES, LANES), LANES)
            parts = []
            for r in range(rows):
                x = source[half + r * levels : half + (r + 1) * levels, at]
                mixed = sum(f * (pltpu.roll(x, -o % levels, 0) if o else x) for o, f in factors)
                part = mixed * member[r * levels : (r + 1) * levels, at]
                out[z, r * levels : (r + 1) * levels, :] = part
                parts.append(part)
            stacked = jnp.concatenate(pieces(jnp.concatenate(parts, axis=0)), axis=0).astype(BF16)
            found = jnp.dot(stacked, hits_all[t], preferred_element_type=F32)
            found = found[0:own] + found[own : 2 * own] + found[2 * own :]
            on = iota(found.shape, 0).astype(F32) == key_all[t][0:1]
            line = jnp.sum(jnp.where(on, found, 0.0), axis=0, keepdims=True)
            for q in range(tiles // block):
                back[q, pl.ds(mirror - t, 1), :] = line[:, q * LANES : (q + 1) * LANES]
    turned = [
        [stagger(back[q, b * block : (b + 1) * block, :]) for b in range(blocks)] for q in range(tiles // block)
    ]
    for z in range(chips):
        for side, out in enumerate((mine_ref, other_ref)):
            out[z, own:, :] = jnp.zeros((out.shape[1] - own, LANES), F32)
            place = 2 * z % block + (core ^ side)
            for b in range(blocks):
                out[z, own + b : own + b + 1, :] = pick(turned[2 * z // block][b], place)


def pair_kernel(mine_ref, got_ref, *outs):
    chip = lax.axis_index("tx") // 2
    for far, out in enumerate(outs):
        out[...] = mine_ref[chip ^ far] + got_ref[chip ^ far]


def final_kernel(near, *refs):
    got, (live_ref, inc_ref, proj_ref, total, wide) = refs[:near], refs[near:]
    levels, rows, _ = inc_ref.shape
    _, tiles, slots = proj_ref.shape
    block = min(tiles, LANES // GROUP)
    sums = got[0][...]
    for ref in got[1:]:
        sums = sums + ref[...]
    total[...] = sums
    for level in range(levels):
        inc_ref[level] = total[pl.ds(level, rows, stride=levels), :]
    for b in range(tiles // block):
        line = jnp.broadcast_to(total[rows * levels + b : rows * levels + b + 1, :], (block, LANES))
        line = pltpu.roll(line, (LANES - GROUP * (block - 1)) % LANES, 1)
        wide[b * block : (b + 1) * block, :] = stagger(line)
    proj_ref[0] = jnp.where(live_ref[:, 0:slots] > 0.0, wide[:, 0:slots], 0.0)


def call(kernel, out_shape, ins, scratch, flops=0, moved=0):
    return pl.pallas_call(
        kernel,
        out_shape=out_shape,
        in_specs=ins,
        out_specs=jax.tree.map(lambda _: VMEM, out_shape),
        scratch_shapes=scratch,
        compiler_params=pltpu.CompilerParams(vmem_limit_bytes=48 << 20),
        cost_estimate=pl.CostEstimate(flops=flops, bytes_accessed=moved, transcendentals=0),
    )


def shards(ensemble, diffusivity, vertical, weights, obs_value, obs_cell, obs_count):
    _, levels, rows, columns = ensemble.shape
    tiles, slots = obs_value.shape[1:]
    chips = tiles // 2
    bands = lax.axis_size("ty")
    devices = bands * tiles
    assert diffusivity.shape == (rows, LANES) and slots == GROUP and rows == 2 * STEPS
    block = min(tiles, LANES // GROUP)
    shape = jax.ShapeDtypeStruct
    height = rows + -(-2 * tiles * GROUP // LANES)
    half, own = STEPS * levels, rows * levels
    lanes = tiles // block * LANES

    sent, turned, to_a, to_b, factors, live = call(
        functools.partial(first_kernel, devices),
        (
            shape((devices * height, LANES), F32),
            shape((own, columns), BF16),
            shape((half, columns), BF16),
            shape((half, columns), BF16),
            shape((2 * BAND + 1, levels, LANES), F32),
            shape((tiles, LANES), F32),
        ),
        [HBM] * 7,
        [
            pltpu.VMEM(obs_value.shape, F32),
            pltpu.VMEM(obs_cell.shape, jnp.int32),
            pltpu.VMEM(obs_count.shape, jnp.int32),
            pltpu.VMEM(diffusivity.shape, F32),
            pltpu.VMEM(ensemble.shape, BF16),
            pltpu.VMEM(vertical.shape, F32),
            pltpu.SMEM(weights.shape, F32),
            pltpu.VMEM((2, tiles, LANES), F32),
            pltpu.VMEM((height, LANES), F32),
            pltpu.VMEM((tiles, own, LANES), F32),
            pltpu.SemaphoreType.DMA((7,)),
        ],
    )(
        *(
            pltpu.with_memory_space_constraint(x, pltpu.HBM)
            for x in (obs_value, obs_cell, obs_count, diffusivity, ensemble, vertical, weights)
        )
    )

    got = lax.all_to_all(
        sent.reshape(devices, 1, height * LANES), ("ty", "tx"), split_axis=0, concat_axis=0, tiled=True
    ).reshape(devices * height, LANES)
    pairs_a = [(i, i ^ 1) for i in range(bands)]
    pairs_b = [(i, (i + 1 if i % 2 else i - 1) % bands) for i in range(bands)]
    from_a = lax.ppermute(to_a, "ty", pairs_a)
    from_b = lax.ppermute(to_b, "ty", pairs_b)

    field, d_all, hits, key = call(
        functools.partial(forcing_kernel, rows, levels, tiles),
        (
            shape((2 * half + own, columns), F32),
            shape((2 * STEPS + rows, columns), F32),
            shape((tiles, LANES, lanes), BF16),
            shape((tiles, 8, lanes), F32),
        ),
        [VMEM],
        [],
    )(got)
    chunk = own + 8
    mine, other = call(
        functools.partial(main_kernel, rows, levels),
        (shape((chips, chunk, LANES), F32), shape((chips, chunk, LANES), F32)),
        [VMEM] * 8,
        [
            pltpu.VMEM((own, columns), F32),
            pltpu.VMEM((2 * half + own, columns), F32),
            pltpu.VMEM((2 * half + own, columns), F32),
            pltpu.VMEM((tiles // block, tiles, LANES), F32),
        ],
    )(field, d_all, hits, key, turned, from_a, from_b, factors)

    def swap(x, far):
        return lax.ppermute(x, "tx", [(i, i ^ far) for i in range(tiles)])

    sums = call(
        pair_kernel, tuple(shape((chunk, LANES), F32) for _ in range(chips)), [VMEM] * 2, []
    )(mine, swap(other, 1))
    sums = [sums[0]] + [swap(sums[far], 2 * far) for far in range(1, chips)]
    return call(
        functools.partial(final_kernel, chips),
        (shape((levels, rows, LANES), F32), shape((1, tiles, slots), F32)),
        [VMEM] * (chips + 1),
        [pltpu.VMEM((chunk, LANES), F32), pltpu.VMEM((tiles, LANES), F32)],
    )(*sums, live)


def solution(mesh):
    placed = (
        P("tx", None, "ty", None),
        P("ty", "tx"),
        P(),
        P(),
        P(("ty", "tx"), None, None),
        P(("ty", "tx"), None, None),
        P(("ty", "tx"), None),
    )
    return jax.shard_map(
        shards,
        mesh=mesh,
        in_specs=placed,
        out_specs=(P(None, "ty", "tx"), P(("ty", "tx"), None, None)),
        check_vma=False,
    )
```

```python
import functools

import jax
import jax.numpy as jnp
from jax import lax
from jax.experimental import pallas as pl
from jax.experimental.pallas import tpu as pltpu
from jax.sharding import PartitionSpec as P

STEPS = 4
BAND = 2
LANES = 128
GROUP = 8
F32, BF16 = jnp.float32, jnp.bfloat16
VMEM = pl.BlockSpec(memory_space=pltpu.VMEM)
HBM = pl.BlockSpec(memory_space=pltpu.HBM)


def round_up(n, m):
    return -(-n // m) * m


def log2(n):
    assert n & (n - 1) == 0
    return n.bit_length() - 1


def iota(shape, axis):
    return lax.broadcasted_iota(jnp.int32, shape, axis)


def pieces(x):
    high = x.astype(BF16).astype(F32)
    rest = x - high
    middle = rest.astype(BF16).astype(F32)
    return high, middle, rest - middle


def stagger(x):
    return pltpu.roll(x, 0, 1, stride=GROUP, stride_axis=0)


def pick(x, place):
    if isinstance(place, int):
        shift = (-GROUP * place) % LANES
    else:
        shift = lax.rem(LANES - GROUP * place, LANES)
    rolled = pltpu.roll(x, shift, 1)
    own = iota(x.shape, 1) // GROUP == iota(x.shape, 0)
    return jnp.sum(jnp.where(own, rolled, 0.0), axis=0, keepdims=True)


def live_mask(count_ref, slots):
    tiles = count_ref.shape[1]
    count = jnp.broadcast_to(count_ref[...].astype(F32), (tiles, tiles))
    diagonal = iota((tiles, tiles), 0) == iota((tiles, tiles), 1)
    column = jnp.sum(jnp.where(diagonal, count, 0.0), axis=1, keepdims=True)
    return iota((tiles, slots), 1).astype(F32) < column


def copy_in(sources, targets, sems):
    moves = [pltpu.make_async_copy(x, y, sems.at[i]) for i, (x, y) in enumerate(zip(sources, targets))]
    for move in moves:
        move.start()
    return moves


def packet_kernel(
    copies, value_hbm, cell_hbm, count_hbm, diff_hbm, sent_ref, live_ref,
    value_ref, cell_ref, count_ref, diff_ref, wide, packet, sems,
):
    moves = copy_in(
        (value_hbm, cell_hbm, count_hbm, diff_hbm), (value_ref, cell_ref, count_ref, diff_ref), sems
    )
    wide[...] = jnp.zeros_like(wide)
    for move in moves:
        move.wait()
    _, tiles, slots = value_ref.shape
    rows = diff_ref.shape[0]
    block = min(tiles, LANES // GROUP)
    live = live_mask(count_ref, slots)
    wide[0, :, 0:slots] = jnp.where(live, value_ref[0], 0.0)
    wide[1, :, 0:slots] = cell_ref[0].astype(F32)
    live_ref[...] = jnp.zeros_like(live_ref)
    live_ref[:, 0:slots] = jnp.where(live, 1.0, 0.0)
    packet[0:rows, :] = diff_ref[...]
    lines = [pick(stagger(wide[q, b : b + block, :]), 0) for q in range(2) for b in range(0, tiles, block)]
    if block * GROUP < LANES:
        lines = [lines[0] + pltpu.roll(lines[1], block * GROUP, 1)]
    for i, line in enumerate(lines):
        packet[rows + i : rows + i + 1, :] = line
    height = packet.shape[0]
    for i in range(copies):
        sent_ref[i * height : (i + 1) * height, :] = packet[...]


def member_kernel(
    ens_hbm, vertical_hbm, weights_hbm, turned_ref, a_ref, b_ref, factors_ref,
    ens_ref, vertical_ref, weights_ref, tall, sems,
):
    moves = copy_in((vertical_hbm, weights_hbm, ens_hbm), (vertical_ref, weights_ref, ens_ref), sems)
    for move in moves:
        move.wait()
    _, levels, rows, columns = ens_ref.shape
    for t in range(columns // LANES):
        at = slice(t * LANES, (t + 1) * LANES)
        tall[t] = ens_ref[0, :, :, at].astype(F32).reshape(levels * rows, LANES)
        for r in range(0, rows, 2):
            both = [tall[t, pl.ds(r + i, levels, stride=rows), :] for i in range(2)]
            turned_ref[r * levels : (r + 2) * levels, at] = jnp.concatenate(both, axis=0).astype(BF16)
    half = STEPS * levels
    even = lax.rem(lax.axis_index("ty"), 2) == 0
    off_a, off_b = jnp.where(even, half, 0), jnp.where(even, 0, half)
    a_ref[...] = turned_ref[pl.ds(pl.multiple_of(off_a, half), half), :]
    b_ref[...] = turned_ref[pl.ds(pl.multiple_of(off_b, half), half), :]
    vertical = vertical_ref[...] * weights_ref[lax.axis_index("tx")]
    gap = iota((levels, levels), 1) - iota((levels, levels), 0)
    for i in range(2 * BAND + 1):
        factor = jnp.sum(jnp.where(gap == i - BAND, vertical, 0.0), axis=1, keepdims=True)
        factors_ref[i] = jnp.broadcast_to(factor, (levels, LANES))


def lines_of(staggered, place, tiles):
    size = staggered[0][0].shape[0]
    groups = LANES // GROUP
    return jnp.concatenate([pick(part, place % groups) for part in staggered[place // groups]], axis=1)


def spread(line_value, line_key, hits, count, first):
    key = line_key - first
    on = iota((count, line_key.shape[1]), 0).astype(F32) == key
    stacked = jnp.concatenate([jnp.where(on, piece, 0.0) for piece in pieces(line_value)], axis=0)
    found = lax.dot_general(
        stacked.astype(BF16), hits, (((1,), (1,)), ((), ())), preferred_element_type=F32
    )
    return found[0:count] + found[count : 2 * count] + found[2 * count :]


def hits_of(line_column):
    shape = (LANES, line_column.shape[1])
    return jnp.where(iota(shape, 0).astype(F32) == line_column, 1.0, 0.0).astype(BF16)


def forcing_kernel(rows, levels, tiles, got_ref, field_ref, d_ref, hits_ref, key_ref):
    band, last = lax.axis_index("ty"), lax.axis_size("ty") - 1
    half, own, deep = STEPS * levels, rows * levels, STEPS - 1
    height = got_ref.shape[0] // (tiles * (last + 1))
    lines, block = height - rows, min(tiles, LANES // GROUP)
    bands = (
        (band, None, half, own, 0, STEPS, rows, 0),
        (jnp.maximum(band - 1, 0), band > 0, 0, half, own - half, 1, deep, rows - deep),
        (jnp.minimum(band + 1, last), band < last, half + own, half, 0, STEPS + rows, deep, 0),
    )
    for side, (which, inside, begin, count, base, d_begin, d_count, d_base) in enumerate(bands):
        start = which * (tiles * height)
        values, keys, columns = [], [], []
        for i in range(lines):
            x = got_ref[pl.ds(start + rows + i, tiles, stride=height), :]
            cell = x.astype(jnp.int32)
            flat = lax.shift_right_logical(cell, log2(LANES))
            key = (flat & (rows - 1)) * levels + lax.shift_right_logical(flat, log2(rows))
            if inside is not None:
                x = jnp.where(inside, x, 0.0)
            for out, part in ((values, x), (keys, key.astype(F32)), (columns, (cell & (LANES - 1)).astype(F32))):
                out.append([stagger(part[q : q + block]) for q in range(0, tiles, block)])
        for t in range(tiles):
            at = slice(t * LANES, (t + 1) * LANES)
            d = got_ref[pl.ds(start + t * height + d_base, d_count), :]
            d_ref[d_begin : d_begin + d_count, at] = d if inside is None else jnp.where(inside, d, 0.0)
            value = lines_of(values, t, tiles)
            key, column = lines_of(keys, tiles + t, tiles), lines_of(columns, tiles + t, tiles)
            hits = hits_of(column)
            if side == 0:
                hits_ref[t] = hits
                key_ref[t] = jnp.broadcast_to(key, (8, key.shape[1]))
            field_ref[begin : begin + count, at] = spread(value, key, hits, count, float(base))


def main_kernel(
    rows, levels, field_ref, d_all, hits_all, key_all, turned_ref, a_ref, b_ref, factors_ref, mine_ref, other_ref,
    member, first, second, back,
):
    tiles = hits_all.shape[0]
    blocks = -(-tiles * GROUP // LANES)
    block = min(tiles, LANES // GROUP)
    columns = turned_ref.shape[1]
    band, me = lax.axis_index("ty"), lax.axis_index("tx")
    chip, core = me // 2, lax.rem(me, 2)
    even, last = lax.rem(band, 2) == 0, lax.axis_size("ty") - 1
    half, own = STEPS * levels, rows * levels

    member[...] = turned_ref[...].astype(F32)
    first[half : half + own, :] = field_ref[half : half + own, :] * member[...]
    got_a, got_b = a_ref[...].astype(F32), b_ref[...].astype(F32)
    above = jnp.where(band == 0, 0.0, jnp.where(even, got_b, got_a))
    below = jnp.where(band == last, 0.0, jnp.where(even, got_a, got_b))
    first[0:half, :] = field_ref[0:half, :] * above
    first[half + own :, :] = field_ref[half + own :, :] * below

    source, target = first, second
    left_end = iota((levels, columns), 1) == 0
    right_end = iota((levels, columns), 1) == columns - 1
    for step in range(STEPS):
        for r in range(step + 1, 2 * STEPS + rows - 1 - step):
            mid = source[r * levels : (r + 1) * levels, :]
            beside = (
                source[(r - 1) * levels : r * levels, :]
                + source[(r + 1) * levels : (r + 2) * levels, :]
                + jnp.where(left_end, 0.0, pltpu.roll(mid, 1, 1))
                + jnp.where(right_end, 0.0, pltpu.roll(mid, columns - 1, 1))
            )
            d = jnp.broadcast_to(d_all[r : r + 1, :], (levels, columns))
            target[r * levels : (r + 1) * levels, :] = mid + d * (beside - 4.0 * mid)
        source, target = target, source

    factors = [(i - BAND, factors_ref[i]) for i in range(2 * BAND + 1)]
    chips = mine_ref.shape[0]
    for z in range(chips):
        for side, out in enumerate((mine_ref, other_ref)):
            t = 2 * z + (core ^ side ^ (chip != z).astype(jnp.int32))
            mirror = 2 * (2 * z // block * block) + block - 1
            at = pl.ds(pl.multiple_of(t * LANES, LANES), LANES)
            parts = []
            for r in range(rows):
                x = source[half + r * levels : half + (r + 1) * levels, at]
                mixed = sum(f * (pltpu.roll(x, -o % levels, 0) if o else x) for o, f in factors)
                part = mixed * member[r * levels : (r + 1) * levels, at]
                out[z, r * levels : (r + 1) * levels, :] = part
                parts.append(part)
            stacked = jnp.concatenate(pieces(jnp.concatenate(parts, axis=0)), axis=0).astype(BF16)
            found = jnp.dot(stacked, hits_all[t], preferred_element_type=F32)
            found = found[0:own] + found[own : 2 * own] + found[2 * own :]
            on = iota(found.shape, 0).astype(F32) == key_all[t][0:1]
            line = jnp.sum(jnp.where(on, found, 0.0), axis=0, keepdims=True)
            for q in range(tiles // block):
                back[q, pl.ds(mirror - t, 1), :] = line[:, q * LANES : (q + 1) * LANES]
    turned = [
        [stagger(back[q, b * block : (b + 1) * block, :]) for b in range(blocks)] for q in range(tiles // block)
    ]
    for z in range(chips):
        for side, out in enumerate((mine_ref, other_ref)):
            out[z, own:, :] = jnp.zeros((out.shape[1] - own, LANES), F32)
            place = 2 * z % block + (core ^ side ^ (chip != z).astype(jnp.int32))
            for b in range(blocks):
                out[z, own + b : own + b + 1, :] = pick(turned[2 * z // block][b], place)


def pair_kernel(mine_ref, got_ref, *outs):
    chip = lax.axis_index("tx") // 2
    for far, out in enumerate(outs):
        out[...] = mine_ref[chip ^ far] + got_ref[chip ^ far]


def final_kernel(near, *refs):
    got, (live_ref, inc_ref, proj_ref, total, wide) = refs[:near], refs[near:]
    levels, rows, _ = inc_ref.shape
    _, tiles, slots = proj_ref.shape
    block = min(tiles, LANES // GROUP)
    sums = got[0][...]
    for ref in got[1:]:
        sums = sums + ref[...]
    total[...] = sums
    for level in range(levels):
        inc_ref[level] = total[pl.ds(level, rows, stride=levels), :]
    for b in range(tiles // block):
        line = jnp.broadcast_to(total[rows * levels + b : rows * levels + b + 1, :], (block, LANES))
        line = pltpu.roll(line, (LANES - GROUP * (block - 1)) % LANES, 1)
        wide[b * block : (b + 1) * block, :] = stagger(line)
    proj_ref[0] = jnp.where(live_ref[:, 0:slots] > 0.0, wide[:, 0:slots], 0.0)


def call(kernel, out_shape, ins, scratch, flops=0, moved=0):
    return pl.pallas_call(
        kernel,
        out_shape=out_shape,
        in_specs=ins,
        out_specs=jax.tree.map(lambda _: VMEM, out_shape),
        scratch_shapes=scratch,
        compiler_params=pltpu.CompilerParams(vmem_limit_bytes=48 << 20),
        cost_estimate=pl.CostEstimate(flops=flops, bytes_accessed=moved, transcendentals=0),
    )


def shards(ensemble, diffusivity, vertical, weights, obs_value, obs_cell, obs_count):
    _, levels, rows, columns = ensemble.shape
    tiles, slots = obs_value.shape[1:]
    chips = tiles // 2
    bands = lax.axis_size("ty")
    devices = bands * tiles
    assert diffusivity.shape == (rows, LANES) and slots == GROUP and rows == 2 * STEPS
    block = min(tiles, LANES // GROUP)
    shape = jax.ShapeDtypeStruct
    height = rows + -(-2 * tiles * GROUP // LANES)
    half, own = STEPS * levels, rows * levels
    lanes = tiles // block * LANES

    def in_hbm(*arrays):
        return [pltpu.with_memory_space_constraint(x, pltpu.HBM) for x in arrays]

    sent, live = call(
        functools.partial(packet_kernel, devices),
        (shape((devices * height, LANES), F32), shape((tiles, LANES), F32)),
        [HBM] * 4,
        [
            pltpu.VMEM(obs_value.shape, F32),
            pltpu.VMEM(obs_cell.shape, jnp.int32),
            pltpu.VMEM(obs_count.shape, jnp.int32),
            pltpu.VMEM(diffusivity.shape, F32),
            pltpu.VMEM((2, tiles, LANES), F32),
            pltpu.VMEM((height, LANES), F32),
            pltpu.SemaphoreType.DMA((4,)),
        ],
    )(*in_hbm(obs_value, obs_cell, obs_count, diffusivity))
    turned, to_a, to_b, factors = call(
        member_kernel,
        (
            shape((own, columns), BF16),
            shape((half, columns), BF16),
            shape((half, columns), BF16),
            shape((2 * BAND + 1, levels, LANES), F32),
        ),
        [HBM] * 3,
        [
            pltpu.VMEM(ensemble.shape, BF16),
            pltpu.VMEM(vertical.shape, F32),
            pltpu.SMEM(weights.shape, F32),
            pltpu.VMEM((tiles, own, LANES), F32),
            pltpu.SemaphoreType.DMA((3,)),
        ],
    )(*in_hbm(ensemble, vertical, weights))

    got = lax.all_to_all(
        sent.reshape(devices, 1, height * LANES), ("ty", "tx"), split_axis=0, concat_axis=0, tiled=True
    ).reshape(devices * height, LANES)
    pairs_a = [(i, i ^ 1) for i in range(bands)]
    pairs_b = [(i, (i + 1 if i % 2 else i - 1) % bands) for i in range(bands)]
    from_a = lax.ppermute(to_a, "ty", pairs_a)
    from_b = lax.ppermute(to_b, "ty", pairs_b)

    field, d_all, hits, key = call(
        functools.partial(forcing_kernel, rows, levels, tiles),
        (
            shape((2 * half + own, columns), F32),
            shape((2 * STEPS + rows, columns), F32),
            shape((tiles, LANES, lanes), BF16),
            shape((tiles, 8, lanes), F32),
        ),
        [VMEM],
        [],
    )(got)
    chunk = own + 8
    mine, other = call(
        functools.partial(main_kernel, rows, levels),
        (shape((chips, chunk, LANES), F32), shape((chips, chunk, LANES), F32)),
        [VMEM] * 8,
        [
            pltpu.VMEM((own, columns), F32),
            pltpu.VMEM((2 * half + own, columns), F32),
            pltpu.VMEM((2 * half + own, columns), F32),
            pltpu.VMEM((tiles // block, tiles, LANES), F32),
        ],
    )(field, d_all, hits, key, turned, from_a, from_b, factors)

    def swap(x, far):
        return lax.ppermute(x, "tx", [(i, i ^ far) for i in range(tiles)])

    sums = call(
        pair_kernel, tuple(shape((chunk, LANES), F32) for _ in range(chips)), [VMEM] * 2, []
    )(mine, swap(other, 1))
    sums = [sums[0]] + [swap(sums[far], 2 * far + 1) for far in range(1, chips)]
    return call(
        functools.partial(final_kernel, chips),
        (shape((levels, rows, LANES), F32), shape((1, tiles, slots), F32)),
        [VMEM] * (chips + 1),
        [pltpu.VMEM((chunk, LANES), F32), pltpu.VMEM((tiles, LANES), F32)],
    )(*sums, live)


def solution(mesh):
    placed = (
        P("tx", None, "ty", None),
        P("ty", "tx"),
        P(),
        P(),
        P(("ty", "tx"), None, None),
        P(("ty", "tx"), None, None),
        P(("ty", "tx"), None),
    )
    return jax.shard_map(
        shards,
        mesh=mesh,
        in_specs=placed,
        out_specs=(P(None, "ty", "tx"), P(("ty", "tx"), None, None)),
        check_vma=False,
    )
```

```python
import functools

import jax
import jax.numpy as jnp
from jax import lax
from jax.experimental import pallas as pl
from jax.experimental.pallas import tpu as pltpu
from jax.sharding import PartitionSpec as P

STEPS = 4
BAND = 2
LANES = 128
GROUP = 8
F32, BF16 = jnp.float32, jnp.bfloat16
VMEM = pl.BlockSpec(memory_space=pltpu.VMEM)
HBM = pl.BlockSpec(memory_space=pltpu.HBM)


def round_up(n, m):
    return -(-n // m) * m


def log2(n):
    assert n & (n - 1) == 0
    return n.bit_length() - 1


def iota(shape, axis):
    return lax.broadcasted_iota(jnp.int32, shape, axis)


def pieces(x):
    high = x.astype(BF16).astype(F32)
    rest = x - high
    middle = rest.astype(BF16).astype(F32)
    return high, middle, rest - middle


def stagger(x):
    return pltpu.roll(x, 0, 1, stride=GROUP, stride_axis=0)


def pick(x, place):
    if isinstance(place, int):
        shift = (-GROUP * place) % LANES
    else:
        shift = lax.rem(LANES - GROUP * place, LANES)
    rolled = pltpu.roll(x, shift, 1)
    own = iota(x.shape, 1) // GROUP == iota(x.shape, 0)
    return jnp.sum(jnp.where(own, rolled, 0.0), axis=0, keepdims=True)


def live_mask(count_ref, slots):
    tiles = count_ref.shape[1]
    count = jnp.broadcast_to(count_ref[...].astype(F32), (tiles, tiles))
    diagonal = iota((tiles, tiles), 0) == iota((tiles, tiles), 1)
    column = jnp.sum(jnp.where(diagonal, count, 0.0), axis=1, keepdims=True)
    return iota((tiles, slots), 1).astype(F32) < column


def copy_in(sources, targets, sems):
    moves = [pltpu.make_async_copy(x, y, sems.at[i]) for i, (x, y) in enumerate(zip(sources, targets))]
    for move in moves:
        move.start()
    return moves


def first_kernel(
    value_hbm, cell_hbm, count_hbm, diff_hbm, ens_hbm, vertical_hbm, weights_hbm,
    packet, turned_ref, a_ref, b_ref, factors_ref, live_ref,
    value_ref, cell_ref, count_ref, diff_ref, ens_ref, vertical_ref, weights_ref, wide, part, tall, sems,
):
    moves = copy_in(
        (value_hbm, cell_hbm, count_hbm, diff_hbm, ens_hbm, vertical_hbm, weights_hbm),
        (value_ref, cell_ref, count_ref, diff_ref, ens_ref, vertical_ref, weights_ref),
        sems,
    )
    wide[...] = jnp.zeros_like(wide)
    for move in moves[:4]:
        move.wait()
    _, tiles, slots = value_ref.shape
    rows = diff_ref.shape[0]
    block = min(tiles, LANES // GROUP)
    live = live_mask(count_ref, slots)
    wide[0, :, 0:slots] = jnp.where(live, value_ref[0], 0.0)
    wide[1, :, 0:slots] = cell_ref[0].astype(F32)
    live_ref[...] = jnp.zeros_like(live_ref)
    live_ref[:, 0:slots] = jnp.where(live, 1.0, 0.0)
    packet[0:rows, :] = diff_ref[...]
    lines = [pick(stagger(wide[q, b : b + block, :]), 0) for q in range(2) for b in range(0, tiles, block)]
    if block * GROUP < LANES:
        lines = [lines[0] + pltpu.roll(lines[1], block * GROUP, 1)]
    packet[rows:, :] = jnp.zeros((packet.shape[0] - rows, LANES), F32)
    for i, line in enumerate(lines):
        packet[rows + i : rows + i + 1, :] = line
    deep, levels = STEPS - 1, ens_ref.shape[1]
    half = STEPS * levels
    even = lax.rem(lax.axis_index("ty"), 2) == 0
    top, low = diff_ref[...], pltpu.roll(diff_ref[...], deep, 0)
    for out, chosen in ((a_ref, jnp.where(even, low, top)), (b_ref, jnp.where(even, top, low))):
        part[...] = chosen
        for i, line in enumerate(lines):
            part[deep + i : deep + i + 1, :] = line
        split = jnp.concatenate([*pieces(part[...]), jnp.zeros((rows, LANES), F32)], axis=0)
        out[tiles * half :, :] = split.astype(BF16)

    for move in moves[4:]:
        move.wait()
    off_a, off_b = jnp.where(even, half, 0), jnp.where(even, 0, half)
    for t in range(tiles):
        at = slice(t * LANES, (t + 1) * LANES)
        tall[t] = ens_ref[0, :, :, at].astype(F32).reshape(levels * rows, LANES)
        for r in range(0, rows, 2):
            both = [tall[t, pl.ds(r + i, levels, stride=rows), :] for i in range(2)]
            turned_ref[t, r * levels : (r + 2) * levels, :] = jnp.concatenate(both, axis=0).astype(BF16)
        a_ref[t * half : (t + 1) * half, :] = turned_ref[t, pl.ds(pl.multiple_of(off_a, half), half), :]
        b_ref[t * half : (t + 1) * half, :] = turned_ref[t, pl.ds(pl.multiple_of(off_b, half), half), :]
    vertical = vertical_ref[...] * weights_ref[lax.axis_index("tx")]
    gap = iota((levels, levels), 1) - iota((levels, levels), 0)
    for i in range(2 * BAND + 1):
        factor = jnp.sum(jnp.where(gap == i - BAND, vertical, 0.0), axis=1, keepdims=True)
        factors_ref[i] = jnp.broadcast_to(factor, (levels, LANES))


def join_kernel(size, at, packet_ref, a_ref, b_ref, out_ref):
    band, last = lax.axis_index("ty"), lax.axis_size("ty") - 1
    even = lax.rem(band, 2) == 0
    own, halo = size
    got = [ref[at:, :].astype(F32) for ref in (a_ref, b_ref)]
    step = got[0].shape[0] // 4
    got_a, got_b = (x[0:step] + x[step : 2 * step] + x[2 * step : 3 * step] for x in got)
    above = jnp.where(band == 0, 0.0, jnp.where(even, got_b, got_a))
    below = jnp.where(band == last, 0.0, jnp.where(even, got_a, got_b))
    out_ref[0:own, :] = packet_ref[0:own, :]
    out_ref[own : own + halo, :] = above[0:halo]
    out_ref[own + halo : own + 2 * halo, :] = below[0:halo]
    rest = out_ref.shape[0] - own - 2 * halo
    if rest:
        out_ref[own + 2 * halo :, :] = jnp.zeros((rest, LANES), F32)


def lines_of(staggered, place, tiles):
    size = staggered[0][0].shape[0]
    groups = LANES // GROUP
    return jnp.concatenate([pick(part, place % groups) for part in staggered[place // groups]], axis=1)


def spread(line_value, line_key, hits, count, first):
    key = line_key - first
    on = iota((count, line_key.shape[1]), 0).astype(F32) == key
    stacked = jnp.concatenate([jnp.where(on, piece, 0.0) for piece in pieces(line_value)], axis=0)
    found = lax.dot_general(
        stacked.astype(BF16), hits, (((1,), (1,)), ((), ())), preferred_element_type=F32
    )
    return found[0:count] + found[count : 2 * count] + found[2 * count :]


def hits_of(line_column):
    shape = (LANES, line_column.shape[1])
    return jnp.where(iota(shape, 0).astype(F32) == line_column, 1.0, 0.0).astype(BF16)


def fill(lines, rows, levels, base, count, write):
    tiles = lines[0].shape[0]
    block = min(tiles, LANES // GROUP)
    values, keys, columns = [], [], []
    for x in lines:
        cell = x.astype(jnp.int32)
        flat = lax.shift_right_logical(cell, log2(LANES))
        key = (flat & (rows - 1)) * levels + lax.shift_right_logical(flat, log2(rows))
        for out, part in ((values, x), (keys, key.astype(F32)), (columns, (cell & (LANES - 1)).astype(F32))):
            out.append([stagger(part[q : q + block]) for q in range(0, tiles, block)])
    for t in range(tiles):
        value = lines_of(values, t, tiles)
        key, column = lines_of(keys, tiles + t, tiles), lines_of(columns, tiles + t, tiles)
        hits = hits_of(column)
        write(t, spread(value, key, hits, count, float(base)), hits, key)


def main_kernel(
    near, rows, levels, lines, *refs,
):
    got, refs = refs[:near], refs[near:]
    turned_ref, a_ref, b_ref, factors_ref, mine_ref, other_ref = refs[:6]
    packs, member, d_all, hits_all, key_all, first, second, back = refs[6:]
    tiles = packs.shape[0]
    blocks = -(-tiles * GROUP // LANES)
    block = min(tiles, LANES // GROUP)
    columns = tiles * LANES
    band, me = lax.axis_index("ty"), lax.axis_index("tx")
    chip, core = me // 2, lax.rem(me, 2)
    even = lax.rem(band, 2) == 0
    half, own, deep = STEPS * levels, rows * levels, STEPS - 1

    own_rows, halo_rows = rows + lines, deep + lines
    for far, ref in enumerate(got):
        for side in range(2):
            packs[2 * (chip ^ far) + (core ^ side ^ (far > 0))] = ref[side]

    for t in range(tiles):
        at = slice(t * LANES, (t + 1) * LANES)
        member[half : half + own, at] = turned_ref[t].astype(F32)
        got_a, got_b = (ref[t * half : (t + 1) * half, :].astype(F32) for ref in (a_ref, b_ref))
        member[0:half, at] = jnp.where(even, got_b, got_a)
        member[half + own :, at] = jnp.where(even, got_a, got_b)
    sides = (
        (half, own, 0, 0, rows, STEPS),
        (0, half, own - half, own_rows, deep, 1),
        (half + own, half, 0, own_rows + halo_rows, deep, STEPS + rows),
    )
    for side, (begin, count, base, at_row, d_count, d_begin) in enumerate(sides):
        found = [packs[:, at_row + d_count + i, :] for i in range(lines)]

        def write(t, field, hits, key, side=side, begin=begin, count=count, at_row=at_row, d_count=d_count, d_begin=d_begin):
            at = slice(t * LANES, (t + 1) * LANES)
            d_all[d_begin : d_begin + d_count, at] = packs[t, at_row : at_row + d_count, :]
            first[begin : begin + count, at] = field * member[begin : begin + count, at]
            if side == 0:
                hits_all[t] = hits
                key_all[t] = jnp.broadcast_to(key, (8, key.shape[1]))

        fill(found, rows, levels, base, count, write)

    source, target = first, second
    left_end = iota((levels, columns), 1) == 0
    right_end = iota((levels, columns), 1) == columns - 1
    for step in range(STEPS):
        for r in range(step + 1, 2 * STEPS + rows - 1 - step):
            mid = source[r * levels : (r + 1) * levels, :]
            beside = (
                source[(r - 1) * levels : r * levels, :]
                + source[(r + 1) * levels : (r + 2) * levels, :]
                + jnp.where(left_end, 0.0, pltpu.roll(mid, 1, 1))
                + jnp.where(right_end, 0.0, pltpu.roll(mid, columns - 1, 1))
            )
            d = jnp.broadcast_to(d_all[r : r + 1, :], (levels, columns))
            target[r * levels : (r + 1) * levels, :] = mid + d * (beside - 4.0 * mid)
        source, target = target, source

    factors = [(i - BAND, factors_ref[i]) for i in range(2 * BAND + 1)]
    chips = mine_ref.shape[0]
    for z in range(chips):
        for side, out in enumerate((mine_ref, other_ref)):
            t = 2 * z + (core ^ side ^ (chip != z).astype(jnp.int32))
            mirror = 2 * (2 * z // block * block) + block - 1
            at = pl.ds(pl.multiple_of(t * LANES, LANES), LANES)
            parts = []
            for r in range(rows):
                x = source[half + r * levels : half + (r + 1) * levels, at]
                mixed = sum(f * (pltpu.roll(x, -o % levels, 0) if o else x) for o, f in factors)
                part = mixed * member[half + r * levels : half + (r + 1) * levels, at]
                out[z, r * levels : (r + 1) * levels, :] = part
                parts.append(part)
            stacked = jnp.concatenate(pieces(jnp.concatenate(parts, axis=0)), axis=0).astype(BF16)
            found = jnp.dot(stacked, hits_all[t], preferred_element_type=F32)
            found = found[0:own] + found[own : 2 * own] + found[2 * own :]
            on = iota(found.shape, 0).astype(F32) == key_all[t][0:1]
            line = jnp.sum(jnp.where(on, found, 0.0), axis=0, keepdims=True)
            for q in range(tiles // block):
                back[q, pl.ds(mirror - t, 1), :] = line[:, q * LANES : (q + 1) * LANES]
    turned = [
        [stagger(back[q, b * block : (b + 1) * block, :]) for b in range(blocks)] for q in range(tiles // block)
    ]
    for z in range(chips):
        for side, out in enumerate((mine_ref, other_ref)):
            out[z, own:, :] = jnp.zeros((out.shape[1] - own, LANES), F32)
            place = 2 * z % block + (core ^ side ^ (chip != z).astype(jnp.int32))
            for b in range(blocks):
                out[z, own + b : own + b + 1, :] = pick(turned[2 * z // block][b], place)


def pair_kernel(mine_ref, got_ref, *outs):
    chip = lax.axis_index("tx") // 2
    for far, out in enumerate(outs):
        out[...] = mine_ref[chip ^ far] + got_ref[chip ^ far]


def final_kernel(near, *refs):
    got, (live_ref, inc_ref, proj_ref, total, wide) = refs[:near], refs[near:]
    levels, rows, _ = inc_ref.shape
    _, tiles, slots = proj_ref.shape
    block = min(tiles, LANES // GROUP)
    sums = got[0][...]
    for ref in got[1:]:
        sums = sums + ref[...]
    total[...] = sums
    for level in range(levels):
        inc_ref[level] = total[pl.ds(level, rows, stride=levels), :]
    for b in range(tiles // block):
        line = jnp.broadcast_to(total[rows * levels + b : rows * levels + b + 1, :], (block, LANES))
        line = pltpu.roll(line, (LANES - GROUP * (block - 1)) % LANES, 1)
        wide[b * block : (b + 1) * block, :] = stagger(line)
    proj_ref[0] = jnp.where(live_ref[:, 0:slots] > 0.0, wide[:, 0:slots], 0.0)


def call(kernel, out_shape, ins, scratch, flops=0, moved=0):
    return pl.pallas_call(
        kernel,
        out_shape=out_shape,
        in_specs=ins,
        out_specs=jax.tree.map(lambda _: VMEM, out_shape),
        scratch_shapes=scratch,
        compiler_params=pltpu.CompilerParams(vmem_limit_bytes=48 << 20),
        cost_estimate=pl.CostEstimate(flops=flops, bytes_accessed=moved, transcendentals=0),
    )


def shards(ensemble, diffusivity, vertical, weights, obs_value, obs_cell, obs_count):
    _, levels, rows, columns = ensemble.shape
    tiles, slots = obs_value.shape[1:]
    chips = tiles // 2
    bands = lax.axis_size("ty")
    assert diffusivity.shape == (rows, LANES) and slots == GROUP and rows == 2 * STEPS
    block = min(tiles, LANES // GROUP)
    shape = jax.ShapeDtypeStruct
    lines = -(-2 * tiles * GROUP // LANES)
    half, own = STEPS * levels, rows * levels
    own_rows, halo_rows = rows + lines, STEPS - 1 + lines
    height, joined = round_up(own_rows, 8), round_up(own_rows + 2 * halo_rows, 8)
    lanes = tiles // block * LANES
    assert halo_rows <= rows

    def in_hbm(*arrays):
        return [pltpu.with_memory_space_constraint(x, pltpu.HBM) for x in arrays]

    def swap(x, far):
        return lax.ppermute(x, "tx", [(i, i ^ far) for i in range(tiles)])

    def swap_bands(x, low):
        mate = [i ^ 1 if low else i + 1 if i % 2 else i - 1 for i in range(bands)]
        pairs = [
            (i * tiles + k, mate[i] * tiles + k if 0 <= mate[i] < bands else i * tiles + (k ^ 1))
            for i in range(bands)
            for k in range(tiles)
        ]
        return lax.ppermute(x, ("ty", "tx"), pairs)

    sent = shape((tiles * half + 4 * rows, LANES), BF16)
    packet, turned, to_a, to_b, factors, live = call(
        first_kernel,
        (
            shape((height, LANES), F32),
            shape((tiles, own, LANES), BF16),
            sent,
            sent,
            shape((2 * BAND + 1, levels, LANES), F32),
            shape((tiles, LANES), F32),
        ),
        [HBM] * 7,
        [
            pltpu.VMEM(obs_value.shape, F32),
            pltpu.VMEM(obs_cell.shape, jnp.int32),
            pltpu.VMEM(obs_count.shape, jnp.int32),
            pltpu.VMEM(diffusivity.shape, F32),
            pltpu.VMEM(ensemble.shape, BF16),
            pltpu.VMEM(vertical.shape, F32),
            pltpu.SMEM(weights.shape, F32),
            pltpu.VMEM((2, tiles, LANES), F32),
            pltpu.VMEM((rows, LANES), F32),
            pltpu.VMEM((tiles, own, LANES), F32),
            pltpu.SemaphoreType.DMA((7,)),
        ],
    )(*in_hbm(obs_value, obs_cell, obs_count, diffusivity, ensemble, vertical, weights))
    from_a, from_b = swap_bands(to_a, True), swap_bands(to_b, False)
    mine = call(
        functools.partial(join_kernel, (own_rows, halo_rows), tiles * half),
        shape((joined, LANES), F32),
        [VMEM] * 3,
        [],
    )(packet, from_a, from_b)
    pair = jnp.stack([mine, swap(mine, 1)])
    row = [pair] + [swap(pair, 2 * far + 1) for far in range(1, chips)]

    chunk = own + 8
    mine, other = call(
        functools.partial(main_kernel, chips, rows, levels, lines),
        (shape((chips, chunk, LANES), F32), shape((chips, chunk, LANES), F32)),
        [VMEM] * (chips + 4),
        [
            pltpu.VMEM((tiles, joined, LANES), F32),
            pltpu.VMEM((2 * half + own, columns), F32),
            pltpu.VMEM((2 * STEPS + rows, columns), F32),
            pltpu.VMEM((tiles, LANES, lanes), BF16),
            pltpu.VMEM((tiles, 8, lanes), F32),
            pltpu.VMEM((2 * half + own, columns), F32),
            pltpu.VMEM((2 * half + own, columns), F32),
            pltpu.VMEM((tiles // block, tiles, LANES), F32),
        ],
    )(*row, turned, from_a, from_b, factors)

    sums = call(
        pair_kernel, tuple(shape((chunk, LANES), F32) for _ in range(chips)), [VMEM] * 2, []
    )(mine, swap(other, 1))
    sums = [sums[0]] + [swap(sums[far], 2 * far + 1) for far in range(1, chips)]
    return call(
        functools.partial(final_kernel, chips),
        (shape((levels, rows, LANES), F32), shape((1, tiles, slots), F32)),
        [VMEM] * (chips + 1),
        [pltpu.VMEM((chunk, LANES), F32), pltpu.VMEM((tiles, LANES), F32)],
    )(*sums, live)


def solution(mesh):
    placed = (
        P("tx", None, "ty", None),
        P("ty", "tx"),
        P(),
        P(),
        P(("ty", "tx"), None, None),
        P(("ty", "tx"), None, None),
        P(("ty", "tx"), None),
    )
    return jax.shard_map(
        shards,
        mesh=mesh,
        in_specs=placed,
        out_specs=(P(None, "ty", "tx"), P(("ty", "tx"), None, None)),
        check_vma=False,
    )
```

```python
import functools

import jax
import jax.numpy as jnp
from jax import lax
from jax.experimental import pallas as pl
from jax.experimental.pallas import tpu as pltpu
from jax.sharding import PartitionSpec as P

STEPS = 4
BAND = 2
LANES = 128
GROUP = 8
F32, BF16 = jnp.float32, jnp.bfloat16
VMEM = pl.BlockSpec(memory_space=pltpu.VMEM)
HBM = pl.BlockSpec(memory_space=pltpu.HBM)


def round_up(n, m):
    return -(-n // m) * m


def log2(n):
    assert n & (n - 1) == 0
    return n.bit_length() - 1


def iota(shape, axis):
    return lax.broadcasted_iota(jnp.int32, shape, axis)


def pieces(x):
    high = x.astype(BF16).astype(F32)
    rest = x - high
    middle = rest.astype(BF16).astype(F32)
    return high, middle, rest - middle


def stagger(x):
    return pltpu.roll(x, 0, 1, stride=GROUP, stride_axis=0)


def pick(x, place):
    if isinstance(place, int):
        shift = (-GROUP * place) % LANES
    else:
        shift = lax.rem(LANES - GROUP * place, LANES)
    rolled = pltpu.roll(x, shift, 1)
    own = iota(x.shape, 1) // GROUP == iota(x.shape, 0)
    return jnp.sum(jnp.where(own, rolled, 0.0), axis=0, keepdims=True)


def live_mask(count_ref, slots):
    tiles = count_ref.shape[1]
    count = jnp.broadcast_to(count_ref[...].astype(F32), (tiles, tiles))
    diagonal = iota((tiles, tiles), 0) == iota((tiles, tiles), 1)
    column = jnp.sum(jnp.where(diagonal, count, 0.0), axis=1, keepdims=True)
    return iota((tiles, slots), 1).astype(F32) < column


def copy_in(sources, targets, sems):
    moves = [pltpu.make_async_copy(x, y, sems.at[i]) for i, (x, y) in enumerate(zip(sources, targets))]
    for move in moves:
        move.start()
    return moves


def first_kernel(
    value_hbm, cell_hbm, count_hbm, diff_hbm, ens_hbm, vertical_hbm, weights_hbm,
    packet, turned_ref, a_ref, b_ref, factors_ref, live_ref,
    value_ref, cell_ref, count_ref, diff_ref, ens_ref, vertical_ref, weights_ref, wide, part, tall, sems,
):
    moves = copy_in(
        (value_hbm, cell_hbm, count_hbm, diff_hbm, ens_hbm, vertical_hbm, weights_hbm),
        (value_ref, cell_ref, count_ref, diff_ref, ens_ref, vertical_ref, weights_ref),
        sems,
    )
    wide[...] = jnp.zeros_like(wide)
    for move in moves[:4]:
        move.wait()
    _, tiles, slots = value_ref.shape
    rows = diff_ref.shape[0]
    block = min(tiles, LANES // GROUP)
    live = live_mask(count_ref, slots)
    wide[0, :, 0:slots] = jnp.where(live, value_ref[0], 0.0)
    wide[1, :, 0:slots] = cell_ref[0].astype(F32)
    live_ref[...] = jnp.zeros_like(live_ref)
    live_ref[:, 0:slots] = jnp.where(live, 1.0, 0.0)
    packet[0:rows, :] = diff_ref[...]
    lines = [pick(stagger(wide[q, b : b + block, :]), 0) for q in range(2) for b in range(0, tiles, block)]
    if block * GROUP < LANES:
        lines = [lines[0] + pltpu.roll(lines[1], block * GROUP, 1)]
    packet[rows:, :] = jnp.zeros((packet.shape[0] - rows, LANES), F32)
    for i, line in enumerate(lines):
        packet[rows + i : rows + i + 1, :] = line
    deep, levels = STEPS - 1, ens_ref.shape[1]
    half = STEPS * levels
    even = lax.rem(lax.axis_index("ty"), 2) == 0
    top, low = diff_ref[...], pltpu.roll(diff_ref[...], deep, 0)
    for out, chosen in ((a_ref, jnp.where(even, low, top)), (b_ref, jnp.where(even, top, low))):
        part[...] = chosen
        for i, line in enumerate(lines):
            part[deep + i : deep + i + 1, :] = line
        split = jnp.concatenate([*pieces(part[...]), jnp.zeros((rows, LANES), F32)], axis=0)
        out[tiles * half :, :] = split.astype(BF16)

    for move in moves[4:]:
        move.wait()
    off_a, off_b = jnp.where(even, half, 0), jnp.where(even, 0, half)
    for t in range(tiles):
        at = slice(t * LANES, (t + 1) * LANES)
        tall[t] = ens_ref[0, :, :, at].astype(F32).reshape(levels * rows, LANES)
        for r in range(0, rows, 2):
            both = [tall[t, pl.ds(r + i, levels, stride=rows), :] for i in range(2)]
            turned_ref[t, r * levels : (r + 2) * levels, :] = jnp.concatenate(both, axis=0).astype(BF16)
        a_ref[t * half : (t + 1) * half, :] = turned_ref[t, pl.ds(pl.multiple_of(off_a, half), half), :]
        b_ref[t * half : (t + 1) * half, :] = turned_ref[t, pl.ds(pl.multiple_of(off_b, half), half), :]
    vertical = vertical_ref[...] * weights_ref[lax.axis_index("tx")]
    gap = iota((levels, levels), 1) - iota((levels, levels), 0)
    for i in range(2 * BAND + 1):
        factor = jnp.sum(jnp.where(gap == i - BAND, vertical, 0.0), axis=1, keepdims=True)
        factors_ref[i] = jnp.broadcast_to(factor, (levels, LANES))


def join_kernel(size, at, packet_ref, a_ref, b_ref, out_ref):
    band, last = lax.axis_index("ty"), lax.axis_size("ty") - 1
    even = lax.rem(band, 2) == 0
    own, halo = size
    got = [ref[at:, :].astype(F32) for ref in (a_ref, b_ref)]
    step = got[0].shape[0] // 4
    got_a, got_b = (x[0:step] + x[step : 2 * step] + x[2 * step : 3 * step] for x in got)
    above = jnp.where(band == 0, 0.0, jnp.where(even, got_b, got_a))
    below = jnp.where(band == last, 0.0, jnp.where(even, got_a, got_b))
    out_ref[0:own, :] = packet_ref[0:own, :]
    out_ref[own : own + halo, :] = above[0:halo]
    out_ref[own + halo : own + 2 * halo, :] = below[0:halo]
    rest = out_ref.shape[0] - own - 2 * halo
    if rest:
        out_ref[own + 2 * halo :, :] = jnp.zeros((rest, LANES), F32)


def lines_of(staggered, place, tiles):
    size = staggered[0][0].shape[0]
    groups = LANES // GROUP
    return jnp.concatenate([pick(part, place % groups) for part in staggered[place // groups]], axis=1)


def spread(line_value, line_key, hits, count, first):
    key = line_key - first
    on = iota((count, line_key.shape[1]), 0).astype(F32) == key
    stacked = jnp.concatenate([jnp.where(on, piece, 0.0) for piece in pieces(line_value)], axis=0)
    found = lax.dot_general(
        stacked.astype(BF16), hits, (((1,), (1,)), ((), ())), preferred_element_type=F32
    )
    return found[0:count] + found[count : 2 * count] + found[2 * count :]


def hits_of(line_column):
    shape = (LANES, line_column.shape[1])
    return jnp.where(iota(shape, 0).astype(F32) == line_column, 1.0, 0.0).astype(BF16)


def fill(lines, rows, levels, base, count, write):
    tiles = lines[0].shape[0]
    block = min(tiles, LANES // GROUP)
    values, keys, columns = [], [], []
    for x in lines:
        cell = x.astype(jnp.int32)
        flat = lax.shift_right_logical(cell, log2(LANES))
        key = (flat & (rows - 1)) * levels + lax.shift_right_logical(flat, log2(rows))
        for out, part in ((values, x), (keys, key.astype(F32)), (columns, (cell & (LANES - 1)).astype(F32))):
            out.append([stagger(part[q : q + block]) for q in range(0, tiles, block)])
    for t in range(tiles):
        value = lines_of(values, t, tiles)
        key, column = lines_of(keys, tiles + t, tiles), lines_of(columns, tiles + t, tiles)
        hits = hits_of(column)
        write(t, spread(value, key, hits, count, float(base)), hits, key)


def main_kernel(
    near, rows, levels, lines, *refs,
):
    got, refs = refs[:near], refs[near:]
    turned_ref, a_ref, b_ref, factors_ref, mine_ref, other_ref = refs[:6]
    packs, member, d_all, keep, hits_all, key_all, first, second, made, back = refs[6:]
    tiles = packs.shape[0]
    block = min(tiles, LANES // GROUP)
    columns = tiles * LANES
    band, me = lax.axis_index("ty"), lax.axis_index("tx")
    chip, core = me // 2, lax.rem(me, 2)
    even = lax.rem(band, 2) == 0
    half, own, deep = STEPS * levels, rows * levels, STEPS - 1

    own_rows, halo_rows = rows + lines, deep + lines
    for far, ref in enumerate(got):
        for side in range(2):
            packs[2 * (chip ^ far) + (core ^ side ^ (far > 0))] = ref[side]

    for t in range(tiles):
        at = slice(t * LANES, (t + 1) * LANES)
        member[half : half + own, at] = turned_ref[t].astype(F32)
        got_a, got_b = (ref[t * half : (t + 1) * half, :].astype(F32) for ref in (a_ref, b_ref))
        member[0:half, at] = jnp.where(even, got_b, got_a)
        member[half + own :, at] = jnp.where(even, got_a, got_b)
    sides = (
        (half, own, 0, 0, rows, STEPS),
        (0, half, own - half, own_rows, deep, 1),
        (half + own, half, 0, own_rows + halo_rows, deep, STEPS + rows),
    )
    for side, (begin, count, base, at_row, d_count, d_begin) in enumerate(sides):
        found = [packs[:, at_row + d_count + i, :] for i in range(lines)]

        def write(t, field, hits, key, side=side, begin=begin, count=count, at_row=at_row, d_count=d_count, d_begin=d_begin):
            at = slice(t * LANES, (t + 1) * LANES)
            d_all[d_begin : d_begin + d_count, at] = packs[t, at_row : at_row + d_count, :]
            first[begin : begin + count, at] = field * member[begin : begin + count, at]
            if side == 0:
                hits_all[t] = hits
                key_all[t] = jnp.broadcast_to(key, (8, key.shape[1]))

        fill(found, rows, levels, base, count, write)

    first[:, columns:] = jnp.zeros((first.shape[0], LANES), F32)
    second[:, columns:] = jnp.zeros((second.shape[0], LANES), F32)
    keep[...] = 1.0 - 4.0 * d_all[...]
    source, target = first, second
    for step in range(STEPS):
        for r in range(step + 1, 2 * STEPS + rows - 1 - step):
            mid = source[r * levels : (r + 1) * levels, :]
            beside = (
                source[(r - 1) * levels : r * levels, 0:columns]
                + source[(r + 1) * levels : (r + 2) * levels, 0:columns]
                + pltpu.roll(mid, 1, 1)[:, 0:columns]
                + pltpu.roll(mid, columns + LANES - 1, 1)[:, 0:columns]
            )
            d, c = (jnp.broadcast_to(x[r : r + 1, :], (levels, columns)) for x in (d_all, keep))
            target[r * levels : (r + 1) * levels, 0:columns] = c * mid[:, 0:columns] + d * beside
        source, target = target, source

    factors = [(i - BAND, factors_ref[i]) for i in range(2 * BAND + 1)]
    for t in range(tiles):
        at = slice(t * LANES, (t + 1) * LANES)
        parts = []
        for r in range(rows):
            x = source[half + r * levels : half + (r + 1) * levels, at]
            mixed = sum(f * (pltpu.roll(x, -o % levels, 0) if o else x) for o, f in factors)
            part = mixed * member[half + r * levels : half + (r + 1) * levels, at]
            made[t, r * levels : (r + 1) * levels, :] = part
            parts.append(part)
        stacked = jnp.concatenate(pieces(jnp.concatenate(parts, axis=0)), axis=0).astype(BF16)
        found = jnp.dot(stacked, hits_all[t], preferred_element_type=F32)
        found = found[0:own] + found[own : 2 * own] + found[2 * own :]
        on = iota(found.shape, 0).astype(F32) == key_all[t][0:1]
        line = jnp.sum(jnp.where(on, found, 0.0), axis=0, keepdims=True)
        for q in range(tiles // block):
            back[q, t : t + 1, :] = line[:, q * LANES : (q + 1) * LANES]
    for t in range(tiles):
        made[t, own:, :] = back[t // block]
    for z in range(mine_ref.shape[0]):
        for side, out in enumerate((mine_ref, other_ref)):
            out[z] = made[2 * z + (core ^ side ^ (chip != z).astype(jnp.int32))]


def pair_kernel(mine_ref, got_ref, *outs):
    chip = lax.axis_index("tx") // 2
    for far, out in enumerate(outs):
        out[...] = mine_ref[chip ^ far] + got_ref[chip ^ far]


def final_kernel(near, *refs):
    got, (live_ref, inc_ref, proj_ref, total) = refs[:near], refs[near:]
    levels, rows, _ = inc_ref.shape
    _, tiles, slots = proj_ref.shape
    sums = got[0][...]
    for ref in got[1:]:
        sums = sums + ref[...]
    total[...] = sums
    for level in range(levels):
        inc_ref[level] = total[pl.ds(level, rows, stride=levels), :]
    place = lax.rem(lax.axis_index("tx"), LANES // GROUP)
    lines = pltpu.roll(sums[rows * levels :], lax.rem(LANES - GROUP * place, LANES), 1)
    proj_ref[0] = jnp.where(live_ref[:, 0:slots] > 0.0, lines[:, 0:slots], 0.0)


def call(kernel, out_shape, ins, scratch, flops=0, moved=0):
    return pl.pallas_call(
        kernel,
        out_shape=out_shape,
        in_specs=ins,
        out_specs=jax.tree.map(lambda _: VMEM, out_shape),
        scratch_shapes=scratch,
        compiler_params=pltpu.CompilerParams(vmem_limit_bytes=48 << 20),
        cost_estimate=pl.CostEstimate(flops=flops, bytes_accessed=moved, transcendentals=0),
    )


def shards(ensemble, diffusivity, vertical, weights, obs_value, obs_cell, obs_count):
    _, levels, rows, columns = ensemble.shape
    tiles, slots = obs_value.shape[1:]
    chips = tiles // 2
    bands = lax.axis_size("ty")
    assert diffusivity.shape == (rows, LANES) and slots == GROUP and rows == 2 * STEPS
    block = min(tiles, LANES // GROUP)
    shape = jax.ShapeDtypeStruct
    lines = -(-2 * tiles * GROUP // LANES)
    half, own = STEPS * levels, rows * levels
    own_rows, halo_rows = rows + lines, STEPS - 1 + lines
    height, joined = round_up(own_rows, 8), round_up(own_rows + 2 * halo_rows, 8)
    lanes = tiles // block * LANES
    assert halo_rows <= rows

    def in_hbm(*arrays):
        return [pltpu.with_memory_space_constraint(x, pltpu.HBM) for x in arrays]

    def swap(x, far):
        return lax.ppermute(x, "tx", [(i, i ^ far) for i in range(tiles)])

    def swap_bands(x, low):
        mate = [i ^ 1 if low else i + 1 if i % 2 else i - 1 for i in range(bands)]
        pairs = [
            (i * tiles + k, mate[i] * tiles + k if 0 <= mate[i] < bands else i * tiles + (k ^ 1))
            for i in range(bands)
            for k in range(tiles)
        ]
        return lax.ppermute(x, ("ty", "tx"), pairs)

    sent = shape((tiles * half + 4 * rows, LANES), BF16)
    packet, turned, to_a, to_b, factors, live = call(
        first_kernel,
        (
            shape((height, LANES), F32),
            shape((tiles, own, LANES), BF16),
            sent,
            sent,
            shape((2 * BAND + 1, levels, LANES), F32),
            shape((tiles, LANES), F32),
        ),
        [HBM] * 7,
        [
            pltpu.VMEM(obs_value.shape, F32),
            pltpu.VMEM(obs_cell.shape, jnp.int32),
            pltpu.VMEM(obs_count.shape, jnp.int32),
            pltpu.VMEM(diffusivity.shape, F32),
            pltpu.VMEM(ensemble.shape, BF16),
            pltpu.VMEM(vertical.shape, F32),
            pltpu.SMEM(weights.shape, F32),
            pltpu.VMEM((2, tiles, LANES), F32),
            pltpu.VMEM((rows, LANES), F32),
            pltpu.VMEM((tiles, own, LANES), F32),
            pltpu.SemaphoreType.DMA((7,)),
        ],
    )(*in_hbm(obs_value, obs_cell, obs_count, diffusivity, ensemble, vertical, weights))
    from_a, from_b = swap_bands(to_a, True), swap_bands(to_b, False)
    mine = call(
        functools.partial(join_kernel, (own_rows, halo_rows), tiles * half),
        shape((joined, LANES), F32),
        [VMEM] * 3,
        [],
    )(packet, from_a, from_b)
    pair = jnp.stack([mine, swap(mine, 1)])
    row = [pair] + [swap(pair, 2 * far + 1) for far in range(1, chips)]

    chunk = own + tiles
    mine, other = call(
        functools.partial(main_kernel, chips, rows, levels, lines),
        (shape((chips, chunk, LANES), F32), shape((chips, chunk, LANES), F32)),
        [VMEM] * (chips + 4),
        [
            pltpu.VMEM((tiles, joined, LANES), F32),
            pltpu.VMEM((2 * half + own, columns), F32),
            pltpu.VMEM((2 * STEPS + rows, columns), F32),
            pltpu.VMEM((2 * STEPS + rows, columns), F32),
            pltpu.VMEM((tiles, LANES, lanes), BF16),
            pltpu.VMEM((tiles, 8, lanes), F32),
            pltpu.VMEM((2 * half + own, columns + LANES), F32),
            pltpu.VMEM((2 * half + own, columns + LANES), F32),
            pltpu.VMEM((tiles, chunk, LANES), F32),
            pltpu.VMEM((tiles // block, tiles, LANES), F32),
        ],
    )(*row, turned, from_a, from_b, factors)

    sums = call(
        pair_kernel, tuple(shape((chunk, LANES), F32) for _ in range(chips)), [VMEM] * 2, []
    )(mine, swap(other, 1))
    sums = [sums[0]] + [swap(sums[far], 2 * far + 1) for far in range(1, chips)]
    return call(
        functools.partial(final_kernel, chips),
        (shape((levels, rows, LANES), F32), shape((1, tiles, slots), F32)),
        [VMEM] * (chips + 1),
        [pltpu.VMEM((chunk, LANES), F32)],
    )(sums[0], *sums[:0:-1], live)


def solution(mesh):
    placed = (
        P("tx", None, "ty", None),
        P("ty", "tx"),
        P(),
        P(),
        P(("ty", "tx"), None, None),
        P(("ty", "tx"), None, None),
        P(("ty", "tx"), None),
    )
    return jax.shard_map(
        shards,
        mesh=mesh,
        in_specs=placed,
        out_specs=(P(None, "ty", "tx"), P(("ty", "tx"), None, None)),
        check_vma=False,
    )
```

```python
import functools

import jax
import jax.numpy as jnp
from jax import lax
from jax.experimental import pallas as pl
from jax.experimental.pallas import tpu as pltpu
from jax.sharding import PartitionSpec as P

STEPS = 4
BAND = 2
LANES = 128
GROUP = 8
CODES, FULL, LEAST = 128, 32700.0, 1.2e-38
F32, BF16 = jnp.float32, jnp.bfloat16
VMEM = pl.BlockSpec(memory_space=pltpu.VMEM)
HBM = pl.BlockSpec(memory_space=pltpu.HBM)


def round_up(n, m):
    return -(-n // m) * m


def log2(n):
    assert n & (n - 1) == 0
    return n.bit_length() - 1


def iota(shape, axis):
    return lax.broadcasted_iota(jnp.int32, shape, axis)


def pieces(x):
    high = x.astype(BF16).astype(F32)
    rest = x - high
    middle = rest.astype(BF16).astype(F32)
    return high, middle, rest - middle


def stagger(x):
    return pltpu.roll(x, 0, 1, stride=GROUP, stride_axis=0)


def pick(x, place):
    if isinstance(place, int):
        shift = (-GROUP * place) % LANES
    else:
        shift = lax.rem(LANES - GROUP * place, LANES)
    rolled = pltpu.roll(x, shift, 1)
    own = iota(x.shape, 1) // GROUP == iota(x.shape, 0)
    return jnp.sum(jnp.where(own, rolled, 0.0), axis=0, keepdims=True)


def live_mask(count_ref, slots):
    tiles = count_ref.shape[1]
    count = jnp.broadcast_to(count_ref[...].astype(F32), (tiles, tiles))
    diagonal = iota((tiles, tiles), 0) == iota((tiles, tiles), 1)
    column = jnp.sum(jnp.where(diagonal, count, 0.0), axis=1, keepdims=True)
    return iota((tiles, slots), 1).astype(F32) < column


def copy_in(sources, targets, sems):
    moves = [pltpu.make_async_copy(x, y, sems.at[i]) for i, (x, y) in enumerate(zip(sources, targets))]
    for move in moves:
        move.start()
    return moves


def first_kernel(
    value_hbm, cell_hbm, count_hbm, diff_hbm, ens_hbm, vertical_hbm, weights_hbm,
    packet, turned_ref, a_ref, b_ref, factors_ref, live_ref,
    value_ref, cell_ref, count_ref, diff_ref, ens_ref, vertical_ref, weights_ref, wide, part, tall, sems,
):
    moves = copy_in(
        (value_hbm, cell_hbm, count_hbm, diff_hbm, ens_hbm, vertical_hbm, weights_hbm),
        (value_ref, cell_ref, count_ref, diff_ref, ens_ref, vertical_ref, weights_ref),
        sems,
    )
    wide[...] = jnp.zeros_like(wide)
    for move in moves[:4]:
        move.wait()
    _, tiles, slots = value_ref.shape
    rows = diff_ref.shape[0]
    block = min(tiles, LANES // GROUP)
    live = live_mask(count_ref, slots)
    wide[0, :, 0:slots] = jnp.where(live, value_ref[0], 0.0)
    wide[1, :, 0:slots] = cell_ref[0].astype(F32)
    live_ref[...] = jnp.zeros_like(live_ref)
    live_ref[:, 0:slots] = jnp.where(live, 1.0, 0.0)
    packet[0:rows, :] = diff_ref[...]
    lines = [pick(stagger(wide[q, b : b + block, :]), 0) for q in range(2) for b in range(0, tiles, block)]
    if block * GROUP < LANES:
        lines = [lines[0] + pltpu.roll(lines[1], block * GROUP, 1)]
    packet[rows:, :] = jnp.zeros((packet.shape[0] - rows, LANES), F32)
    for i, line in enumerate(lines):
        packet[rows + i : rows + i + 1, :] = line
    deep, levels = STEPS - 1, ens_ref.shape[1]
    half = STEPS * levels
    even = lax.rem(lax.axis_index("ty"), 2) == 0
    top, low = diff_ref[...], pltpu.roll(diff_ref[...], deep, 0)
    for out, chosen in ((a_ref, jnp.where(even, low, top)), (b_ref, jnp.where(even, top, low))):
        part[...] = chosen
        for i, line in enumerate(lines):
            part[deep + i : deep + i + 1, :] = line
        split = jnp.concatenate([*pieces(part[...]), jnp.zeros((rows, LANES), F32)], axis=0)
        out[tiles * half :, :] = split.astype(BF16)

    for move in moves[4:]:
        move.wait()
    off_a, off_b = jnp.where(even, half, 0), jnp.where(even, 0, half)
    for t in range(tiles):
        at = slice(t * LANES, (t + 1) * LANES)
        tall[t] = ens_ref[0, :, :, at].astype(F32).reshape(levels * rows, LANES)
        for r in range(0, rows, 2):
            both = [tall[t, pl.ds(r + i, levels, stride=rows), :] for i in range(2)]
            turned_ref[t, r * levels : (r + 2) * levels, :] = jnp.concatenate(both, axis=0).astype(BF16)
        a_ref[t * half : (t + 1) * half, :] = turned_ref[t, pl.ds(pl.multiple_of(off_a, half), half), :]
        b_ref[t * half : (t + 1) * half, :] = turned_ref[t, pl.ds(pl.multiple_of(off_b, half), half), :]
    vertical = vertical_ref[...] * weights_ref[lax.axis_index("tx")]
    gap = iota((levels, levels), 1) - iota((levels, levels), 0)
    for i in range(2 * BAND + 1):
        factor = jnp.sum(jnp.where(gap == i - BAND, vertical, 0.0), axis=1, keepdims=True)
        factors_ref[i] = jnp.broadcast_to(factor, (levels, LANES))


def join_kernel(size, at, packet_ref, a_ref, b_ref, out_ref):
    band, last = lax.axis_index("ty"), lax.axis_size("ty") - 1
    even = lax.rem(band, 2) == 0
    own, halo = size
    got = [ref[at:, :].astype(F32) for ref in (a_ref, b_ref)]
    step = got[0].shape[0] // 4
    got_a, got_b = (x[0:step] + x[step : 2 * step] + x[2 * step : 3 * step] for x in got)
    above = jnp.where(band == 0, 0.0, jnp.where(even, got_b, got_a))
    below = jnp.where(band == last, 0.0, jnp.where(even, got_a, got_b))
    out_ref[0:own, :] = packet_ref[0:own, :]
    out_ref[own : own + halo, :] = above[0:halo]
    out_ref[own + halo : own + 2 * halo, :] = below[0:halo]
    rest = out_ref.shape[0] - own - 2 * halo
    if rest:
        out_ref[own + 2 * halo :, :] = jnp.zeros((rest, LANES), F32)


def lines_of(staggered, place, tiles):
    size = staggered[0][0].shape[0]
    groups = LANES // GROUP
    return jnp.concatenate([pick(part, place % groups) for part in staggered[place // groups]], axis=1)


def spread(line_value, line_key, hits, count, first):
    key = line_key - first
    on = iota((count, line_key.shape[1]), 0).astype(F32) == key
    stacked = jnp.concatenate([jnp.where(on, piece, 0.0) for piece in pieces(line_value)], axis=0)
    found = lax.dot_general(
        stacked.astype(BF16), hits, (((1,), (1,)), ((), ())), preferred_element_type=F32
    )
    return found[0:count] + found[count : 2 * count] + found[2 * count :]


def hits_of(line_column):
    shape = (LANES, line_column.shape[1])
    return jnp.where(iota(shape, 0).astype(F32) == line_column, 1.0, 0.0).astype(BF16)


def fill(lines, rows, levels, base, count, write):
    tiles = lines[0].shape[0]
    block = min(tiles, LANES // GROUP)
    values, keys, columns = [], [], []
    for x in lines:
        cell = x.astype(jnp.int32)
        flat = lax.shift_right_logical(cell, log2(LANES))
        key = (flat & (rows - 1)) * levels + lax.shift_right_logical(flat, log2(rows))
        for out, part in ((values, x), (keys, key.astype(F32)), (columns, (cell & (LANES - 1)).astype(F32))):
            out.append([stagger(part[q : q + block]) for q in range(0, tiles, block)])
    for t in range(tiles):
        value = lines_of(values, t, tiles)
        key, column = lines_of(keys, tiles + t, tiles), lines_of(columns, tiles + t, tiles)
        hits = hits_of(column)
        write(t, spread(value, key, hits, count, float(base)), hits, key)


def main_kernel(
    near, rows, levels, lines, *refs,
):
    got, refs = refs[:near], refs[near:]
    turned_ref, a_ref, b_ref, factors_ref, mine_ref, other_ref = refs[:6]
    packs, member, d_all, keep, hits_all, key_all, first, second, made, back = refs[6:]
    tiles = packs.shape[0]
    block = min(tiles, LANES // GROUP)
    columns = tiles * LANES
    band, me = lax.axis_index("ty"), lax.axis_index("tx")
    chip, core = me // 2, lax.rem(me, 2)
    even = lax.rem(band, 2) == 0
    half, own, deep = STEPS * levels, rows * levels, STEPS - 1

    own_rows, halo_rows = rows + lines, deep + lines
    for far, ref in enumerate(got):
        for side in range(2):
            packs[2 * (chip ^ far) + (core ^ side ^ (far > 0))] = ref[side]

    for t in range(tiles):
        at = slice(t * LANES, (t + 1) * LANES)
        member[half : half + own, at] = turned_ref[t].astype(F32)
        got_a, got_b = (ref[t * half : (t + 1) * half, :].astype(F32) for ref in (a_ref, b_ref))
        member[0:half, at] = jnp.where(even, got_b, got_a)
        member[half + own :, at] = jnp.where(even, got_a, got_b)
    sides = (
        (half, own, 0, 0, rows, STEPS),
        (0, half, own - half, own_rows, deep, 1),
        (half + own, half, 0, own_rows + halo_rows, deep, STEPS + rows),
    )
    for side, (begin, count, base, at_row, d_count, d_begin) in enumerate(sides):
        found = [packs[:, at_row + d_count + i, :] for i in range(lines)]

        def write(t, field, hits, key, side=side, begin=begin, count=count, at_row=at_row, d_count=d_count, d_begin=d_begin):
            at = slice(t * LANES, (t + 1) * LANES)
            d_all[d_begin : d_begin + d_count, at] = packs[t, at_row : at_row + d_count, :]
            first[begin : begin + count, at] = field * member[begin : begin + count, at]
            if side == 0:
                hits_all[t] = hits
                key_all[t] = jnp.broadcast_to(key, (8, key.shape[1]))

        fill(found, rows, levels, base, count, write)

    first[:, columns:] = jnp.zeros((first.shape[0], LANES), F32)
    second[:, columns:] = jnp.zeros((second.shape[0], LANES), F32)
    keep[...] = 1.0 - 4.0 * d_all[...]
    source, target = first, second
    for step in range(STEPS):
        for r in range(step + 1, 2 * STEPS + rows - 1 - step):
            mid = source[r * levels : (r + 1) * levels, :]
            beside = (
                source[(r - 1) * levels : r * levels, 0:columns]
                + source[(r + 1) * levels : (r + 2) * levels, 0:columns]
                + pltpu.roll(mid, 1, 1)[:, 0:columns]
                + pltpu.roll(mid, columns + LANES - 1, 1)[:, 0:columns]
            )
            d, c = (jnp.broadcast_to(x[r : r + 1, :], (levels, columns)) for x in (d_all, keep))
            target[r * levels : (r + 1) * levels, 0:columns] = c * mid[:, 0:columns] + d * beside
        source, target = target, source

    factors = [(i - BAND, factors_ref[i]) for i in range(2 * BAND + 1)]
    for t in range(tiles):
        at = slice(t * LANES, (t + 1) * LANES)
        parts = []
        for r in range(rows):
            x = source[half + r * levels : half + (r + 1) * levels, at]
            mixed = sum(f * (pltpu.roll(x, -o % levels, 0) if o else x) for o, f in factors)
            part = mixed * member[half + r * levels : half + (r + 1) * levels, at]
            made[t, r * levels : (r + 1) * levels, :] = part
            parts.append(part)
        stacked = jnp.concatenate(pieces(jnp.concatenate(parts, axis=0)), axis=0).astype(BF16)
        found = jnp.dot(stacked, hits_all[t], preferred_element_type=F32)
        found = found[0:own] + found[own : 2 * own] + found[2 * own :]
        on = iota(found.shape, 0).astype(F32) == key_all[t][0:1]
        line = jnp.sum(jnp.where(on, found, 0.0), axis=0, keepdims=True)
        for q in range(tiles // block):
            back[q, t : t + 1, :] = line[:, q * LANES : (q + 1) * LANES]
    for t in range(tiles):
        made[t, own:, :] = back[t // block]
    for z in range(mine_ref.shape[0]):
        for side, out in enumerate((mine_ref, other_ref)):
            out[z] = made[2 * z + (core ^ side ^ (chip != z).astype(jnp.int32))]


def scale_of(code):
    return jnp.exp2(code.astype(F32) * (1.0 / CODES))


def pair_kernel(split, mine_ref, got_ref, near_ref, *outs):
    chip = lax.axis_index("tx") // 2
    near_ref[...] = mine_ref[chip] + got_ref[chip]
    for far, out in enumerate(outs, 1):
        x = mine_ref[chip ^ far] + got_ref[chip ^ far]
        whole, codes = [], []
        for part in (x[0:split], x[split:]):
            largest = jnp.maximum(jnp.max(jnp.abs(part), axis=0, keepdims=True), LEAST)
            code = jnp.minimum(jnp.ceil(jnp.log2(largest) * CODES).astype(jnp.int32), CODES * 128 - 1)
            sized = jnp.clip(part * (1.0 / scale_of(code)), -1.0, 1.0)
            whole.append(jnp.floor(sized * FULL + 0.5).astype(jnp.int32))
            codes.append(code)
        rest = out.shape[0] - x.shape[0]
        row = iota((rest, LANES), 0)
        tail = jnp.where(row == 0, codes[0], jnp.where(row == 1, codes[1], 0))
        out[...] = jnp.concatenate([*whole, tail], axis=0).astype(jnp.int16)


def final_kernel(split, *refs):
    got, (live_ref, inc_ref, proj_ref, total) = refs[:-4], refs[-4:]
    levels, rows, _ = inc_ref.shape
    _, tiles, slots = proj_ref.shape
    size = got[0].shape[0]
    top, low = got[0][0:split, :], got[0][split:, :]
    for ref in got[1:]:
        x = ref[...].astype(jnp.int32)
        sent = x[0:size].astype(F32) * (1.0 / FULL)
        top = top + sent[0:split] * scale_of(x[size : size + 1])
        low = low + sent[split:] * scale_of(x[size + 1 : size + 2])
    total[...] = top
    for level in range(levels):
        inc_ref[level] = total[pl.ds(level, rows, stride=levels), :]
    place = lax.rem(lax.axis_index("tx"), LANES // GROUP)
    lines = pltpu.roll(low, lax.rem(LANES - GROUP * place, LANES), 1)
    proj_ref[0] = jnp.where(live_ref[:, 0:slots] > 0.0, lines[:, 0:slots], 0.0)


def call(kernel, out_shape, ins, scratch, flops=0, moved=0):
    return pl.pallas_call(
        kernel,
        out_shape=out_shape,
        in_specs=ins,
        out_specs=jax.tree.map(lambda _: VMEM, out_shape),
        scratch_shapes=scratch,
        compiler_params=pltpu.CompilerParams(vmem_limit_bytes=48 << 20),
        cost_estimate=pl.CostEstimate(flops=flops, bytes_accessed=moved, transcendentals=0),
    )


def shards(ensemble, diffusivity, vertical, weights, obs_value, obs_cell, obs_count):
    _, levels, rows, columns = ensemble.shape
    tiles, slots = obs_value.shape[1:]
    chips = tiles // 2
    bands = lax.axis_size("ty")
    assert diffusivity.shape == (rows, LANES) and slots == GROUP and rows == 2 * STEPS
    block = min(tiles, LANES // GROUP)
    shape = jax.ShapeDtypeStruct
    lines = -(-2 * tiles * GROUP // LANES)
    half, own = STEPS * levels, rows * levels
    own_rows, halo_rows = rows + lines, STEPS - 1 + lines
    height, joined = round_up(own_rows, 8), round_up(own_rows + 2 * halo_rows, 8)
    lanes = tiles // block * LANES
    assert halo_rows <= rows

    def in_hbm(*arrays):
        return [pltpu.with_memory_space_constraint(x, pltpu.HBM) for x in arrays]

    def swap(x, far):
        return lax.ppermute(x, "tx", [(i, i ^ far) for i in range(tiles)])

    def swap_bands(x, low):
        mate = [i ^ 1 if low else i + 1 if i % 2 else i - 1 for i in range(bands)]
        pairs = [
            (i * tiles + k, mate[i] * tiles + k if 0 <= mate[i] < bands else i * tiles + (k ^ 1))
            for i in range(bands)
            for k in range(tiles)
        ]
        return lax.ppermute(x, ("ty", "tx"), pairs)

    sent = shape((tiles * half + 4 * rows, LANES), BF16)
    packet, turned, to_a, to_b, factors, live = call(
        first_kernel,
        (
            shape((height, LANES), F32),
            shape((tiles, own, LANES), BF16),
            sent,
            sent,
            shape((2 * BAND + 1, levels, LANES), F32),
            shape((tiles, LANES), F32),
        ),
        [HBM] * 7,
        [
            pltpu.VMEM(obs_value.shape, F32),
            pltpu.VMEM(obs_cell.shape, jnp.int32),
            pltpu.VMEM(obs_count.shape, jnp.int32),
            pltpu.VMEM(diffusivity.shape, F32),
            pltpu.VMEM(ensemble.shape, BF16),
            pltpu.VMEM(vertical.shape, F32),
            pltpu.SMEM(weights.shape, F32),
            pltpu.VMEM((2, tiles, LANES), F32),
            pltpu.VMEM((rows, LANES), F32),
            pltpu.VMEM((tiles, own, LANES), F32),
            pltpu.SemaphoreType.DMA((7,)),
        ],
    )(*in_hbm(obs_value, obs_cell, obs_count, diffusivity, ensemble, vertical, weights))
    from_a, from_b = swap_bands(to_a, True), swap_bands(to_b, False)
    mine = call(
        functools.partial(join_kernel, (own_rows, halo_rows), tiles * half),
        shape((joined, LANES), F32),
        [VMEM] * 3,
        [],
    )(packet, from_a, from_b)
    pair = jnp.stack([mine, swap(mine, 1)])
    row = [pair] + [swap(pair, 2 * far + 1) for far in range(1, chips)]

    chunk = own + tiles
    mine, other = call(
        functools.partial(main_kernel, chips, rows, levels, lines),
        (shape((chips, chunk, LANES), F32), shape((chips, chunk, LANES), F32)),
        [VMEM] * (chips + 4),
        [
            pltpu.VMEM((tiles, joined, LANES), F32),
            pltpu.VMEM((2 * half + own, columns), F32),
            pltpu.VMEM((2 * STEPS + rows, columns), F32),
            pltpu.VMEM((2 * STEPS + rows, columns), F32),
            pltpu.VMEM((tiles, LANES, lanes), BF16),
            pltpu.VMEM((tiles, 8, lanes), F32),
            pltpu.VMEM((2 * half + own, columns + LANES), F32),
            pltpu.VMEM((2 * half + own, columns + LANES), F32),
            pltpu.VMEM((tiles, chunk, LANES), F32),
            pltpu.VMEM((tiles // block, tiles, LANES), F32),
        ],
    )(*row, turned, from_a, from_b, factors)

    coded = shape((round_up(chunk + 2, 16), LANES), jnp.int16)
    sums = call(
        functools.partial(pair_kernel, own), (shape((chunk, LANES), F32), *[coded] * (chips - 1)), [VMEM] * 2, []
    )(mine, swap(other, 1))
    sums = [sums[0]] + [swap(sums[far], 2 * far + 1) for far in range(1, chips)]
    return call(
        functools.partial(final_kernel, own),
        (shape((levels, rows, LANES), F32), shape((1, tiles, slots), F32)),
        [VMEM] * (chips + 1),
        [pltpu.VMEM((own, LANES), F32)],
    )(sums[0], *sums[:0:-1], live)


def solution(mesh):
    placed = (
        P("tx", None, "ty", None),
        P("ty", "tx"),
        P(),
        P(),
        P(("ty", "tx"), None, None),
        P(("ty", "tx"), None, None),
        P(("ty", "tx"), None),
    )
    return jax.shard_map(
        shards,
        mesh=mesh,
        in_specs=placed,
        out_specs=(P(None, "ty", "tx"), P(("ty", "tx"), None, None)),
        check_vma=False,
    )
```

```python
import functools

import jax
import jax.numpy as jnp
from jax import lax
from jax.experimental import pallas as pl
from jax.experimental.pallas import tpu as pltpu
from jax.sharding import PartitionSpec as P

STEPS = 4
BAND = 2
LANES = 128
GROUP = 8
CODES, FULL, LEAST = 128, 32700.0, 1.2e-38
F32, BF16 = jnp.float32, jnp.bfloat16
VMEM = pl.BlockSpec(memory_space=pltpu.VMEM)
HBM = pl.BlockSpec(memory_space=pltpu.HBM)


def round_up(n, m):
    return -(-n // m) * m


def log2(n):
    assert n & (n - 1) == 0
    return n.bit_length() - 1


def iota(shape, axis):
    return lax.broadcasted_iota(jnp.int32, shape, axis)


def pieces(x):
    high = x.astype(BF16).astype(F32)
    rest = x - high
    middle = rest.astype(BF16).astype(F32)
    return high, middle, rest - middle


def stagger(x):
    return pltpu.roll(x, 0, 1, stride=GROUP, stride_axis=0)


def pick(x, place):
    if isinstance(place, int):
        shift = (-GROUP * place) % LANES
    else:
        shift = lax.rem(LANES - GROUP * place, LANES)
    rolled = pltpu.roll(x, shift, 1)
    own = iota(x.shape, 1) // GROUP == iota(x.shape, 0)
    return jnp.sum(jnp.where(own, rolled, 0.0), axis=0, keepdims=True)


def live_mask(count_ref, slots):
    tiles = count_ref.shape[1]
    count = jnp.broadcast_to(count_ref[...].astype(F32), (tiles, tiles))
    diagonal = iota((tiles, tiles), 0) == iota((tiles, tiles), 1)
    column = jnp.sum(jnp.where(diagonal, count, 0.0), axis=1, keepdims=True)
    return iota((tiles, slots), 1).astype(F32) < column


def copy_in(sources, targets, sems):
    moves = [pltpu.make_async_copy(x, y, sems.at[i]) for i, (x, y) in enumerate(zip(sources, targets))]
    for move in moves:
        move.start()
    return moves


def packet_kernel(
    value_hbm, cell_hbm, count_hbm, diff_hbm, packet, live_ref,
    value_ref, cell_ref, count_ref, diff_ref, wide, sems,
):
    moves = copy_in(
        (value_hbm, cell_hbm, count_hbm, diff_hbm), (value_ref, cell_ref, count_ref, diff_ref), sems
    )
    wide[...] = jnp.zeros_like(wide)
    for move in moves:
        move.wait()
    _, tiles, slots = value_ref.shape
    rows = diff_ref.shape[0]
    block = min(tiles, LANES // GROUP)
    live = live_mask(count_ref, slots)
    wide[0, :, 0:slots] = jnp.where(live, value_ref[0], 0.0)
    wide[1, :, 0:slots] = cell_ref[0].astype(F32)
    live_ref[...] = jnp.zeros_like(live_ref)
    live_ref[:, 0:slots] = jnp.where(live, 1.0, 0.0)
    packet[0:rows, :] = diff_ref[...]
    lines = [pick(stagger(wide[q, b : b + block, :]), 0) for q in range(2) for b in range(0, tiles, block)]
    if block * GROUP < LANES:
        lines = [lines[0] + pltpu.roll(lines[1], block * GROUP, 1)]
    packet[rows:, :] = jnp.zeros((packet.shape[0] - rows, LANES), F32)
    for i, line in enumerate(lines):
        packet[rows + i : rows + i + 1, :] = line


def member_kernel(
    ens_hbm, vertical_hbm, weights_hbm, turned_ref, factors_ref,
    ens_ref, vertical_ref, weights_ref, tall, sems,
):
    moves = copy_in((vertical_hbm, weights_hbm, ens_hbm), (vertical_ref, weights_ref, ens_ref), sems)
    for move in moves:
        move.wait()
    _, levels, rows, columns = ens_ref.shape
    for t in range(columns // LANES):
        at = slice(t * LANES, (t + 1) * LANES)
        tall[t] = ens_ref[0, :, :, at].astype(F32).reshape(levels * rows, LANES)
        for r in range(0, rows, 2):
            both = [tall[t, pl.ds(r + i, levels, stride=rows), :] for i in range(2)]
            turned_ref[t, r * levels : (r + 2) * levels, :] = jnp.concatenate(both, axis=0).astype(BF16)
    vertical = vertical_ref[...] * weights_ref[lax.axis_index("tx")]
    gap = iota((levels, levels), 1) - iota((levels, levels), 0)
    for i in range(2 * BAND + 1):
        factor = jnp.sum(jnp.where(gap == i - BAND, vertical, 0.0), axis=1, keepdims=True)
        factors_ref[i] = jnp.broadcast_to(factor, (levels, LANES))


def lines_of(staggered, place, tiles):
    size = staggered[0][0].shape[0]
    groups = LANES // GROUP
    return jnp.concatenate([pick(part, place % groups) for part in staggered[place // groups]], axis=1)


def spread(line_value, line_key, hits, count, first):
    key = line_key - first
    on = iota((count, line_key.shape[1]), 0).astype(F32) == key
    stacked = jnp.concatenate([jnp.where(on, piece, 0.0) for piece in pieces(line_value)], axis=0)
    found = lax.dot_general(
        stacked.astype(BF16), hits, (((1,), (1,)), ((), ())), preferred_element_type=F32
    )
    return found[0:count] + found[count : 2 * count] + found[2 * count :]


def hits_of(line_column):
    shape = (LANES, line_column.shape[1])
    return jnp.where(iota(shape, 0).astype(F32) == line_column, 1.0, 0.0).astype(BF16)


def gather_kernel(near, rows, lines, levels, *refs):
    got, (turned_ref, d_ref, slots_ref, hits_ref, a_ref, b_ref, packs) = refs[:near], refs[near:]
    tiles = packs.shape[0]
    size = min(tiles, LANES // GROUP)
    me, even = lax.axis_index("tx"), lax.rem(lax.axis_index("ty"), 2) == 0
    chip, core = me // 2, lax.rem(me, 2)
    for far, ref in enumerate(got):
        for side in range(2):
            packs[2 * (chip ^ far) + (core ^ side ^ (far > 0))] = ref[side]
    values, keys, columns = [], [], []
    for i in range(lines):
        x = packs[:, rows + i, :]
        cell = x.astype(jnp.int32)
        flat = lax.shift_right_logical(cell, log2(LANES))
        key = (flat & (rows - 1)) * levels + lax.shift_right_logical(flat, log2(rows))
        for out, part in ((values, x), (keys, key.astype(F32)), (columns, (cell & (LANES - 1)).astype(F32))):
            out.append([stagger(part[q : q + size]) for q in range(0, tiles, size)])
    deep = STEPS - 1
    for t in range(tiles):
        value = lines_of(values, t, tiles)
        key, column = lines_of(keys, tiles + t, tiles), lines_of(columns, tiles + t, tiles)
        hits = hits_of(column)
        hits_ref[t] = hits
        found = jnp.dot(turned_ref[t], hits, preferred_element_type=F32)
        on = iota(found.shape, 0).astype(F32) == key
        product = value * jnp.sum(jnp.where(on, found, 0.0), axis=0, keepdims=True)
        d = packs[t, 0:rows, :]
        d_ref[:, t * LANES : (t + 1) * LANES] = d
        low = pltpu.roll(d, deep, 0)
        for out, part in ((a_ref, jnp.where(even, low, d)), (b_ref, jnp.where(even, d, low))):
            out[t, 0:rows, :] = part
            for i, line in enumerate((product, key, column)):
                for q in range(tiles // size):
                    out[t, deep + 3 * q + i : deep + 3 * q + i + 1, :] = line[:, q * LANES : (q + 1) * LANES]
        for i, line in enumerate((product, key)):
            slots_ref[t, i : i + 1, :] = line


def own_kernel(slots_ref, hits_ref, start_ref):
    count = start_ref.shape[0]
    for t in range(slots_ref.shape[0]):
        at = slice(t * LANES, (t + 1) * LANES)
        start_ref[:, at] = spread(slots_ref[t, 0:1, :], slots_ref[t, 1:2, :], hits_ref[t], count, 0.0)


def main_kernel(
    rows, levels, start_ref, d_ref, slots_ref, hits_ref, turned_ref, a_ref, b_ref, factors_ref, mine_ref, other_ref,
    member, d_all, keep, first, second, made, back,
):
    tiles = hits_ref.shape[0]
    block = min(tiles, LANES // GROUP)
    columns = tiles * LANES
    band, last, me = lax.axis_index("ty"), lax.axis_size("ty") - 1, lax.axis_index("tx")
    chip, core = me // 2, lax.rem(me, 2)
    even = lax.rem(band, 2) == 0
    half, own, deep = STEPS * levels, rows * levels, STEPS - 1

    first[half : half + own, 0:columns] = start_ref[...]
    d_all[STEPS : STEPS + rows, :] = d_ref[...]
    for t in range(tiles):
        at = slice(t * LANES, (t + 1) * LANES)
        member[:, at] = turned_ref[t].astype(F32)
        got_a, got_b = a_ref[t], b_ref[t]
        above = jnp.where(band == 0, 0.0, jnp.where(even, got_b, got_a))
        below = jnp.where(band == last, 0.0, jnp.where(even, got_a, got_b))
        for got, begin, base, d_begin in ((above, 0, own - half, 1), (below, half + own, 0, STEPS + rows)):
            d_all[d_begin : d_begin + deep, at] = got[0:deep]
            product, key, column = (
                jnp.concatenate([got[deep + 3 * q + i : deep + 3 * q + i + 1] for q in range(tiles // block)], axis=1)
                for i in range(3)
            )
            first[begin : begin + half, at] = spread(product, key, hits_of(column), half, float(base))

    first[:, columns:] = jnp.zeros((first.shape[0], LANES), F32)
    second[:, columns:] = jnp.zeros((second.shape[0], LANES), F32)
    keep[...] = 1.0 - 4.0 * d_all[...]
    factors = [(i - BAND, factors_ref[i]) for i in range(2 * BAND + 1)]
    source, target = first, second
    for step in range(STEPS):
        for r in range(step + 1, 2 * STEPS + rows - 1 - step):
            mid = source[r * levels : (r + 1) * levels, :]
            beside = (
                source[(r - 1) * levels : r * levels, 0:columns]
                + source[(r + 1) * levels : (r + 2) * levels, 0:columns]
                + pltpu.roll(mid, 1, 1)[:, 0:columns]
                + pltpu.roll(mid, columns + LANES - 1, 1)[:, 0:columns]
            )
            d, c = (jnp.broadcast_to(x[r : r + 1, :], (levels, columns)) for x in (d_all, keep))
            x = c * mid[:, 0:columns] + d * beside
            if step < STEPS - 1:
                target[r * levels : (r + 1) * levels, 0:columns] = x
                continue
            row = slice((r - STEPS) * levels, (r - STEPS + 1) * levels)
            for t in range(tiles):
                at = slice(t * LANES, (t + 1) * LANES)
                mixed = sum(f * (pltpu.roll(x[:, at], -o % levels, 0) if o else x[:, at]) for o, f in factors)
                made[t, row, :] = mixed * member[row, at]
        source, target = target, source

    for t in range(tiles):
        stacked = jnp.concatenate(pieces(made[t]), axis=0).astype(BF16)
        found = jnp.dot(stacked, hits_ref[t], preferred_element_type=F32)
        found = found[0:own] + found[own : 2 * own] + found[2 * own :]
        on = iota(found.shape, 0).astype(F32) == slots_ref[t, 1:2, :]
        line = jnp.sum(jnp.where(on, found, 0.0), axis=0, keepdims=True)
        for q in range(tiles // block):
            back[q, t : t + 1, :] = line[:, q * LANES : (q + 1) * LANES]
    for z in range(mine_ref.shape[0]):
        for side, out in enumerate((mine_ref, other_ref)):
            out[z, 0:own, :] = made[2 * z + (core ^ side ^ (chip != z).astype(jnp.int32))]
            out[z, own:, :] = back[2 * z // block]


def scale_of(code):
    return jnp.exp2(code.astype(F32) * (1.0 / CODES))


def pair_kernel(split, mine_ref, got_ref, near_ref, *outs):
    chip = lax.axis_index("tx") // 2
    near_ref[...] = mine_ref[chip] + got_ref[chip]
    for far, out in enumerate(outs, 1):
        x = mine_ref[chip ^ far] + got_ref[chip ^ far]
        whole, codes = [], []
        for part in (x[0:split], x[split:]):
            largest = jnp.maximum(jnp.max(jnp.abs(part), axis=0, keepdims=True), LEAST)
            code = jnp.minimum(jnp.ceil(jnp.log2(largest) * CODES).astype(jnp.int32), CODES * 128 - 1)
            sized = jnp.clip(part * (1.0 / scale_of(code)), -1.0, 1.0)
            whole.append(jnp.floor(sized * FULL + 0.5).astype(jnp.int32))
            codes.append(code)
        rest = out.shape[0] - x.shape[0]
        row = iota((rest, LANES), 0)
        tail = jnp.where(row == 0, codes[0], jnp.where(row == 1, codes[1], 0))
        out[...] = jnp.concatenate([*whole, tail], axis=0).astype(jnp.int16)


def final_kernel(split, *refs):
    got, (live_ref, inc_ref, proj_ref, total) = refs[:-4], refs[-4:]
    levels, rows, _ = inc_ref.shape
    _, tiles, slots = proj_ref.shape
    size = got[0].shape[0]
    top, low = got[0][0:split, :], got[0][split:, :]
    for ref in got[1:]:
        x = ref[...].astype(jnp.int32)
        sent = x[0:size].astype(F32) * (1.0 / FULL)
        top = top + sent[0:split] * scale_of(x[size : size + 1])
        low = low + sent[split:] * scale_of(x[size + 1 : size + 2])
    total[...] = top
    for level in range(levels):
        inc_ref[level] = total[pl.ds(level, rows, stride=levels), :]
    place = lax.rem(lax.axis_index("tx"), LANES // GROUP)
    lines = pltpu.roll(low, lax.rem(LANES - GROUP * place, LANES), 1)
    proj_ref[0] = jnp.where(live_ref[:, 0:slots] > 0.0, lines[:, 0:slots], 0.0)


def call(kernel, out_shape, ins, scratch, flops=0, moved=0):
    return pl.pallas_call(
        kernel,
        out_shape=out_shape,
        in_specs=ins,
        out_specs=jax.tree.map(lambda _: VMEM, out_shape),
        scratch_shapes=scratch,
        compiler_params=pltpu.CompilerParams(vmem_limit_bytes=48 << 20),
        cost_estimate=pl.CostEstimate(flops=flops, bytes_accessed=moved, transcendentals=0),
    )


def shards(ensemble, diffusivity, vertical, weights, obs_value, obs_cell, obs_count):
    _, levels, rows, columns = ensemble.shape
    tiles, slots = obs_value.shape[1:]
    chips = tiles // 2
    bands = lax.axis_size("ty")
    assert diffusivity.shape == (rows, LANES) and slots == GROUP and rows == 2 * STEPS
    block = min(tiles, LANES // GROUP)
    shape = jax.ShapeDtypeStruct
    lines = -(-2 * tiles * GROUP // LANES)
    half, own = STEPS * levels, rows * levels
    height, halo_height = round_up(rows + lines, 8), round_up(max(rows, STEPS - 1 + 3 * (tiles // block)), 8)
    lanes = tiles // block * LANES

    def in_hbm(*arrays):
        return [pltpu.with_memory_space_constraint(x, pltpu.HBM) for x in arrays]

    def swap(x, far):
        return lax.ppermute(x, "tx", [(i, i ^ far) for i in range(tiles)])

    def swap_bands(x, low):
        mate = [i ^ 1 if low else i + 1 if i % 2 else i - 1 for i in range(bands)]
        pairs = [
            (i * tiles + k, mate[i] * tiles + k if 0 <= mate[i] < bands else i * tiles + (k ^ 1))
            for i in range(bands)
            for k in range(tiles)
        ]
        return lax.ppermute(x, ("ty", "tx"), pairs)

    packet, live = call(
        packet_kernel,
        (shape((height, LANES), F32), shape((tiles, LANES), F32)),
        [HBM] * 4,
        [
            pltpu.VMEM(obs_value.shape, F32),
            pltpu.VMEM(obs_cell.shape, jnp.int32),
            pltpu.VMEM(obs_count.shape, jnp.int32),
            pltpu.VMEM(diffusivity.shape, F32),
            pltpu.VMEM((2, tiles, LANES), F32),
            pltpu.SemaphoreType.DMA((4,)),
        ],
    )(*in_hbm(obs_value, obs_cell, obs_count, diffusivity))
    turned, factors = call(
        member_kernel,
        (shape((tiles, own, LANES), BF16), shape((2 * BAND + 1, levels, LANES), F32)),
        [HBM] * 3,
        [
            pltpu.VMEM(ensemble.shape, BF16),
            pltpu.VMEM(vertical.shape, F32),
            pltpu.SMEM(weights.shape, F32),
            pltpu.VMEM((tiles, own, LANES), F32),
            pltpu.SemaphoreType.DMA((3,)),
        ],
        1000000,
        1000000,
    )(*in_hbm(ensemble, vertical, weights))

    pair = jnp.stack([packet, swap(packet, 1)])
    row = [pair] + [swap(pair, 2 * far + 1) for far in range(1, chips)]
    halo = shape((tiles, halo_height, LANES), F32)
    d_row, slots_row, hits, to_a, to_b = call(
        functools.partial(gather_kernel, chips, rows, lines, levels),
        (
            shape((rows, columns), F32),
            shape((tiles, 8, lanes), F32),
            shape((tiles, LANES, lanes), BF16),
            halo,
            halo,
        ),
        [VMEM] * (chips + 1),
        [pltpu.VMEM((tiles, height, LANES), F32)],
    )(*row, turned)
    from_a, from_b = swap_bands(to_a, True), swap_bands(to_b, False)
    start = call(own_kernel, shape((own, columns), F32), [VMEM] * 2, [], 1000000, 1000000)(slots_row, hits)

    chunk = own + tiles
    mine, other = call(
        functools.partial(main_kernel, rows, levels),
        (shape((chips, chunk, LANES), F32), shape((chips, chunk, LANES), F32)),
        [VMEM] * 8,
        [
            pltpu.VMEM((own, columns), F32),
            pltpu.VMEM((2 * STEPS + rows, columns), F32),
            pltpu.VMEM((2 * STEPS + rows, columns), F32),
            pltpu.VMEM((2 * half + own, columns + LANES), F32),
            pltpu.VMEM((2 * half + own, columns + LANES), F32),
            pltpu.VMEM((tiles, own, LANES), F32),
            pltpu.VMEM((tiles // block, tiles, LANES), F32),
        ],
    )(start, d_row, slots_row, hits, turned, from_a, from_b, factors)

    coded = shape((round_up(chunk + 2, 16), LANES), jnp.int16)
    sums = call(
        functools.partial(pair_kernel, own), (shape((chunk, LANES), F32), *[coded] * (chips - 1)), [VMEM] * 2, []
    )(mine, swap(other, 1))
    sums = [sums[0]] + [swap(sums[far], 2 * far + 1) for far in range(1, chips)]
    return call(
        functools.partial(final_kernel, own),
        (shape((levels, rows, LANES), F32), shape((1, tiles, slots), F32)),
        [VMEM] * (chips + 1),
        [pltpu.VMEM((own, LANES), F32)],
    )(sums[0], *sums[:0:-1], live)


def solution(mesh):
    placed = (
        P("tx", None, "ty", None),
        P("ty", "tx"),
        P(),
        P(),
        P(("ty", "tx"), None, None),
        P(("ty", "tx"), None, None),
        P(("ty", "tx"), None),
    )
    return jax.shard_map(
        shards,
        mesh=mesh,
        in_specs=placed,
        out_specs=(P(None, "ty", "tx"), P(("ty", "tx"), None, None)),
        check_vma=False,
    )
```

```python
import functools

import jax
import jax.numpy as jnp
from jax import lax
from jax.experimental import pallas as pl
from jax.experimental.pallas import tpu as pltpu
from jax.sharding import PartitionSpec as P

STEPS = 4
BAND = 2
LANES = 128
GROUP = 8
CODES, FULL, LEAST = 128, 32700.0, 1.2e-38
F32, BF16 = jnp.float32, jnp.bfloat16
VMEM = pl.BlockSpec(memory_space=pltpu.VMEM)
HBM = pl.BlockSpec(memory_space=pltpu.HBM)


def round_up(n, m):
    return -(-n // m) * m


def log2(n):
    assert n & (n - 1) == 0
    return n.bit_length() - 1


def iota(shape, axis):
    return lax.broadcasted_iota(jnp.int32, shape, axis)


def pieces(x):
    high = x.astype(BF16).astype(F32)
    rest = x - high
    middle = rest.astype(BF16).astype(F32)
    return high, middle, rest - middle


def stagger(x):
    return pltpu.roll(x, 0, 1, stride=GROUP, stride_axis=0)


def pick(x, place):
    if isinstance(place, int):
        shift = (-GROUP * place) % LANES
    else:
        shift = lax.rem(LANES - GROUP * place, LANES)
    rolled = pltpu.roll(x, shift, 1)
    own = iota(x.shape, 1) // GROUP == iota(x.shape, 0)
    return jnp.sum(jnp.where(own, rolled, 0.0), axis=0, keepdims=True)


def live_mask(count_ref, slots):
    tiles = count_ref.shape[1]
    count = jnp.broadcast_to(count_ref[...].astype(F32), (tiles, tiles))
    diagonal = iota((tiles, tiles), 0) == iota((tiles, tiles), 1)
    column = jnp.sum(jnp.where(diagonal, count, 0.0), axis=1, keepdims=True)
    return iota((tiles, slots), 1).astype(F32) < column


def copy_in(sources, targets, sems):
    moves = [pltpu.make_async_copy(x, y, sems.at[i]) for i, (x, y) in enumerate(zip(sources, targets))]
    for move in moves:
        move.start()
    return moves


def packet_kernel(
    value_hbm, cell_hbm, count_hbm, diff_hbm, packet, live_ref,
    value_ref, cell_ref, count_ref, diff_ref, wide, sems,
):
    moves = copy_in(
        (value_hbm, cell_hbm, count_hbm, diff_hbm), (value_ref, cell_ref, count_ref, diff_ref), sems
    )
    wide[...] = jnp.zeros_like(wide)
    for move in moves:
        move.wait()
    _, tiles, slots = value_ref.shape
    rows = diff_ref.shape[0]
    block = min(tiles, LANES // GROUP)
    live = live_mask(count_ref, slots)
    wide[0, :, 0:slots] = jnp.where(live, value_ref[0], 0.0)
    wide[1, :, 0:slots] = cell_ref[0].astype(F32)
    live_ref[...] = jnp.zeros_like(live_ref)
    live_ref[:, 0:slots] = jnp.where(live, 1.0, 0.0)
    packet[0:rows, :] = diff_ref[...]
    lines = [pick(stagger(wide[q, b : b + block, :]), 0) for q in range(2) for b in range(0, tiles, block)]
    if block * GROUP < LANES:
        lines = [lines[0] + pltpu.roll(lines[1], block * GROUP, 1)]
    packet[rows:, :] = jnp.zeros((packet.shape[0] - rows, LANES), F32)
    for i, line in enumerate(lines):
        packet[rows + i : rows + i + 1, :] = line


def member_kernel(
    ens_hbm, vertical_hbm, weights_hbm, turned_ref, factors_ref,
    ens_ref, vertical_ref, weights_ref, tall, sems,
):
    moves = copy_in((vertical_hbm, weights_hbm, ens_hbm), (vertical_ref, weights_ref, ens_ref), sems)
    for move in moves:
        move.wait()
    _, levels, rows, columns = ens_ref.shape
    for t in range(columns // LANES):
        at = slice(t * LANES, (t + 1) * LANES)
        tall[t] = ens_ref[0, :, :, at].astype(F32).reshape(levels * rows, LANES)
        for r in range(0, rows, 2):
            both = [tall[t, pl.ds(r + i, levels, stride=rows), :] for i in range(2)]
            turned_ref[t, r * levels : (r + 2) * levels, :] = jnp.concatenate(both, axis=0).astype(BF16)
    vertical = vertical_ref[...] * weights_ref[lax.axis_index("tx")]
    gap = iota((levels, levels), 1) - iota((levels, levels), 0)
    for i in range(2 * BAND + 1):
        factor = jnp.sum(jnp.where(gap == i - BAND, vertical, 0.0), axis=1, keepdims=True)
        factors_ref[i] = jnp.broadcast_to(factor, (levels, LANES))


def lines_of(staggered, place, tiles):
    size = staggered[0][0].shape[0]
    groups = LANES // GROUP
    return jnp.concatenate([pick(part, place % groups) for part in staggered[place // groups]], axis=1)


def spread(line_value, line_key, hits, count, first):
    key = line_key - first
    on = iota((count, line_key.shape[1]), 0).astype(F32) == key
    stacked = jnp.concatenate([jnp.where(on, piece, 0.0) for piece in pieces(line_value)], axis=0)
    found = lax.dot_general(
        stacked.astype(BF16), hits, (((1,), (1,)), ((), ())), preferred_element_type=F32
    )
    return found[0:count] + found[count : 2 * count] + found[2 * count :]


def hits_of(line_column):
    shape = (LANES, line_column.shape[1])
    return jnp.where(iota(shape, 0).astype(F32) == line_column, 1.0, 0.0).astype(BF16)


def places(cell, rows, levels):
    cell = cell.astype(jnp.int32)
    flat = lax.shift_right_logical(cell, log2(LANES))
    key = (flat & (rows - 1)) * levels + lax.shift_right_logical(flat, log2(rows))
    return key.astype(F32), (cell & (LANES - 1)).astype(F32)


def gather_kernel(order, rows, lines, levels, *refs):
    got, (turned_ref, d_ref, slots_ref, hits_ref, a_ref, b_ref, packs) = refs[: len(order)], refs[len(order) :]
    tiles = packs.shape[0]
    size = min(tiles, LANES // GROUP)
    me, even = lax.axis_index("tx"), lax.rem(lax.axis_index("ty"), 2) == 0
    chip, core = me // 2, lax.rem(me, 2)
    for far, ref in zip(order, got):
        for side in range(2):
            packs[2 * (chip ^ far) + (core ^ side ^ (far > 0))] = ref[side]
    slots = []
    for i in range(lines):
        x = packs[:, rows + i, :]
        slots.append([stagger(x[q : q + size]) for q in range(0, tiles, size)])
    deep = STEPS - 1
    step = deep + lines
    for t in range(tiles):
        value, cell = lines_of(slots, t, tiles), lines_of(slots, tiles + t, tiles)
        key, column = places(cell, rows, levels)
        hits = hits_of(column)
        hits_ref[t] = hits
        found = jnp.dot(turned_ref[t], hits, preferred_element_type=F32)
        on = iota(found.shape, 0).astype(F32) == key
        product = value * jnp.sum(jnp.where(on, found, 0.0), axis=0, keepdims=True)
        d = packs[t, 0:rows, :]
        d_ref[:, t * LANES : (t + 1) * LANES] = d
        low = pltpu.roll(d, deep, 0)
        sent = [line[:, q : q + LANES] for line in (product, cell) for q in range(0, line.shape[1], LANES)]
        if len(sent) > lines:
            sent = [sent[0] + pltpu.roll(sent[1], tiles * GROUP, 1)]
        for out, part in ((a_ref, jnp.where(even, low, d)), (b_ref, jnp.where(even, d, low))):
            out[t * step : t * step + deep, :] = part[0:deep]
            for i, line in enumerate(sent):
                out[t * step + deep + i : t * step + deep + i + 1, :] = line
        for i, line in enumerate((product, key)):
            slots_ref[t, i : i + 1, :] = line


def step_row(rows3, d, c, columns):
    above, mid, below = rows3
    beside = (
        above[:, 0:columns]
        + below[:, 0:columns]
        + pltpu.roll(mid, 1, 1)[:, 0:columns]
        + pltpu.roll(mid, mid.shape[1] - 1, 1)[:, 0:columns]
    )
    return jnp.broadcast_to(c, beside.shape) * mid[:, 0:columns] + jnp.broadcast_to(d, beside.shape) * beside


def own_kernel(slots_ref, hits_ref, turned_ref, d_ref, member_ref, keep_ref, *fields):
    tiles, own, _ = turned_ref.shape
    columns = tiles * LANES
    rows = d_ref.shape[0]
    levels = own // rows
    for field in fields:
        field[:, columns:] = jnp.zeros((own, LANES), F32)
    keep_ref[...] = 1.0 - 4.0 * d_ref[...]
    for t in range(tiles):
        at = slice(t * LANES, (t + 1) * LANES)
        member_ref[:, at] = turned_ref[t].astype(F32)
        fields[0][:, at] = spread(slots_ref[t, 0:1, :], slots_ref[t, 1:2, :], hits_ref[t], own, 0.0)
    for step in range(1, len(fields)):
        for r in range(step, rows - step):
            near = [fields[step - 1][i * levels : (i + 1) * levels, :] for i in (r - 1, r, r + 1)]
            x = step_row(near, d_ref[r : r + 1, :], keep_ref[r : r + 1, :], columns)
            fields[step][r * levels : (r + 1) * levels, 0:columns] = x


def main_kernel(rows, levels, d_ref, slots_ref, hits_ref, b_ref, a_ref, factors_ref, member, keep_ref, *refs):
    fields, (mine_ref, other_ref, d_all, keep, first, second, made, back) = refs[:STEPS], refs[STEPS:]
    tiles = hits_ref.shape[0]
    block = min(tiles, LANES // GROUP)
    columns = tiles * LANES
    band, last, me = lax.axis_index("ty"), lax.axis_size("ty") - 1, lax.axis_index("tx")
    chip, core = me // 2, lax.rem(me, 2)
    even = lax.rem(band, 2) == 0
    half, own, deep = STEPS * levels, rows * levels, STEPS - 1
    step = a_ref.shape[0] // tiles

    for t in range(tiles):
        at = slice(t * LANES, (t + 1) * LANES)
        got_a, got_b = (ref[t * step : (t + 1) * step, :] for ref in (a_ref, b_ref))
        above = jnp.where(band == 0, 0.0, jnp.where(even, got_b, got_a))
        below = jnp.where(band == last, 0.0, jnp.where(even, got_a, got_b))
        for got, begin, base, d_begin in ((above, 0, own - half, 1), (below, half + own, 0, STEPS + rows)):
            d_all[d_begin : d_begin + deep, at] = got[0:deep]
            keep[d_begin : d_begin + deep, at] = 1.0 - 4.0 * got[0:deep]
            parts = [got[deep + i : deep + i + 1] for i in range(step - deep)]
            if len(parts) == 1:
                parts.append(pltpu.roll(parts[0], LANES - tiles * GROUP, 1))
                parts[0] = jnp.where(iota((1, LANES), 1) < tiles * GROUP, parts[0], 0.0)
            product, cell = (jnp.concatenate(parts[i : i + len(parts) // 2], axis=1) for i in (0, len(parts) // 2))
            key, column = places(cell, rows, levels)
            first[begin : begin + half, at] = spread(product, key, hits_of(column), half, float(base))
    for field in (first, second):
        field[:, columns:] = jnp.zeros((field.shape[0], LANES), F32)

    def inner(step, r):
        return step <= r - STEPS < rows - step

    def row_of(step, r):
        ref, i = (fields[step], r - STEPS) if inner(step, r) else ((first, second)[step % 2], r)
        return ref[i * levels : (i + 1) * levels, :]

    factors = [(i - BAND, factors_ref[i]) for i in range(2 * BAND + 1)]
    for step in range(1, STEPS + 1):
        for r in range(step, 2 * STEPS + rows - step):
            if step < STEPS and inner(step, r):
                continue
            if 0 <= r - STEPS < rows:
                d, c = (ref[r - STEPS : r - STEPS + 1, :] for ref in (d_ref, keep_ref))
            else:
                d, c = (ref[r : r + 1, :] for ref in (d_all, keep))
            x = step_row([row_of(step - 1, i) for i in (r - 1, r, r + 1)], d, c, columns)
            if step < STEPS:
                (first, second)[step % 2][r * levels : (r + 1) * levels, 0:columns] = x
                continue
            row = slice((r - STEPS) * levels, (r - STEPS + 1) * levels)
            for t in range(tiles):
                at = slice(t * LANES, (t + 1) * LANES)
                mixed = sum(f * (pltpu.roll(x[:, at], -o % levels, 0) if o else x[:, at]) for o, f in factors)
                made[t, row, :] = mixed * member[row, at]

    for t in range(tiles):
        stacked = jnp.concatenate(pieces(made[t]), axis=0).astype(BF16)
        found = jnp.dot(stacked, hits_ref[t], preferred_element_type=F32)
        found = found[0:own] + found[own : 2 * own] + found[2 * own :]
        on = iota(found.shape, 0).astype(F32) == slots_ref[t, 1:2, :]
        line = jnp.sum(jnp.where(on, found, 0.0), axis=0, keepdims=True)
        for q in range(tiles // block):
            back[q, t : t + 1, :] = line[:, q * LANES : (q + 1) * LANES]
    for z in range(mine_ref.shape[0]):
        for side, out in enumerate((mine_ref, other_ref)):
            out[z, 0:own, :] = made[2 * z + (core ^ side ^ (chip != z).astype(jnp.int32))]
            out[z, own:, :] = back[2 * z // block]


def scale_of(code):
    return jnp.exp2(code.astype(F32) * (1.0 / CODES))


def pair_kernel(split, mine_ref, got_ref, near_ref, *outs):
    chip = lax.axis_index("tx") // 2
    near_ref[...] = mine_ref[chip] + got_ref[chip]
    for far, out in enumerate(outs, 1):
        x = mine_ref[chip ^ far] + got_ref[chip ^ far]
        whole, codes = [], []
        for part in (x[0:split], x[split:]):
            largest = jnp.maximum(jnp.max(jnp.abs(part), axis=0, keepdims=True), LEAST)
            code = jnp.minimum(jnp.ceil(jnp.log2(largest) * CODES).astype(jnp.int32), CODES * 128 - 1)
            sized = jnp.clip(part * (1.0 / scale_of(code)), -1.0, 1.0)
            whole.append(jnp.floor(sized * FULL + 0.5).astype(jnp.int32))
            codes.append(code)
        rest = out.shape[0] - x.shape[0]
        row = iota((rest, LANES), 0)
        tail = jnp.where(row == 0, codes[0], jnp.where(row == 1, codes[1], 0))
        out[...] = jnp.concatenate([*whole, tail], axis=0).astype(jnp.int16)


def final_kernel(split, *refs):
    got, (live_ref, inc_ref, proj_ref, total) = refs[:-4], refs[-4:]
    levels, rows, _ = inc_ref.shape
    _, tiles, slots = proj_ref.shape
    size = got[0].shape[0]
    top, low = got[0][0:split, :], got[0][split:, :]
    for ref in got[1:]:
        x = ref[...].astype(jnp.int32)
        sent = x[0:size].astype(F32) * (1.0 / FULL)
        top = top + sent[0:split] * scale_of(x[size : size + 1])
        low = low + sent[split:] * scale_of(x[size + 1 : size + 2])
    total[...] = top
    for level in range(levels):
        inc_ref[level] = total[pl.ds(level, rows, stride=levels), :]
    place = lax.rem(lax.axis_index("tx"), LANES // GROUP)
    lines = pltpu.roll(low, lax.rem(LANES - GROUP * place, LANES), 1)
    proj_ref[0] = jnp.where(live_ref[:, 0:slots] > 0.0, lines[:, 0:slots], 0.0)


def call(kernel, out_shape, ins, scratch, flops=0, moved=0):
    return pl.pallas_call(
        kernel,
        out_shape=out_shape,
        in_specs=ins,
        out_specs=jax.tree.map(lambda _: VMEM, out_shape),
        scratch_shapes=scratch,
        compiler_params=pltpu.CompilerParams(vmem_limit_bytes=48 << 20),
        cost_estimate=pl.CostEstimate(flops=flops, bytes_accessed=moved, transcendentals=0),
    )


def shards(ensemble, diffusivity, vertical, weights, obs_value, obs_cell, obs_count):
    _, levels, rows, columns = ensemble.shape
    tiles, slots = obs_value.shape[1:]
    chips = tiles // 2
    bands = lax.axis_size("ty")
    assert diffusivity.shape == (rows, LANES) and slots == GROUP and rows == 2 * STEPS
    block = min(tiles, LANES // GROUP)
    shape = jax.ShapeDtypeStruct
    lines = -(-2 * tiles * GROUP // LANES)
    half, own = STEPS * levels, rows * levels
    height = round_up(rows + lines, 8)
    lanes = tiles // block * LANES

    def in_hbm(*arrays):
        return [pltpu.with_memory_space_constraint(x, pltpu.HBM) for x in arrays]

    def swap(x, far):
        return lax.ppermute(x, "tx", [(i, i ^ far) for i in range(tiles)])

    def swap_bands(x, low):
        mate = [i ^ 1 if low else i + 1 if i % 2 else i - 1 for i in range(bands)]
        pairs = [
            (i * tiles + k, mate[i] * tiles + k if 0 <= mate[i] < bands else i * tiles + (k ^ 1))
            for i in range(bands)
            for k in range(tiles)
        ]
        return lax.ppermute(x, ("ty", "tx"), pairs)

    packet, live = call(
        packet_kernel,
        (shape((height, LANES), F32), shape((tiles, LANES), F32)),
        [HBM] * 4,
        [
            pltpu.VMEM(obs_value.shape, F32),
            pltpu.VMEM(obs_cell.shape, jnp.int32),
            pltpu.VMEM(obs_count.shape, jnp.int32),
            pltpu.VMEM(diffusivity.shape, F32),
            pltpu.VMEM((2, tiles, LANES), F32),
            pltpu.SemaphoreType.DMA((4,)),
        ],
    )(*in_hbm(obs_value, obs_cell, obs_count, diffusivity))
    turned, factors = call(
        member_kernel,
        (shape((tiles, own, LANES), BF16), shape((2 * BAND + 1, levels, LANES), F32)),
        [HBM] * 3,
        [
            pltpu.VMEM(ensemble.shape, BF16),
            pltpu.VMEM(vertical.shape, F32),
            pltpu.SMEM(weights.shape, F32),
            pltpu.VMEM((tiles, own, LANES), F32),
            pltpu.SemaphoreType.DMA((3,)),
        ],
        1000000,
        1000000,
    )(*in_hbm(ensemble, vertical, weights))

    pair = jnp.stack([packet, swap(packet, 1)])
    order = [0] + sorted(range(1, chips), key=lambda far: (far % 2 == 0, far))
    row = [swap(pair, 2 * far + 1) if far else pair for far in order]
    halo = shape((tiles * (STEPS - 1 + lines), LANES), F32)
    d_row, slots_row, hits, to_a, to_b = call(
        functools.partial(gather_kernel, order, rows, lines, levels),
        (
            shape((rows, columns), F32),
            shape((tiles, 8, lanes), F32),
            shape((tiles, LANES, lanes), BF16),
            halo,
            halo,
        ),
        [VMEM] * (chips + 1),
        [pltpu.VMEM((tiles, height, LANES), F32)],
    )(*row, turned)
    from_a, from_b = swap_bands(to_a, True), swap_bands(to_b, False)
    wide = shape((own, columns + LANES), F32)
    member, keep, *fields = call(
        own_kernel,
        (shape((own, columns), F32), shape((rows, columns), F32), *[wide] * STEPS),
        [VMEM] * 4,
        [],
        1000000,
        1000000,
    )(slots_row, hits, turned, d_row)

    chunk = own + tiles
    mine, other = call(
        functools.partial(main_kernel, rows, levels),
        (shape((chips, chunk, LANES), F32), shape((chips, chunk, LANES), F32)),
        [VMEM] * (8 + STEPS),
        [
            pltpu.VMEM((2 * STEPS + rows, columns), F32),
            pltpu.VMEM((2 * STEPS + rows, columns), F32),
            pltpu.VMEM((2 * half + own, columns + LANES), F32),
            pltpu.VMEM((2 * half + own, columns + LANES), F32),
            pltpu.VMEM((tiles, own, LANES), F32),
            pltpu.VMEM((tiles // block, tiles, LANES), F32),
        ],
    )(d_row, slots_row, hits, from_b, from_a, factors, member, keep, *fields)

    coded = shape((round_up(chunk + 2, 16), LANES), jnp.int16)
    sums = call(
        functools.partial(pair_kernel, own), (shape((chunk, LANES), F32), *[coded] * (chips - 1)), [VMEM] * 2, []
    )(mine, swap(other, 1))
    sums = [sums[0]] + [swap(sums[far], 2 * far + 1) for far in range(1, chips)]
    return call(
        functools.partial(final_kernel, own),
        (shape((levels, rows, LANES), F32), shape((1, tiles, slots), F32)),
        [VMEM] * (chips + 1),
        [pltpu.VMEM((own, LANES), F32)],
    )(sums[0], *sums[:0:-1], live)


def solution(mesh):
    placed = (
        P("tx", None, "ty", None),
        P("ty", "tx"),
        P(),
        P(),
        P(("ty", "tx"), None, None),
        P(("ty", "tx"), None, None),
        P(("ty", "tx"), None),
    )
    return jax.shard_map(
        shards,
        mesh=mesh,
        in_specs=placed,
        out_specs=(P(None, "ty", "tx"), P(("ty", "tx"), None, None)),
        check_vma=False,
    )
```

```python
import functools

import jax
import jax.numpy as jnp
from jax import lax
from jax.experimental import pallas as pl
from jax.experimental.pallas import tpu as pltpu
from jax.sharding import PartitionSpec as P

STEPS = 4
BAND = 2
LANES = 128
GROUP = 8
CODES, FULL, LEAST = 128, 32700.0, 1.2e-38
F32, BF16 = jnp.float32, jnp.bfloat16
VMEM = pl.BlockSpec(memory_space=pltpu.VMEM)
HBM = pl.BlockSpec(memory_space=pltpu.HBM)


def round_up(n, m):
    return -(-n // m) * m


def log2(n):
    assert n & (n - 1) == 0
    return n.bit_length() - 1


def iota(shape, axis):
    return lax.broadcasted_iota(jnp.int32, shape, axis)


def pieces(x):
    high = x.astype(BF16).astype(F32)
    rest = x - high
    middle = rest.astype(BF16).astype(F32)
    return high, middle, rest - middle


def stagger(x):
    return pltpu.roll(x, 0, 1, stride=GROUP, stride_axis=0)


def pick(x, place):
    if isinstance(place, int):
        shift = (-GROUP * place) % LANES
    else:
        shift = lax.rem(LANES - GROUP * place, LANES)
    rolled = pltpu.roll(x, shift, 1)
    own = iota(x.shape, 1) // GROUP == iota(x.shape, 0)
    return jnp.sum(jnp.where(own, rolled, 0.0), axis=0, keepdims=True)


def live_mask(count_ref, slots):
    tiles = count_ref.shape[1]
    count = jnp.broadcast_to(count_ref[...].astype(F32), (tiles, tiles))
    diagonal = iota((tiles, tiles), 0) == iota((tiles, tiles), 1)
    column = jnp.sum(jnp.where(diagonal, count, 0.0), axis=1, keepdims=True)
    return iota((tiles, slots), 1).astype(F32) < column


def copy_in(sources, targets, sems):
    moves = [pltpu.make_async_copy(x, y, sems.at[i]) for i, (x, y) in enumerate(zip(sources, targets))]
    for move in moves:
        move.start()
    return moves


def packet_kernel(
    value_hbm, cell_hbm, count_hbm, diff_hbm, packet, live_ref,
    value_ref, cell_ref, count_ref, diff_ref, wide, sems,
):
    moves = copy_in(
        (value_hbm, cell_hbm, count_hbm, diff_hbm), (value_ref, cell_ref, count_ref, diff_ref), sems
    )
    wide[...] = jnp.zeros_like(wide)
    for move in moves:
        move.wait()
    _, tiles, slots = value_ref.shape
    rows = diff_ref.shape[0]
    block = min(tiles, LANES // GROUP)
    live = live_mask(count_ref, slots)
    wide[0, :, 0:slots] = jnp.where(live, value_ref[0], 0.0)
    wide[1, :, 0:slots] = cell_ref[0].astype(F32)
    live_ref[...] = jnp.zeros_like(live_ref)
    live_ref[:, 0:slots] = jnp.where(live, 1.0, 0.0)
    packet[0:rows, :] = diff_ref[...]
    lines = [pick(stagger(wide[q, b : b + block, :]), 0) for q in range(2) for b in range(0, tiles, block)]
    if block * GROUP < LANES:
        lines = [lines[0] + pltpu.roll(lines[1], block * GROUP, 1)]
    packet[rows:, :] = jnp.zeros((packet.shape[0] - rows, LANES), F32)
    for i, line in enumerate(lines):
        packet[rows + i : rows + i + 1, :] = line


def member_kernel(
    ens_hbm, vertical_hbm, weights_hbm, turned_ref, factors_ref,
    ens_ref, vertical_ref, weights_ref, tall, sems,
):
    moves = copy_in((vertical_hbm, weights_hbm, ens_hbm), (vertical_ref, weights_ref, ens_ref), sems)
    for move in moves:
        move.wait()
    _, levels, rows, columns = ens_ref.shape
    for t in range(columns // LANES):
        at = slice(t * LANES, (t + 1) * LANES)
        tall[t] = ens_ref[0, :, :, at].astype(F32).reshape(levels * rows, LANES)
        for r in range(0, rows, 2):
            both = [tall[t, pl.ds(r + i, levels, stride=rows), :] for i in range(2)]
            turned_ref[t, r * levels : (r + 2) * levels, :] = jnp.concatenate(both, axis=0).astype(BF16)
    vertical = vertical_ref[...] * weights_ref[lax.axis_index("tx")]
    gap = iota((levels, levels), 1) - iota((levels, levels), 0)
    for i in range(2 * BAND + 1):
        factor = jnp.sum(jnp.where(gap == i - BAND, vertical, 0.0), axis=1, keepdims=True)
        factors_ref[i] = jnp.broadcast_to(factor, (levels, LANES))


def lines_of(staggered, place, tiles):
    size = staggered[0][0].shape[0]
    groups = LANES // GROUP
    return jnp.concatenate([pick(part, place % groups) for part in staggered[place // groups]], axis=1)


def spread(line_value, line_key, hits, count, first):
    key = line_key - first
    on = iota((count, line_key.shape[1]), 0).astype(F32) == key
    stacked = jnp.concatenate([jnp.where(on, piece, 0.0) for piece in pieces(line_value)], axis=0)
    found = lax.dot_general(
        stacked.astype(BF16), hits, (((1,), (1,)), ((), ())), preferred_element_type=F32
    )
    return found[0:count] + found[count : 2 * count] + found[2 * count :]


def hits_of(line_column):
    shape = (LANES, line_column.shape[1])
    return jnp.where(iota(shape, 0).astype(F32) == line_column, 1.0, 0.0).astype(BF16)


def places(cell, rows, levels):
    cell = cell.astype(jnp.int32)
    flat = lax.shift_right_logical(cell, log2(LANES))
    key = (flat & (rows - 1)) * levels + lax.shift_right_logical(flat, log2(rows))
    return key.astype(F32), (cell & (LANES - 1)).astype(F32)


def gather_kernel(order, rows, lines, levels, *refs):
    got, (turned_ref, d_ref, slots_ref, hits_ref, a_ref, b_ref, packs) = refs[: len(order)], refs[len(order) :]
    tiles = packs.shape[0]
    size = min(tiles, LANES // GROUP)
    me, even = lax.axis_index("tx"), lax.rem(lax.axis_index("ty"), 2) == 0
    chip, core, used = me // 2, lax.rem(me, 2), rows + lines
    for far, ref in zip(order, got):
        for side in range(2):
            packs[2 * (chip ^ far) + (core ^ side ^ (far > 0)), 0:used, :] = ref[side * used : (side + 1) * used, :]
    slots = []
    for i in range(lines):
        x = packs[:, rows + i, :]
        slots.append([stagger(x[q : q + size]) for q in range(0, tiles, size)])
    deep = STEPS - 1
    step = deep + lines
    for t in range(tiles):
        value, cell = lines_of(slots, t, tiles), lines_of(slots, tiles + t, tiles)
        key, column = places(cell, rows, levels)
        hits = hits_of(column)
        hits_ref[t] = hits
        found = jnp.dot(turned_ref[t], hits, preferred_element_type=F32)
        on = iota(found.shape, 0).astype(F32) == key
        product = value * jnp.sum(jnp.where(on, found, 0.0), axis=0, keepdims=True)
        d = packs[t, 0:rows, :]
        d_ref[:, t * LANES : (t + 1) * LANES] = d
        low = pltpu.roll(d, deep, 0)
        sent = [line[:, q : q + LANES] for line in (product, cell) for q in range(0, line.shape[1], LANES)]
        if len(sent) > lines:
            sent = [sent[0] + pltpu.roll(sent[1], tiles * GROUP, 1)]
        for out, part in ((a_ref, jnp.where(even, low, d)), (b_ref, jnp.where(even, d, low))):
            out[t * step : t * step + deep, :] = part[0:deep]
            for i, line in enumerate(sent):
                out[t * step + deep + i : t * step + deep + i + 1, :] = line
        for i, line in enumerate((product, key)):
            slots_ref[t, i : i + 1, :] = line


def step_row(rows3, d, c, columns):
    above, mid, below = rows3
    beside = (
        above[:, 0:columns]
        + below[:, 0:columns]
        + pltpu.roll(mid, 1, 1)[:, 0:columns]
        + pltpu.roll(mid, mid.shape[1] - 1, 1)[:, 0:columns]
    )
    return jnp.broadcast_to(c, beside.shape) * mid[:, 0:columns] + jnp.broadcast_to(d, beside.shape) * beside


def own_kernel(slots_ref, hits_ref, turned_ref, d_ref, member_ref, keep_ref, *fields):
    tiles, own, _ = turned_ref.shape
    columns = tiles * LANES
    rows = d_ref.shape[0]
    levels = own // rows
    for field in fields:
        field[:, columns:] = jnp.zeros((own, LANES), F32)
    keep_ref[...] = 1.0 - 4.0 * d_ref[...]
    for t in range(tiles):
        at = slice(t * LANES, (t + 1) * LANES)
        member_ref[:, at] = turned_ref[t].astype(F32)
        fields[0][:, at] = spread(slots_ref[t, 0:1, :], slots_ref[t, 1:2, :], hits_ref[t], own, 0.0)
    for step in range(1, len(fields)):
        for r in range(step, rows - step):
            near = [fields[step - 1][i * levels : (i + 1) * levels, :] for i in (r - 1, r, r + 1)]
            x = step_row(near, d_ref[r : r + 1, :], keep_ref[r : r + 1, :], columns)
            fields[step][r * levels : (r + 1) * levels, 0:columns] = x


def main_kernel(rows, levels, d_ref, slots_ref, hits_ref, b_ref, a_ref, factors_ref, member, keep_ref, *refs):
    fields, (mine_ref, other_ref, d_all, keep, first, second, made, back) = refs[:STEPS], refs[STEPS:]
    tiles = hits_ref.shape[0]
    block = min(tiles, LANES // GROUP)
    columns = tiles * LANES
    band, last, me = lax.axis_index("ty"), lax.axis_size("ty") - 1, lax.axis_index("tx")
    chip, core = me // 2, lax.rem(me, 2)
    even = lax.rem(band, 2) == 0
    half, own, deep = STEPS * levels, rows * levels, STEPS - 1
    step = a_ref.shape[0] // tiles

    for t in range(tiles):
        at = slice(t * LANES, (t + 1) * LANES)
        got_a, got_b = (ref[t * step : (t + 1) * step, :] for ref in (a_ref, b_ref))
        above = jnp.where(band == 0, 0.0, jnp.where(even, got_b, got_a))
        below = jnp.where(band == last, 0.0, jnp.where(even, got_a, got_b))
        for got, begin, base, d_begin in ((above, 0, own - half, 1), (below, half + own, 0, STEPS + rows)):
            d_all[d_begin : d_begin + deep, at] = got[0:deep]
            keep[d_begin : d_begin + deep, at] = 1.0 - 4.0 * got[0:deep]
            parts = [got[deep + i : deep + i + 1] for i in range(step - deep)]
            if len(parts) == 1:
                parts.append(pltpu.roll(parts[0], LANES - tiles * GROUP, 1))
                parts[0] = jnp.where(iota((1, LANES), 1) < tiles * GROUP, parts[0], 0.0)
            product, cell = (jnp.concatenate(parts[i : i + len(parts) // 2], axis=1) for i in (0, len(parts) // 2))
            key, column = places(cell, rows, levels)
            first[begin : begin + half, at] = spread(product, key, hits_of(column), half, float(base))
    for field in (first, second):
        field[:, columns:] = jnp.zeros((field.shape[0], LANES), F32)

    def inner(step, r):
        return step <= r - STEPS < rows - step

    def row_of(step, r):
        ref, i = (fields[step], r - STEPS) if inner(step, r) else ((first, second)[step % 2], r)
        return ref[i * levels : (i + 1) * levels, :]

    factors = [(i - BAND, factors_ref[i]) for i in range(2 * BAND + 1)]
    for step in range(1, STEPS):
        for r in range(step, 2 * STEPS + rows - step):
            if inner(step, r):
                continue
            if 0 <= r - STEPS < rows:
                d, c = (ref[r - STEPS : r - STEPS + 1, :] for ref in (d_ref, keep_ref))
            else:
                d, c = (ref[r : r + 1, :] for ref in (d_all, keep))
            x = step_row([row_of(step - 1, i) for i in (r - 1, r, r + 1)], d, c, columns)
            (first, second)[step % 2][r * levels : (r + 1) * levels, 0:columns] = x

    rowed = [row_of(STEPS - 1, r) for r in range(STEPS - 1, STEPS + rows + 1)]
    lane = iota((levels, LANES), 1)
    zero = jnp.zeros((levels, LANES), F32)

    def piece(r, t):
        return rowed[r + 1][:, t * LANES : (t + 1) * LANES] if 0 <= t < tiles else zero

    before = [zero] * rows
    here = [piece(r, 0) for r in range(rows)]
    for t in range(tiles):
        at = slice(t * LANES, (t + 1) * LANES)
        after = [piece(r, t + 1) for r in range(rows)]
        parts = []
        for r in range(rows):
            mid = here[r]
            left = pltpu.roll(jnp.where(lane == LANES - 1, before[r], mid), 1, 1)
            right = pltpu.roll(jnp.where(lane == 0, after[r], mid), LANES - 1, 1)
            beside = piece(r - 1, t) + piece(r + 1, t) + left + right
            d, c = (jnp.broadcast_to(ref[r : r + 1, at], mid.shape) for ref in (d_ref, keep_ref))
            x = c * mid + d * beside
            mixed = sum(f * (pltpu.roll(x, -o % levels, 0) if o else x) for o, f in factors)
            row = slice(r * levels, (r + 1) * levels)
            parts.append(mixed * member[row, at])
            made[t, row, :] = parts[-1]
        before, here = here, after
        stacked = jnp.concatenate(pieces(jnp.concatenate(parts, axis=0)), axis=0).astype(BF16)
        found = jnp.dot(stacked, hits_ref[t], preferred_element_type=F32)
        found = found[0:own] + found[own : 2 * own] + found[2 * own :]
        on = iota(found.shape, 0).astype(F32) == slots_ref[t, 1:2, :]
        line = jnp.sum(jnp.where(on, found, 0.0), axis=0, keepdims=True)
        for q in range(tiles // block):
            back[q, t : t + 1, :] = line[:, q * LANES : (q + 1) * LANES]
    for z in range(mine_ref.shape[0]):
        for side, out in enumerate((mine_ref, other_ref)):
            out[z, 0:own, :] = made[2 * z + (core ^ side ^ (chip != z).astype(jnp.int32))]
            out[z, own:, :] = back[2 * z // block]


def scale_of(code):
    return jnp.exp2(code.astype(F32) * (1.0 / CODES))


def pair_kernel(split, mine_ref, got_ref, near_ref, *outs):
    chip = lax.axis_index("tx") // 2
    near_ref[...] = mine_ref[chip] + got_ref[chip]
    for far, out in enumerate(outs, 1):
        x = mine_ref[chip ^ far] + got_ref[chip ^ far]
        whole, codes = [], []
        for part in (x[0:split], x[split:]):
            largest = jnp.maximum(jnp.max(jnp.abs(part), axis=0, keepdims=True), LEAST)
            code = jnp.minimum(jnp.ceil(jnp.log2(largest) * CODES).astype(jnp.int32), CODES * 128 - 1)
            sized = jnp.clip(part * (1.0 / scale_of(code)), -1.0, 1.0)
            whole.append(jnp.floor(sized * FULL + 0.5).astype(jnp.int32))
            codes.append(code)
        rest = out.shape[0] - x.shape[0]
        row = iota((rest, LANES), 0)
        tail = jnp.where(row == 0, codes[0], jnp.where(row == 1, codes[1], 0))
        out[...] = jnp.concatenate([*whole, tail], axis=0).astype(jnp.int16)


def final_kernel(split, *refs):
    got, (live_ref, inc_ref, proj_ref, total) = refs[:-4], refs[-4:]
    levels, rows, _ = inc_ref.shape
    _, tiles, slots = proj_ref.shape
    size = got[0].shape[0]
    top, low = got[0][0:split, :], got[0][split:, :]
    for ref in got[1:]:
        x = ref[...].astype(jnp.int32)
        sent = x[0:size].astype(F32) * (1.0 / FULL)
        top = top + sent[0:split] * scale_of(x[size : size + 1])
        low = low + sent[split:] * scale_of(x[size + 1 : size + 2])
    total[...] = top
    for level in range(levels):
        inc_ref[level] = total[pl.ds(level, rows, stride=levels), :]
    place = lax.rem(lax.axis_index("tx"), LANES // GROUP)
    lines = pltpu.roll(low, lax.rem(LANES - GROUP * place, LANES), 1)
    proj_ref[0] = jnp.where(live_ref[:, 0:slots] > 0.0, lines[:, 0:slots], 0.0)


def call(kernel, out_shape, ins, scratch, flops=0, moved=0):
    return pl.pallas_call(
        kernel,
        out_shape=out_shape,
        in_specs=ins,
        out_specs=jax.tree.map(lambda _: VMEM, out_shape),
        scratch_shapes=scratch,
        compiler_params=pltpu.CompilerParams(vmem_limit_bytes=48 << 20),
        cost_estimate=pl.CostEstimate(flops=flops, bytes_accessed=moved, transcendentals=0),
    )


def shards(ensemble, diffusivity, vertical, weights, obs_value, obs_cell, obs_count):
    _, levels, rows, columns = ensemble.shape
    tiles, slots = obs_value.shape[1:]
    chips = tiles // 2
    bands = lax.axis_size("ty")
    assert diffusivity.shape == (rows, LANES) and slots == GROUP and rows == 2 * STEPS
    block = min(tiles, LANES // GROUP)
    shape = jax.ShapeDtypeStruct
    lines = -(-2 * tiles * GROUP // LANES)
    half, own = STEPS * levels, rows * levels
    height = round_up(rows + lines, 8)
    lanes = tiles // block * LANES

    def in_hbm(*arrays):
        return [pltpu.with_memory_space_constraint(x, pltpu.HBM) for x in arrays]

    def swap(x, far):
        return lax.ppermute(x, "tx", [(i, i ^ far) for i in range(tiles)])

    def swap_bands(x, low):
        mate = [i ^ 1 if low else i + 1 if i % 2 else i - 1 for i in range(bands)]
        pairs = [
            (i * tiles + k, mate[i] * tiles + k if 0 <= mate[i] < bands else i * tiles + (k ^ 1))
            for i in range(bands)
            for k in range(tiles)
        ]
        return lax.ppermute(x, ("ty", "tx"), pairs)

    packet, live = call(
        packet_kernel,
        (shape((height, LANES), F32), shape((tiles, LANES), F32)),
        [HBM] * 4,
        [
            pltpu.VMEM(obs_value.shape, F32),
            pltpu.VMEM(obs_cell.shape, jnp.int32),
            pltpu.VMEM(obs_count.shape, jnp.int32),
            pltpu.VMEM(diffusivity.shape, F32),
            pltpu.VMEM((2, tiles, LANES), F32),
            pltpu.SemaphoreType.DMA((4,)),
        ],
    )(*in_hbm(obs_value, obs_cell, obs_count, diffusivity))
    turned, factors = call(
        member_kernel,
        (shape((tiles, own, LANES), BF16), shape((2 * BAND + 1, levels, LANES), F32)),
        [HBM] * 3,
        [
            pltpu.VMEM(ensemble.shape, BF16),
            pltpu.VMEM(vertical.shape, F32),
            pltpu.SMEM(weights.shape, F32),
            pltpu.VMEM((tiles, own, LANES), F32),
            pltpu.SemaphoreType.DMA((3,)),
        ],
        1000000,
        1000000,
    )(*in_hbm(ensemble, vertical, weights))

    used = rows + lines
    spare = jnp.zeros((round_up(2 * used, 8) - 2 * used, LANES), F32)
    pair = jnp.concatenate([packet[:used], swap(packet, 1)[:used], spare])
    order = [0] + sorted(range(1, chips), key=lambda far: (far % 2 == 0, far))
    row = [swap(pair, 2 * far + 1) if far else pair for far in order]
    halo = shape((tiles * (STEPS - 1 + lines), LANES), F32)
    d_row, slots_row, hits, to_a, to_b = call(
        functools.partial(gather_kernel, order, rows, lines, levels),
        (
            shape((rows, columns), F32),
            shape((tiles, 8, lanes), F32),
            shape((tiles, LANES, lanes), BF16),
            halo,
            halo,
        ),
        [VMEM] * (chips + 1),
        [pltpu.VMEM((tiles, height, LANES), F32)],
    )(*row, turned)
    from_a, from_b = swap_bands(to_a, True), swap_bands(to_b, False)
    wide = shape((own, columns + LANES), F32)
    member, keep, *fields = call(
        own_kernel,
        (shape((own, columns), F32), shape((rows, columns), F32), *[wide] * STEPS),
        [VMEM] * 4,
        [],
        1000000,
        1000000,
    )(slots_row, hits, turned, d_row)

    chunk = own + tiles
    mine, other = call(
        functools.partial(main_kernel, rows, levels),
        (shape((chips, chunk, LANES), F32), shape((chips, chunk, LANES), F32)),
        [VMEM] * (8 + STEPS),
        [
            pltpu.VMEM((2 * STEPS + rows, columns), F32),
            pltpu.VMEM((2 * STEPS + rows, columns), F32),
            pltpu.VMEM((2 * half + own, columns + LANES), F32),
            pltpu.VMEM((2 * half + own, columns + LANES), F32),
            pltpu.VMEM((tiles, own, LANES), F32),
            pltpu.VMEM((tiles // block, tiles, LANES), F32),
        ],
    )(d_row, slots_row, hits, from_b, from_a, factors, member, keep, *fields)

    coded = shape((round_up(chunk + 2, 16), LANES), jnp.int16)
    sums = call(
        functools.partial(pair_kernel, own), (shape((chunk, LANES), F32), *[coded] * (chips - 1)), [VMEM] * 2, []
    )(mine, swap(other, 1))
    sums = [sums[0]] + [swap(sums[far], 2 * far + 1) for far in range(1, chips)]
    return call(
        functools.partial(final_kernel, own),
        (shape((levels, rows, LANES), F32), shape((1, tiles, slots), F32)),
        [VMEM] * (chips + 1),
        [pltpu.VMEM((own, LANES), F32)],
    )(sums[0], *sums[:0:-1], live)


def solution(mesh):
    placed = (
        P("tx", None, "ty", None),
        P("ty", "tx"),
        P(),
        P(),
        P(("ty", "tx"), None, None),
        P(("ty", "tx"), None, None),
        P(("ty", "tx"), None),
    )
    return jax.shard_map(
        shards,
        mesh=mesh,
        in_specs=placed,
        out_specs=(P(None, "ty", "tx"), P(("ty", "tx"), None, None)),
        check_vma=False,
    )
```

```python
import functools

import jax
import jax.numpy as jnp
from jax import lax
from jax.experimental import pallas as pl
from jax.experimental.pallas import tpu as pltpu
from jax.sharding import PartitionSpec as P

STEPS = 4
BAND = 2
LANES = 128
GROUP = 8
CODES, FULL, LEAST = 128, 32700.0, 1.2e-38
F32, BF16 = jnp.float32, jnp.bfloat16
VMEM = pl.BlockSpec(memory_space=pltpu.VMEM)
HBM = pl.BlockSpec(memory_space=pltpu.HBM)


def round_up(n, m):
    return -(-n // m) * m


def log2(n):
    assert n & (n - 1) == 0
    return n.bit_length() - 1


def iota(shape, axis):
    return lax.broadcasted_iota(jnp.int32, shape, axis)


def pieces(x):
    high = x.astype(BF16).astype(F32)
    rest = x - high
    middle = rest.astype(BF16).astype(F32)
    return high, middle, rest - middle


def stagger(x):
    return pltpu.roll(x, 0, 1, stride=GROUP, stride_axis=0)


def pick(x, place):
    if isinstance(place, int):
        shift = (-GROUP * place) % LANES
    else:
        shift = lax.rem(LANES - GROUP * place, LANES)
    rolled = pltpu.roll(x, shift, 1)
    own = iota(x.shape, 1) // GROUP == iota(x.shape, 0)
    return jnp.sum(jnp.where(own, rolled, 0.0), axis=0, keepdims=True)


def live_mask(count_ref, slots):
    tiles = count_ref.shape[1]
    count = jnp.broadcast_to(count_ref[...].astype(F32), (tiles, tiles))
    diagonal = iota((tiles, tiles), 0) == iota((tiles, tiles), 1)
    column = jnp.sum(jnp.where(diagonal, count, 0.0), axis=1, keepdims=True)
    return iota((tiles, slots), 1).astype(F32) < column


def copy_in(sources, targets, sems):
    moves = [pltpu.make_async_copy(x, y, sems.at[i]) for i, (x, y) in enumerate(zip(sources, targets))]
    for move in moves:
        move.start()
    return moves


def packet_kernel(
    value_hbm, cell_hbm, count_hbm, diff_hbm, packet, live_ref,
    value_ref, cell_ref, count_ref, diff_ref, wide, sems,
):
    moves = copy_in(
        (value_hbm, cell_hbm, count_hbm, diff_hbm), (value_ref, cell_ref, count_ref, diff_ref), sems
    )
    wide[...] = jnp.zeros_like(wide)
    for move in moves:
        move.wait()
    _, tiles, slots = value_ref.shape
    rows = diff_ref.shape[0]
    block = min(tiles, LANES // GROUP)
    live = live_mask(count_ref, slots)
    wide[0, :, 0:slots] = jnp.where(live, value_ref[0], 0.0)
    wide[1, :, 0:slots] = cell_ref[0].astype(F32)
    live_ref[...] = jnp.zeros_like(live_ref)
    live_ref[:, 0:slots] = jnp.where(live, 1.0, 0.0)
    packet[0:rows, :] = diff_ref[...]
    lines = [pick(stagger(wide[q, b : b + block, :]), 0) for q in range(2) for b in range(0, tiles, block)]
    if block * GROUP < LANES:
        lines = [lines[0] + pltpu.roll(lines[1], block * GROUP, 1)]
    packet[rows:, :] = jnp.zeros((packet.shape[0] - rows, LANES), F32)
    for i, line in enumerate(lines):
        packet[rows + i : rows + i + 1, :] = line


def member_kernel(
    ens_hbm, vertical_hbm, weights_hbm, turned_ref, factors_ref,
    ens_ref, vertical_ref, weights_ref, tall, sems,
):
    moves = copy_in((vertical_hbm, weights_hbm, ens_hbm), (vertical_ref, weights_ref, ens_ref), sems)
    for move in moves:
        move.wait()
    _, levels, rows, columns = ens_ref.shape
    for t in range(columns // LANES):
        at = slice(t * LANES, (t + 1) * LANES)
        tall[t] = ens_ref[0, :, :, at].astype(F32).reshape(levels * rows, LANES)
        for r in range(0, rows, 2):
            both = [tall[t, pl.ds(r + i, levels, stride=rows), :] for i in range(2)]
            turned_ref[t, r * levels : (r + 2) * levels, :] = jnp.concatenate(both, axis=0).astype(BF16)
    vertical = vertical_ref[...] * weights_ref[lax.axis_index("tx")]
    gap = iota((levels, levels), 1) - iota((levels, levels), 0)
    for i in range(2 * BAND + 1):
        factor = jnp.sum(jnp.where(gap == i - BAND, vertical, 0.0), axis=1, keepdims=True)
        factors_ref[i] = jnp.broadcast_to(factor, (levels, LANES))


def lines_of(staggered, place, tiles):
    size = staggered[0][0].shape[0]
    groups = LANES // GROUP
    return jnp.concatenate([pick(part, place % groups) for part in staggered[place // groups]], axis=1)


def spread(line_value, line_key, hits, count, first):
    key = line_key - first
    on = iota((count, line_key.shape[1]), 0).astype(F32) == key
    stacked = jnp.concatenate([jnp.where(on, piece, 0.0) for piece in pieces(line_value)], axis=0)
    found = lax.dot_general(
        stacked.astype(BF16), hits, (((1,), (1,)), ((), ())), preferred_element_type=F32
    )
    return found[0:count] + found[count : 2 * count] + found[2 * count :]


def hits_of(line_column):
    shape = (LANES, line_column.shape[1])
    return jnp.where(iota(shape, 0).astype(F32) == line_column, 1.0, 0.0).astype(BF16)


def places(cell, rows, levels):
    cell = cell.astype(jnp.int32)
    flat = lax.shift_right_logical(cell, log2(LANES))
    key = (flat & (rows - 1)) * levels + lax.shift_right_logical(flat, log2(rows))
    return key.astype(F32), (cell & (LANES - 1)).astype(F32)


def gather_kernel(order, rows, lines, levels, *refs):
    got, (turned_ref, d_ref, slots_ref, hits_ref, a_ref, b_ref, packs) = refs[: len(order)], refs[len(order) :]
    tiles = packs.shape[0]
    size = min(tiles, LANES // GROUP)
    me, even = lax.axis_index("tx"), lax.rem(lax.axis_index("ty"), 2) == 0
    chip, core, used = me // 2, lax.rem(me, 2), rows + lines
    for far, ref in zip(order, got):
        for side in range(2):
            packs[2 * (chip ^ far) + (core ^ side ^ (far > 0)), 0:used, :] = ref[side * used : (side + 1) * used, :]
    slots = []
    for i in range(lines):
        x = packs[:, rows + i, :]
        slots.append([stagger(x[q : q + size]) for q in range(0, tiles, size)])
    deep = STEPS - 1
    step = deep + lines
    for t in range(tiles):
        value, cell = lines_of(slots, t, tiles), lines_of(slots, tiles + t, tiles)
        key, column = places(cell, rows, levels)
        hits = hits_of(column)
        hits_ref[t] = hits
        found = jnp.dot(turned_ref[t], hits, preferred_element_type=F32)
        on = iota(found.shape, 0).astype(F32) == key
        product = value * jnp.sum(jnp.where(on, found, 0.0), axis=0, keepdims=True)
        d = packs[t, 0:rows, :]
        d_ref[:, t * LANES : (t + 1) * LANES] = d
        low = pltpu.roll(d, deep, 0)
        sent = [line[:, q : q + LANES] for line in (product, cell) for q in range(0, line.shape[1], LANES)]
        if len(sent) > lines:
            sent = [sent[0] + pltpu.roll(sent[1], tiles * GROUP, 1)]
        for out, part in ((a_ref, jnp.where(even, low, d)), (b_ref, jnp.where(even, d, low))):
            out[t * step : t * step + deep, :] = part[0:deep]
            for i, line in enumerate(sent):
                out[t * step + deep + i : t * step + deep + i + 1, :] = line
        for i, line in enumerate((product, key)):
            slots_ref[t, i : i + 1, :] = line


def step_row(rows3, d, c, columns):
    above, mid, below = rows3
    beside = (
        above[:, 0:columns]
        + below[:, 0:columns]
        + pltpu.roll(mid, 1, 1)[:, 0:columns]
        + pltpu.roll(mid, mid.shape[1] - 1, 1)[:, 0:columns]
    )
    return jnp.broadcast_to(c, beside.shape) * mid[:, 0:columns] + jnp.broadcast_to(d, beside.shape) * beside


def own_kernel(slots_ref, hits_ref, turned_ref, d_ref, member_ref, keep_ref, *fields):
    tiles, own, _ = turned_ref.shape
    columns = tiles * LANES
    rows = d_ref.shape[0]
    levels = own // rows
    for field in fields:
        field[:, columns:] = jnp.zeros((own, LANES), F32)
    keep_ref[...] = 1.0 - 4.0 * d_ref[...]
    for t in range(tiles):
        at = slice(t * LANES, (t + 1) * LANES)
        member_ref[:, at] = turned_ref[t].astype(F32)
        fields[0][:, at] = spread(slots_ref[t, 0:1, :], slots_ref[t, 1:2, :], hits_ref[t], own, 0.0)
    for step in range(1, len(fields)):
        for r in range(step, rows - step):
            near = [fields[step - 1][i * levels : (i + 1) * levels, :] for i in (r - 1, r, r + 1)]
            x = step_row(near, d_ref[r : r + 1, :], keep_ref[r : r + 1, :], columns)
            fields[step][r * levels : (r + 1) * levels, 0:columns] = x


def main_kernel(rows, levels, d_ref, slots_ref, hits_ref, b_ref, a_ref, factors_ref, member, keep_ref, *refs):
    fields, (mine_ref, other_ref, d_all, keep, first, second, made, back) = refs[:STEPS], refs[STEPS:]
    tiles = hits_ref.shape[0]
    block = min(tiles, LANES // GROUP)
    columns = tiles * LANES
    band, last, me = lax.axis_index("ty"), lax.axis_size("ty") - 1, lax.axis_index("tx")
    chip, core = me // 2, lax.rem(me, 2)
    even = lax.rem(band, 2) == 0
    half, own, deep = STEPS * levels, rows * levels, STEPS - 1
    step = a_ref.shape[0] // tiles

    for t in range(tiles):
        at = slice(t * LANES, (t + 1) * LANES)
        got_a, got_b = (ref[t * step : (t + 1) * step, :] for ref in (a_ref, b_ref))
        above = jnp.where(band == 0, 0.0, jnp.where(even, got_b, got_a))
        below = jnp.where(band == last, 0.0, jnp.where(even, got_a, got_b))
        for got, begin, base, d_begin in ((above, 0, own - half, 1), (below, half + own, 0, STEPS + rows)):
            d_all[d_begin : d_begin + deep, at] = got[0:deep]
            keep[d_begin : d_begin + deep, at] = 1.0 - 4.0 * got[0:deep]
            parts = [got[deep + i : deep + i + 1] for i in range(step - deep)]
            if len(parts) == 1:
                parts.append(pltpu.roll(parts[0], LANES - tiles * GROUP, 1))
                parts[0] = jnp.where(iota((1, LANES), 1) < tiles * GROUP, parts[0], 0.0)
            product, cell = (jnp.concatenate(parts[i : i + len(parts) // 2], axis=1) for i in (0, len(parts) // 2))
            key, column = places(cell, rows, levels)
            first[begin : begin + half, at] = spread(product, key, hits_of(column), half, float(base))
    for field in (first, second):
        field[:, columns:] = jnp.zeros((field.shape[0], LANES), F32)

    def inner(step, r):
        return step <= r - STEPS < rows - step

    def row_of(step, r):
        ref, i = (fields[step], r - STEPS) if inner(step, r) else ((first, second)[step % 2], r)
        return ref[i * levels : (i + 1) * levels, :]

    factors = [(i - BAND, factors_ref[i]) for i in range(2 * BAND + 1)]
    for step in range(1, STEPS):
        for r in range(step, 2 * STEPS + rows - step):
            if inner(step, r):
                continue
            if 0 <= r - STEPS < rows:
                d, c = (ref[r - STEPS : r - STEPS + 1, :] for ref in (d_ref, keep_ref))
            else:
                d, c = (ref[r : r + 1, :] for ref in (d_all, keep))
            x = step_row([row_of(step - 1, i) for i in (r - 1, r, r + 1)], d, c, columns)
            (first, second)[step % 2][r * levels : (r + 1) * levels, 0:columns] = x

    rowed = [row_of(STEPS - 1, r) for r in range(STEPS - 1, STEPS + rows + 1)]
    lane = iota((levels, LANES), 1)
    zero = jnp.zeros((levels, LANES), F32)

    def piece(r, t):
        return rowed[r + 1][:, t * LANES : (t + 1) * LANES] if 0 <= t < tiles else zero

    before = [zero] * rows
    here = [piece(r, 0) for r in range(rows)]
    for t in range(tiles):
        at = slice(t * LANES, (t + 1) * LANES)
        after = [piece(r, t + 1) for r in range(rows)]
        parts = []
        for r in range(rows):
            mid = here[r]
            left = pltpu.roll(jnp.where(lane == LANES - 1, before[r], mid), 1, 1)
            right = pltpu.roll(jnp.where(lane == 0, after[r], mid), LANES - 1, 1)
            beside = piece(r - 1, t) + piece(r + 1, t) + left + right
            d, c = (jnp.broadcast_to(ref[r : r + 1, at], mid.shape) for ref in (d_ref, keep_ref))
            x = c * mid + d * beside
            mixed = sum(f * (pltpu.roll(x, -o % levels, 0) if o else x) for o, f in factors)
            row = slice(r * levels, (r + 1) * levels)
            parts.append(mixed * member[row, at])
            made[t, row, :] = parts[-1]
        before, here = here, after
        stacked = jnp.concatenate(pieces(jnp.concatenate(parts, axis=0))[:2], axis=0).astype(BF16)
        found = jnp.dot(stacked, hits_ref[t], preferred_element_type=F32)
        found = found[0:own] + found[own:]
        on = iota(found.shape, 0).astype(F32) == slots_ref[t, 1:2, :]
        line = jnp.sum(jnp.where(on, found, 0.0), axis=0, keepdims=True)
        for q in range(tiles // block):
            back[q, t : t + 1, :] = line[:, q * LANES : (q + 1) * LANES]
    for z in range(mine_ref.shape[0]):
        for side, out in enumerate((mine_ref, other_ref)):
            out[z, 0:own, :] = made[2 * z + (core ^ side ^ (chip != z).astype(jnp.int32))]
            out[z, own:, :] = back[2 * z // block]


def scale_of(code):
    return jnp.exp2(code.astype(F32) * (1.0 / CODES))


def pair_kernel(split, mine_ref, got_ref, near_ref, *outs):
    chip = lax.axis_index("tx") // 2
    near_ref[...] = mine_ref[chip] + got_ref[chip]
    for far, out in enumerate(outs, 1):
        x = mine_ref[chip ^ far] + got_ref[chip ^ far]
        whole, codes = [], []
        for part in (x[0:split], x[split:]):
            largest = jnp.maximum(jnp.max(jnp.abs(part), axis=0, keepdims=True), LEAST)
            code = jnp.minimum(jnp.ceil(jnp.log2(largest) * CODES).astype(jnp.int32), CODES * 128 - 1)
            sized = jnp.clip(part * (1.0 / scale_of(code)), -1.0, 1.0)
            whole.append(jnp.floor(sized * FULL + 0.5).astype(jnp.int32))
            codes.append(code)
        rest = out.shape[0] - x.shape[0]
        row = iota((rest, LANES), 0)
        tail = jnp.where(row == 0, codes[0], jnp.where(row == 1, codes[1], 0))
        out[...] = jnp.concatenate([*whole, tail], axis=0).astype(jnp.int16)


def final_kernel(split, *refs):
    got, (live_ref, inc_ref, proj_ref, total) = refs[:-4], refs[-4:]
    levels, rows, _ = inc_ref.shape
    _, tiles, slots = proj_ref.shape
    size = got[0].shape[0]
    top, low = got[0][0:split, :], got[0][split:, :]
    for ref in got[1:]:
        x = ref[...].astype(jnp.int32)
        sent = x[0:size].astype(F32) * (1.0 / FULL)
        top = top + sent[0:split] * scale_of(x[size : size + 1])
        low = low + sent[split:] * scale_of(x[size + 1 : size + 2])
    total[...] = top
    for level in range(levels):
        inc_ref[level] = total[pl.ds(level, rows, stride=levels), :]
    place = lax.rem(lax.axis_index("tx"), LANES // GROUP)
    lines = pltpu.roll(low, lax.rem(LANES - GROUP * place, LANES), 1)
    proj_ref[0] = jnp.where(live_ref[:, 0:slots] > 0.0, lines[:, 0:slots], 0.0)


def call(kernel, out_shape, ins, scratch, flops=0, moved=0):
    return pl.pallas_call(
        kernel,
        out_shape=out_shape,
        in_specs=ins,
        out_specs=jax.tree.map(lambda _: VMEM, out_shape),
        scratch_shapes=scratch,
        compiler_params=pltpu.CompilerParams(vmem_limit_bytes=48 << 20),
        cost_estimate=pl.CostEstimate(flops=flops, bytes_accessed=moved, transcendentals=0),
    )


def shards(ensemble, diffusivity, vertical, weights, obs_value, obs_cell, obs_count):
    _, levels, rows, columns = ensemble.shape
    tiles, slots = obs_value.shape[1:]
    chips = tiles // 2
    bands = lax.axis_size("ty")
    assert diffusivity.shape == (rows, LANES) and slots == GROUP and rows == 2 * STEPS
    block = min(tiles, LANES // GROUP)
    shape = jax.ShapeDtypeStruct
    lines = -(-2 * tiles * GROUP // LANES)
    half, own = STEPS * levels, rows * levels
    height = round_up(rows + lines, 8)
    lanes = tiles // block * LANES

    def in_hbm(*arrays):
        return [pltpu.with_memory_space_constraint(x, pltpu.HBM) for x in arrays]

    def swap(x, far):
        return lax.ppermute(x, "tx", [(i, i ^ far) for i in range(tiles)])

    def swap_bands(x, low):
        mate = [i ^ 1 if low else i + 1 if i % 2 else i - 1 for i in range(bands)]
        pairs = [
            (i * tiles + k, mate[i] * tiles + k if 0 <= mate[i] < bands else i * tiles + (k ^ 1))
            for i in range(bands)
            for k in range(tiles)
        ]
        return lax.ppermute(x, ("ty", "tx"), pairs)

    packet, live = call(
        packet_kernel,
        (shape((height, LANES), F32), shape((tiles, LANES), F32)),
        [HBM] * 4,
        [
            pltpu.VMEM(obs_value.shape, F32),
            pltpu.VMEM(obs_cell.shape, jnp.int32),
            pltpu.VMEM(obs_count.shape, jnp.int32),
            pltpu.VMEM(diffusivity.shape, F32),
            pltpu.VMEM((2, tiles, LANES), F32),
            pltpu.SemaphoreType.DMA((4,)),
        ],
    )(*in_hbm(obs_value, obs_cell, obs_count, diffusivity))
    turned, factors = call(
        member_kernel,
        (shape((tiles, own, LANES), BF16), shape((2 * BAND + 1, levels, LANES), F32)),
        [HBM] * 3,
        [
            pltpu.VMEM(ensemble.shape, BF16),
            pltpu.VMEM(vertical.shape, F32),
            pltpu.SMEM(weights.shape, F32),
            pltpu.VMEM((tiles, own, LANES), F32),
            pltpu.SemaphoreType.DMA((3,)),
        ],
        1000000,
        1000000,
    )(*in_hbm(ensemble, vertical, weights))

    used = rows + lines
    spare = jnp.zeros((round_up(2 * used, 8) - 2 * used, LANES), F32)
    pair = jnp.concatenate([packet[:used], swap(packet, 1)[:used], spare])
    order = [0] + sorted(range(1, chips), key=lambda far: (far % 2 == 0, far))
    row = [swap(pair, 2 * far + 1) if far else pair for far in order]
    halo = shape((tiles * (STEPS - 1 + lines), LANES), F32)
    d_row, slots_row, hits, to_a, to_b = call(
        functools.partial(gather_kernel, order, rows, lines, levels),
        (
            shape((rows, columns), F32),
            shape((tiles, 8, lanes), F32),
            shape((tiles, LANES, lanes), BF16),
            halo,
            halo,
        ),
        [VMEM] * (chips + 1),
        [pltpu.VMEM((tiles, height, LANES), F32)],
    )(*row, turned)
    from_a, from_b = swap_bands(to_a, True), swap_bands(to_b, False)
    wide = shape((own, columns + LANES), F32)
    member, keep, *fields = call(
        own_kernel,
        (shape((own, columns), F32), shape((rows, columns), F32), *[wide] * STEPS),
        [VMEM] * 4,
        [],
        1000000,
        1000000,
    )(slots_row, hits, turned, d_row)

    chunk = own + tiles
    mine, other = call(
        functools.partial(main_kernel, rows, levels),
        (shape((chips, chunk, LANES), F32), shape((chips, chunk, LANES), F32)),
        [VMEM] * (8 + STEPS),
        [
            pltpu.VMEM((2 * STEPS + rows, columns), F32),
            pltpu.VMEM((2 * STEPS + rows, columns), F32),
            pltpu.VMEM((2 * half + own, columns + LANES), F32),
            pltpu.VMEM((2 * half + own, columns + LANES), F32),
            pltpu.VMEM((tiles, own, LANES), F32),
            pltpu.VMEM((tiles // block, tiles, LANES), F32),
        ],
    )(d_row, slots_row, hits, from_b, from_a, factors, member, keep, *fields)

    coded = shape((round_up(chunk + 2, 16), LANES), jnp.int16)
    sums = call(
        functools.partial(pair_kernel, own), (shape((chunk, LANES), F32), *[coded] * (chips - 1)), [VMEM] * 2, []
    )(mine, swap(other, 1))
    sums = [sums[0]] + [swap(sums[far], 2 * far + 1) for far in range(1, chips)]
    return call(
        functools.partial(final_kernel, own),
        (shape((levels, rows, LANES), F32), shape((1, tiles, slots), F32)),
        [VMEM] * (chips + 1),
        [pltpu.VMEM((own, LANES), F32)],
    )(sums[0], *sums[:0:-1], live)


def solution(mesh):
    placed = (
        P("tx", None, "ty", None),
        P("ty", "tx"),
        P(),
        P(),
        P(("ty", "tx"), None, None),
        P(("ty", "tx"), None, None),
        P(("ty", "tx"), None),
    )
    return jax.shard_map(
        shards,
        mesh=mesh,
        in_specs=placed,
        out_specs=(P(None, "ty", "tx"), P(("ty", "tx"), None, None)),
        check_vma=False,
    )
```
